32 devices in a mesh: batch: 8 (over y, x, core), row: 4 (over z).
Axes of the slice: x: 2, y: 2, z: 4, core: 2. Of those that a mesh axis runs over, the one named last changes fastest.
Arguments:
- input_field: bfloat16 [64, 128, 192, 128], P('batch', 'row'), may hold values from -6 to 6
- cotangent: bfloat16 [64, 128, 192, 128], P('batch', 'row'), may hold values from -6 to 6
- sample_scale: int32 [64], P('batch'), may hold values from 0 to 7
- scale_table: float32 [8], replicated, may hold values from 0.5 to 2
- owner_map: int32 [256], replicated, may hold values from 0 to 255, as said below
- spectral_master: float32 [256, 48, 384], P(('batch', 'row')), may hold values from -1.25 to 1.25
- spectral_momentum: float32 [256, 48, 384], P(('batch', 'row')), may hold values from -96 to 96
- pointwise_master: float32 [48, 192], replicated, may hold values from -0.3125 to 0.3125
- pointwise_momentum: float32 [48, 192], replicated, may hold values from -8192 to 8192
Outputs:
- output_field: bfloat16 [64, 128, 192, 128], P('batch', 'row')
- input_grad: bfloat16 [64, 128, 192, 128], P('batch', 'row')
- spectral_grad: float32 [256, 48, 384], P(('batch', 'row'))
- spectral_moment: float32 [256, 48, 384], P(('batch', 'row'))
- spectral_weight: float32 [256, 48, 384], P(('batch', 'row'))
- spectral_weight_low: bfloat16 [256, 48, 384], P(('batch', 'row'))
- pointwise_grad: float32 [48, 192], replicated
- pointwise_moment: float32 [48, 192], replicated
- pointwise_weight: float32 [48, 192], replicated
- pointwise_weight_low: bfloat16 [48, 192], replicated
The draws below stay inside these ranges and needn't reach their ends.
Inputs may be any that keep to these rules, and one draw needn't show every extreme that they name: owner_map is a permutation of the 256 modes; slot t names a mode m whose column frequency l = m mod 16 satisfies l // 4 == (t // 8) mod 4.
All inputs are finite; a program needn't handle non-finite values.
Results may differ from the reference program's by a relative error of at most 0.011.
Values may be sent and summed in bfloat16 or wider, within the bound.
A program may use at most 192 MiB of HBM per device.

```python
import math
import jax
import jax.numpy as jnp
import numpy as np
from jax import lax

CHANNELS = 48
GRID_SIZE = 128
ROW_MODES = 16
COLUMN_MODES = 16
SCALES = 8
MODES = 256
SLOTS_DEV = 8
SAMPLES = 64
N_BATCH = 8
N_ROW = 4


def draw_owner_map(key, part):
    key = jax.random.fold_in(key, 11)
    local_columns = COLUMN_MODES // N_ROW
    group_size = ROW_MODES * local_columns

    def shuffle_group(group_key):
        return jax.random.permutation(group_key, group_size)
    shuffled = jax.vmap(shuffle_group)(jax.random.split(key, N_ROW)).astype(jnp.int32)
    quarter = jnp.arange(N_ROW, dtype=jnp.int32)[:, None]
    modes_named = shuffled // local_columns * COLUMN_MODES + quarter * local_columns + shuffled % local_columns
    arranged = modes_named.reshape(N_ROW, N_BATCH, SLOTS_DEV).transpose(1, 0, 2)
    return arranged.reshape(MODES).astype(jnp.int32)


def touch_ends(values, key, low, top_value):
    extent = values.shape
    index_at = [jax.random.randint(jax.random.fold_in(key, axis), (), 0, extent[axis]) for axis in range(len(extent))]
    values = values.at[tuple(index_at)].set(low)
    longest = extent.index(max(extent))
    index_at[longest] = (index_at[longest] + 1) % extent[longest]
    return values.at[tuple(index_at)].set(top_value)


def block_levels(stream_key, extent, cuts, smallest, largest):
    def one(dim, shards_of):
        draws = jax.random.uniform(jax.random.fold_in(jax.random.fold_in(stream_key, 6), dim), (shards_of,), jnp.float32, smallest / len(cuts), largest / len(cuts))
        return jnp.repeat(jnp.exp(draws), extent[dim] // shards_of).reshape((-1,) + (1,) * (len(extent) - dim - 1))

    loudness = one(*cuts[0])
    for cut in cuts[1:]:
        loudness = loudness * one(*cut)
    return loudness


def bell_draw(stream_key, dims, scale, most, shards=(), kind=jnp.bfloat16):
    gain = block_levels(stream_key, dims, shards, -0.22, 0.18) if shards else 1.0
    values = jax.random.normal(stream_key, dims, jnp.float32) * scale * gain
    return jnp.minimum(jnp.maximum(values, -most), most).astype(kind)


def setup_inputs(seed: int = 0) -> dict:
    keys = jax.random.split(jax.random.key(seed), 10)
    return {
        "input_field": bell_draw(keys[0], (SAMPLES, GRID_SIZE, 4 * CHANNELS, GRID_SIZE), 1.0, 6.0, ((0, 8), (1, 4))),
        "cotangent": bell_draw(keys[1], (SAMPLES, GRID_SIZE, 4 * CHANNELS, GRID_SIZE), 1.0, 6.0, ((0, 8), (1, 4))),
        "sample_scale": touch_ends(jax.random.randint(keys[2], (SAMPLES,), 0, SCALES), jax.random.fold_in(keys[2], 1), 0, SCALES - 1).astype(jnp.int32),
        "scale_table": jnp.clip(jnp.exp(jax.random.uniform(keys[3], (SCALES,), jnp.float32, math.log(0.5), math.log(2.0))), 0.5, 2.0),
        "owner_map": draw_owner_map(jax.random.fold_in(keys[9], 71), 0),
        "spectral_master": bell_draw(keys[5], (MODES, CHANNELS, 8 * CHANNELS), (32 * ROW_MODES * COLUMN_MODES * CHANNELS // (GRID_SIZE * GRID_SIZE)) ** -0.5, 1.25, ((0, 32),), jnp.float32),
        "spectral_momentum": bell_draw(keys[6], (MODES, CHANNELS, 8 * CHANNELS), ((4 * SAMPLES) ** 0.5), 96.0, ((0, 32),), jnp.float32),
        "pointwise_master": bell_draw(keys[7], (CHANNELS, 4 * CHANNELS), (8 * CHANNELS) ** -0.5, 0.3125, (), jnp.float32),
        "pointwise_momentum": bell_draw(keys[8], (CHANNELS, 4 * CHANNELS), (GRID_SIZE * (2 * SAMPLES) ** 0.5), 8192.0, (), jnp.float32),
    }


BLADE_SIGNS = np.array([[1, 1, 1, 1], [1, 1, 1, 1], [1, -1, 1, -1], [1, -1, 1, -1]], np.float32)
QUINTIC_FIRST = 3.4445
QUINTIC_SECOND = -4.775
QUINTIC_THIRD = 2.0315
SPECTRAL_RATE = 4.0
POINTWISE_RATE = 0.8
MOMENTUM_DECAY = 0.5
PRECISE = lax.Precision.HIGHEST

@jax.custom_vjp
def low(v):
    return lax.optimization_barrier(v.astype(jnp.bfloat16)).astype(jnp.float32)

@jax.custom_vjp
def low_back(v):
    return v

def low_keep(v):
    return (low(v), None)

def low_pass(kept, grad):
    return (grad,)

def back_keep(v):
    return (v, None)

def back_low(kept, grad):
    return (low(grad),)
low.defvjp(low_keep, low_pass)
low_back.defvjp(back_keep, back_low)

def angles_of(first, second, grid_size):
    return 2.0 * math.pi / grid_size * (first * second % grid_size).astype(jnp.float32)

def row_frequencies(grid_size, mode_count):
    indices = jnp.arange(mode_count, dtype=jnp.int32)
    return jnp.where(indices < mode_count // 2, indices, grid_size - mode_count + indices)

def column_table(grid_size, mode_count):
    position = jnp.arange(grid_size, dtype=jnp.int32)[:, None]
    frequency = jnp.arange(mode_count, dtype=jnp.int32)[None, :]
    angles = angles_of(position, frequency, grid_size)
    return jnp.concatenate([jnp.cos(angles), -jnp.sin(angles)], axis=1).astype(jnp.bfloat16)

def row_table(grid_size, mode_count):
    frequency = row_frequencies(grid_size, mode_count)[:, None]
    position = jnp.arange(grid_size, dtype=jnp.int32)[None, :]
    angles = angles_of(frequency, position, grid_size)
    cosine, sines = (jnp.cos(angles), jnp.sin(angles))
    upper_half = jnp.stack([cosine, sines], axis=-1)
    bottom = jnp.stack([-sines, cosine], axis=-1)
    return jnp.stack([upper_half, bottom], axis=0).reshape(2 * mode_count, 2 * grid_size).astype(jnp.bfloat16)

def inverse_row_table(grid_size, mode_count):
    position = jnp.arange(grid_size, dtype=jnp.int32)[:, None]
    frequency = row_frequencies(grid_size, mode_count)[None, :]
    angles = angles_of(position, frequency, grid_size)
    cosine, sines = (jnp.cos(angles), jnp.sin(angles))
    real_rows = jnp.stack([cosine, -sines], axis=1)
    imaginary_rows = jnp.stack([sines, cosine], axis=1)
    return jnp.stack([real_rows, imaginary_rows], axis=1).reshape(2 * grid_size, 2 * mode_count).astype(jnp.bfloat16)

def inverse_column_table(grid_size, mode_count):
    frequency = jnp.arange(mode_count, dtype=jnp.int32)[:, None]
    position = jnp.arange(grid_size, dtype=jnp.int32)[None, :]
    angles = angles_of(frequency, position, grid_size)
    weight = jnp.where(frequency == 0, 1.0, 2.0) / (grid_size * grid_size)
    return jnp.concatenate([weight * jnp.cos(angles), -weight * jnp.sin(angles)], axis=0).astype(jnp.bfloat16)

def expand(blade_parts):
    channels = blade_parts.shape[-1]
    source = np.array([[k ^ a for a in range(4)] for k in range(4)], np.int32)
    sign_table = np.array([[BLADE_SIGNS[a, k ^ a] for a in range(4)] for k in range(4)], np.float32)
    picked = blade_parts[..., source, :] * jnp.asarray(sign_table, blade_parts.dtype)[:, :, None]
    real_part = picked[..., 0, :, :, :]
    imaginary = picked[..., 1, :, :, :]
    upper_half = jnp.stack([real_part, -imaginary], axis=-3)
    bottom = jnp.stack([imaginary, real_part], axis=-3)
    stacked = jnp.stack([upper_half, bottom], axis=-4)
    return stacked.reshape(stacked.shape[:-5] + (8, 8 * channels))

def point_kernel(point_weight):
    channels = point_weight.shape[0]
    source = np.array([[k ^ b for k in range(4)] for b in range(4)], np.int32)
    sign_table = np.array([[BLADE_SIGNS[k ^ b, b] for k in range(4)] for b in range(4)], np.float32)
    blades = point_weight.reshape(channels, 4, channels)
    picked = blades[:, source, :] * jnp.asarray(sign_table, point_weight.dtype)[None, :, :, None]
    return picked.transpose(1, 3, 2, 0).reshape(4 * channels, 4 * channels)

def orthogonalize(matrices):
    norm_size = jnp.sqrt(lax.optimization_barrier(jnp.sum(matrices * matrices, axis=(-2, -1), keepdims=True)))
    current = matrices / (norm_size + 1e-07)
    for repeat in range(5):
        gram_matrix = jnp.einsum('...ij,...kj->...ik', current, current, precision=PRECISE)
        polynomial = QUINTIC_SECOND * gram_matrix + QUINTIC_THIRD * jnp.einsum('...ij,...jk->...ik', gram_matrix, gram_matrix, precision=PRECISE)
        current = QUINTIC_FIRST * current + jnp.einsum('...ij,...jk->...ik', polynomial, current, precision=PRECISE)
    return current

def reference(input_field, cotangent, sample_scale, scale_table, owner_map, spectral_master, spectral_momentum, pointwise_master, pointwise_momentum):
    blade_width = 4 * CHANNELS
    column_fwd = column_table(GRID_SIZE, COLUMN_MODES).astype(jnp.float32)
    row_fwd = row_table(GRID_SIZE, ROW_MODES).astype(jnp.float32)
    row_inv = inverse_row_table(GRID_SIZE, ROW_MODES).astype(jnp.float32)
    column_inv = inverse_column_table(GRID_SIZE, COLUMN_MODES).astype(jnp.float32)
    positions = jnp.arange(MODES, dtype=jnp.int32)
    inverse_map = jnp.zeros((MODES,), jnp.int32).at[owner_map].set(positions)
    factors = jnp.take(scale_table, sample_scale)

    def forward(sample_values, masters, pointwise, factor):
        weights = jnp.take(low(masters), inverse_map, axis=0)
        columns = low_back(low(jnp.einsum('hkw,wm->hmk', sample_values, column_fwd, precision=PRECISE)))
        columns = columns.reshape(2 * GRID_SIZE, COLUMN_MODES, blade_width)
        spectra = low_back(low(jnp.einsum('xy,yqk->xqk', row_fwd, columns, precision=PRECISE)))
        blade_parts = spectra.reshape(2, ROW_MODES, COLUMN_MODES, 4, CHANNELS).transpose(1, 2, 0, 3, 4).reshape(MODES, 2, 4, CHANNELS)
        spread = expand(blade_parts)
        product = low_back(low(jnp.einsum('myz,moz->myo', spread, weights, precision=PRECISE)))
        product = product.reshape(ROW_MODES, COLUMN_MODES, 4, 2, CHANNELS).transpose(3, 0, 1, 2, 4).reshape(2 * ROW_MODES, COLUMN_MODES, blade_width)
        rows_back = low_back(low(jnp.einsum('yx,xqk->yqk', row_inv, product, precision=PRECISE)))
        rows_back = rows_back.reshape(GRID_SIZE, 2 * COLUMN_MODES, blade_width)
        spectral = jnp.einsum('hmk,mw->hkw', rows_back, column_inv, precision=PRECISE)
        kernel = point_kernel(low(pointwise))
        pointwise_part = jnp.einsum('hkw,kj->hjw', sample_values, kernel, precision=PRECISE)
        branch = low_back(spectral + pointwise_part)
        return sample_values + jax.nn.gelu(factor * branch)

    def per_sample(totals, sample_items):
        sample_field, sample_cot, factor = sample_items

        def sample_forward(sample_values, masters, pointwise):
            return forward(sample_values, masters, pointwise, factor)
        outputs, pullback = jax.vjp(sample_forward, sample_field.astype(jnp.float32), spectral_master, pointwise_master)
        grad_field, grad_master, grad_point = pullback(sample_cot.astype(jnp.float32))
        return ((totals[0] + grad_master, totals[1] + grad_point), (outputs.astype(jnp.bfloat16), grad_field.astype(jnp.bfloat16)))
    start = (jnp.zeros(spectral_master.shape, jnp.float32), jnp.zeros(pointwise_master.shape, jnp.float32))
    (spectral_grad, pointwise_grad), (output_field, input_grad) = lax.scan(per_sample, start, (input_field, cotangent, factors))
    spectral_moment = MOMENTUM_DECAY * spectral_momentum + spectral_grad
    spectral_weight = spectral_master - SPECTRAL_RATE * orthogonalize(spectral_moment)
    pointwise_moment = MOMENTUM_DECAY * pointwise_momentum + pointwise_grad
    pointwise_weight = pointwise_master - POINTWISE_RATE * orthogonalize(pointwise_moment)
    return (output_field, input_grad, spectral_grad, spectral_moment, spectral_weight, spectral_weight.astype(jnp.bfloat16), pointwise_grad, pointwise_moment, pointwise_weight, pointwise_weight.astype(jnp.bfloat16))
```

```python
import functools
import math

import jax
import jax.numpy as jnp
import ml_dtypes
import numpy as np
from jax import lax
from jax.experimental import pallas as pl
from jax.experimental.pallas import tpu as pltpu
from jax.sharding import PartitionSpec as P

ROW_MODES = 16
COLUMN_MODES = 16

BLADE_SIGNS = np.array([[1, 1, 1, 1], [1, 1, 1, 1], [1, -1, 1, -1], [1, -1, 1, -1]], np.float32)
QUINTIC_FIRST = 3.4445
QUINTIC_SECOND = -4.775
QUINTIC_THIRD = 2.0315
SPECTRAL_RATE = 4.0
POINTWISE_RATE = 0.8
MOMENTUM_DECAY = 0.5
PRECISE = lax.Precision.HIGHEST
MESH = pl.DeviceIdType.MESH
F32 = jnp.float32
BF16 = jnp.bfloat16
GELU_A = math.sqrt(2.0 / math.pi)
GELU_B = GELU_A * 0.044715


def column_block(grid_size):
    angles = 2.0 * np.pi / grid_size * (np.arange(COLUMN_MODES)[:, None] * np.arange(grid_size)[None] % grid_size)
    table = np.concatenate([np.cos(angles), -np.sin(angles)], 0)
    return np.kron(np.eye(2), table).astype(ml_dtypes.bfloat16)


def row_blocks(grid_size, row_count):
    rows = grid_size // row_count
    local = COLUMN_MODES // row_count
    r = np.arange(ROW_MODES)
    frequency = np.where(r < ROW_MODES // 2, r, grid_size - ROW_MODES + r)
    angles = 2.0 * np.pi / grid_size * (frequency[:, None] * np.arange(grid_size)[None] % grid_size)
    cosine, sine = np.cos(angles), np.sin(angles)
    table = np.stack([np.stack([cosine, sine], -1), np.stack([-sine, cosine], -1)], 0)
    table = table.reshape(2, ROW_MODES, row_count, rows, 2)
    same = np.eye(COLUMN_MODES).reshape(row_count, local, COLUMN_MODES)
    full = np.einsum("qrzhp,cdl->zqcrdhpl", table, same)
    return full.reshape(
        row_count, 2 * ROW_MODES * COLUMN_MODES, rows * 2 * COLUMN_MODES
    ).astype(ml_dtypes.bfloat16)


def product_signs(channels):
    signs = np.zeros((2, 4, 2, 4, 2, 4), np.float32)
    for q in range(2):
        for p in range(2):
            pw = p ^ q
            part = -1.0 if (q == 0 and p == 1) else 1.0
            for k in range(4):
                for b in range(4):
                    signs[q, k, pw, k ^ b, p, b] = part * BLADE_SIGNS[k ^ b, b]
    full = np.einsum("qkwapb,ij->qkwaipbj", signs, np.eye(channels, dtype=np.float32))
    return full.reshape(8, 8 * channels, 8 * channels).astype(ml_dtypes.bfloat16)


def dot(a, b):
    return lax.dot_general(a, b, (((1,), (0,)), ((), ())), preferred_element_type=F32)


def dot_nt(a, b):
    return lax.dot_general(a, b, (((1,), (1,)), ((), ())), preferred_element_type=F32)


def layer_kernel(
    sizes,
    x_hbm, ct_hbm, factor, rk_hbm, pi_hbm, cblk_ref, eye_ref, perm_ref, master_ref, point_ref,
    out_hbm, gb_hbm, dw_ref, pg_ref, kk_ref, gb2,
    xb, cb, rk, pi, bigw, cols, res, l2, kt1, ktb, acc, gk_ref, pa, pz,
    pb1, rb1, gb1, pb2, rb2,
    xs, xr, ps, pr, gs, gr, hs, hr,
    x_sem, g_sem, ld_sem, ci_sem, co_sem, pa_s, pa_r, pz_s, pz_r,
    rs1_s, rs1_r, rs2_s, rs2_r, ag1_s, ag1_r, ag2_s, ag2_r, a2a_s, a2a_r,
):
    nb, nz, S, H, K, W, slots, M = sizes
    wide = 2 * K
    channels = K // 4
    pairs = H // 2
    me = lax.axis_index("batch")
    z = lax.axis_index("row")
    last = nz - 1

    loads = [pltpu.make_async_copy(rk_hbm.at[z], rk, ld_sem.at[0]), pltpu.make_async_copy(pi_hbm, pi, ld_sem.at[1])]
    x_copy = lambda s: pltpu.make_async_copy(x_hbm.at[s], xb.at[s], x_sem.at[s])
    ct_copy = lambda s: pltpu.make_async_copy(ct_hbm.at[s], cb.at[lax.rem(s, 2)], ci_sem.at[lax.rem(s, 2)])
    out_copy = lambda s: pltpu.make_async_copy(cb.at[lax.rem(s, 2)], out_hbm.at[s], co_sem.at[lax.rem(s, 2)])
    g_copy = lambda s: pltpu.make_async_copy(xb.at[s], gb_hbm.at[s], g_sem.at[s])

    barrier = pltpu.get_barrier_semaphore()

    def greet(d, carry):
        peer = lax.rem(me + d, nb)
        pl.semaphore_signal(barrier, inc=1, device_id=(peer, z), device_id_type=MESH)
        return carry

    lax.fori_loop(1, nb, greet, 0)

    def greet_z(d, carry):
        pl.semaphore_signal(barrier, inc=1, device_id=(me, lax.rem(z + d, nz)), device_id_type=MESH)
        return carry

    lax.fori_loop(1, nz, greet_z, 0)
    x_copy(0).start()
    for one in loads:
        one.start()

    def load_x(s, carry):
        x_copy(s).start()
        return carry

    lax.fori_loop(1, S, load_x, 0)
    ct_copy(0).start()
    cols[...] = jnp.zeros_like(cols)
    gk_ref[...] = jnp.zeros_like(gk_ref)
    for one in loads:
        one.wait()

    point = point_ref[...].astype(BF16)
    kernel_t = jnp.concatenate([dot(point, pi[k, 0:K, 0:256]) for k in range(4)], axis=0)
    kt1[...] = kernel_t[:, 0:128].astype(BF16)
    ktb[...] = kernel_t[:, 128:256]
    padded = jnp.concatenate([kernel_t.astype(BF16), jnp.zeros((256 - K, 256), BF16)], axis=0)
    kernel_n = dot_nt(eye_ref[0:K, 0:256], padded)
    kk_ref[...] = kernel_n

    def expand_weights(kq, carry):
        every = master_ref[...].reshape(slots * channels, wide).astype(BF16)
        block = dot(every, pi[kq]).astype(BF16)
        for i in range(slots):
            bigw[i, pl.ds(pl.multiple_of(kq * channels, channels), channels), :] = block[
                i * channels : (i + 1) * channels
            ]
        return carry

    lax.fori_loop(0, 8, expand_weights, 0)

    def rs_copy(s, up, c, pb, rb, ssem, rsem):
        way = 0 if up else 1
        return pltpu.make_async_remote_copy(
            src_ref=pb.at[s, c], dst_ref=rb.at[s, way, c],
            send_sem=ssem.at[s, way, c], recv_sem=rsem.at[s, way, c],
            device_id=(me, z + 1 if up else z - 1), device_id_type=MESH,
        )

    def rs_hop(j, s, bufs, finish=False):
        pb, rb = bufs[0], bufs[1]
        for up in (True, False):
            place = z if up else last - z
            c = (last - j + z) if up else (z - (last - j))

            @pl.when(place <= j)
            def _():
                copy = rs_copy(s, up, c, *bufs)
                if finish:
                    copy.wait_send()
                else:
                    @pl.when(place > 0)
                    def _():
                        way = 0 if up else 1
                        copy.wait_recv()
                        pb[s, c] = (pb[s, c].astype(F32) + rb[s, way, c].astype(F32)).astype(BF16)

                    copy.start()

    def rs_final(s, bufs):
        pb, rb = bufs[0], bufs[1]
        acc[...] = pb[s, z].astype(F32)

        @pl.when(z > 0)
        def _():
            rs_copy(s, True, z, *bufs).wait_recv()
            acc[...] += rb[s, 0, z].astype(F32)

        @pl.when(z < last)
        def _():
            rs_copy(s, False, z, *bufs).wait_recv()
            acc[...] += rb[s, 1, z].astype(F32)

        return acc[...].astype(BF16)

    def ag_copy(s, up, c, gb, ssem, rsem):
        way = 0 if up else 1
        return pltpu.make_async_remote_copy(
            src_ref=gb.at[s, c], dst_ref=gb.at[s, c],
            send_sem=ssem.at[s, way, c], recv_sem=rsem.at[s, c],
            device_id=(me, z + 1 if up else z - 1), device_id_type=MESH,
        )

    def ag_hop(j, s, bufs, finish=False):
        for up in (True, False):
            c = z - j if up else z + j
            more = z < last if up else z > 0

            @pl.when((c >= 0) if up else (c <= last))
            def _():
                copy = ag_copy(s, up, c, *bufs)
                if j > 0 and not finish:
                    copy.wait_recv()

                if j < last:
                    @pl.when(more)
                    def _():
                        if finish:
                            copy.wait_send()
                        else:
                            copy.start()

    tiled = slots % 8 == 0

    def block_of(ref, s, d):
        if tiled:
            return ref.at[s, :, pl.ds(pl.multiple_of(d * slots, slots), slots)]
        return ref.at[s, d]

    def blocks_of(ref, s):
        if tiled:
            return ref.at[s, :, pl.ds(0, (nb - 1) * slots)]
        return ref.at[s, pl.ds(0, nb - 1)]

    def whole_of(ref, s):
        if tiled:
            return jnp.concatenate([ref[s, g] for g in range(wide // 128)], axis=1)
        return ref[s].reshape(nb * slots, wide)

    def put_whole(ref, s, value):
        if tiled:
            for g in range(wide // 128):
                ref[s, g] = value[:, g * 128 : (g + 1) * 128]
        else:
            ref[s] = value.reshape(nb, slots, wide)

    def slot_rows(ref, s, i):
        if tiled:
            return jnp.concatenate([ref[s, g, pl.ds(i, nb, stride=slots), :] for g in range(wide // 128)], axis=1)
        return ref[s, :, i, :]

    def put_slot_rows(ref, s, i, value):
        if tiled:
            for g in range(wide // 128):
                ref[s, g, pl.ds(i, nb, stride=slots), :] = value[:, g * 128 : (g + 1) * 128]
        else:
            ref[s, :, i, :] = value

    def exchange(s, src, dst, which):
        def send(d, carry):
            peer = lax.rem(me + d, nb)
            pltpu.make_async_remote_copy(
                src_ref=block_of(src, s, peer), dst_ref=block_of(dst, s, me),
                send_sem=a2a_s.at[which, s], recv_sem=a2a_r.at[which, s],
                device_id=(peer, z), device_id_type=MESH,
            ).start()
            return carry

        lax.fori_loop(1, nb, send, 0)
        block_of(dst, s, me)[...] = block_of(src, s, me)[...]

    def exchanged(s, src, dst, which):
        return pltpu.make_async_remote_copy(
            src_ref=blocks_of(src, s), dst_ref=blocks_of(dst, s),
            send_sem=a2a_s.at[which, s], recv_sem=a2a_r.at[which, s],
            device_id=(lax.rem(me + 1, nb), z), device_id_type=MESH,
        )

    def forward_rows(s, pb):
        res[...] = dot(rk[...], cols[...])
        for c in range(nz):
            first = res[c * M : (c + 1) * M, :]
            second = pltpu.roll(res[nz * M + c * M : nz * M + (c + 1) * M, :], 64, 1)
            pb[s, c, :, 0:128] = first[:, 0:128].astype(BF16)
            pb[s, c, :, 128:256] = (first[:, 128:256] + second[:, 0:128]).astype(BF16)
            pb[s, c, :, 256:384] = second[:, 128:256].astype(BF16)

    def inverse_rows(s, gb, base, target):
        spread = dot_nt(eye_ref[...], gb[s].reshape(nz * M, wide)).astype(BF16)
        left = jnp.concatenate([spread[0:K], spread[K:]], axis=1)
        keep = base[...]
        high = lax.broadcasted_iota(jnp.int32, (K, 128), 1) >= 64
        for n in range(H * 2 * COLUMN_MODES // 256):
            part = dot(left, rk[:, n * 256 : (n + 1) * 256])
            turned = pltpu.roll(part, 64, 1)
            for half in range(2):
                cut = slice(half * 128, half * 128 + 128)
                target[4 * n + 2 * half] = jnp.where(high, turned[:, cut], keep).astype(BF16)
                target[4 * n + 2 * half + 1] = jnp.where(high, part[:, cut], keep).astype(BF16)

    def pair_of(ref, s, p):
        return jnp.concatenate([ref[s, 2 * p], ref[s, 2 * p + 1]], axis=1)

    def stage_a(s):
        x_copy(s).wait()

        def some(blk, carry):
            for u in range(4):
                p = blk * 4 + u
                part = dot_nt(cblk_ref[...], pair_of(xb, s, p))
                cols[pl.ds(pl.multiple_of(p * 64, 64), 64), 0:K] = part.astype(BF16)
            return carry

        lax.fori_loop(0, pairs // 4, some, 0)
        forward_rows(s, pb1)

    def stage_b(s):
        exchanged(s, xs, xr, 0).wait_recv()
        for i in range(slots):
            put_slot_rows(ps, s, i, dot_nt(slot_rows(xr, s, i).astype(BF16), bigw[i]))
        exchange(s, ps, pr, 1)

    def stage_d(s):
        exchanged(s, gs, gr, 2).wait_recv()
        for i in range(slots):
            put_slot_rows(hs, s, i, dot(slot_rows(gr, s, i).astype(BF16), bigw[i]))
        exchange(s, hs, hr, 3)

    def stage_f(s, bufs, table, src, dst, which):
        put_whole(src, s, dot(perm_ref[table], rs_final(s, bufs)))
        exchange(s, src, dst, which)

    def stage_u(s, bufs, table, src, dst, which):
        exchanged(s, src, dst, which).wait_recv()
        bufs[0][s, z] = dot(perm_ref[table], whole_of(dst, s).astype(BF16)).astype(BF16)
        ag_hop(0, s, bufs)

    def stage_c(s, half):
        slot = lax.rem(s, 2)
        if half == 0:
            @pl.when(s >= 1)
            def _():
                out_copy(s - 1).wait()

            @pl.when(s + 1 < S)
            def _():
                ct_copy(s + 1).start()

            inverse_rows(s, gb1, ktb, l2)
            ct_copy(s).wait()
        f = factor[s]

        def some(blk, carry):
            for u in range(4):
                p = blk * 4 + u
                x2 = pair_of(xb, s, p)
                both = jnp.concatenate([x2, cblk_ref[...]], axis=0)
                branch = dot(jnp.concatenate([kt1[...], l2[p]], axis=1), both)
                v = f * branch
                square = v * v
                rise = 0.5 + 0.5 * jnp.tanh(v * (GELU_A + GELU_B * square))
                y = x2.astype(F32) + v * rise
                slope = rise + rise * (1.0 - rise) * (v * (2.0 * GELU_A + 6.0 * GELU_B * square))
                c2 = pair_of(cb, slot, p).astype(F32)
                g2 = (f * c2 * slope).astype(BF16)
                y = y.astype(BF16)
                for e in range(2):
                    cb[slot, 2 * p + e] = y[:, e * W : (e + 1) * W]
                    xb[s, 2 * p + e] = g2[:, e * W : (e + 1) * W]
                back = dot_nt(both, g2)
                gk_ref[...] += back[0:K]
                cols[pl.ds(pl.multiple_of(p * 64, 64), 64), 0:K] = back[K:].astype(BF16)
            return carry

        lax.fori_loop(half * (pairs // 8), (half + 1) * (pairs // 8), some, 0)
        if half == 1:
            out_copy(s).start()
            g_copy(s).start()
            forward_rows(s, pb2)

    def pa_copy(peer):
        return pltpu.make_async_remote_copy(
            src_ref=pa.at[me], dst_ref=pa.at[me], send_sem=pa_s.at[0], recv_sem=pa_r.at[0],
            device_id=(peer, z), device_id_type=MESH,
        )

    def pz_copy(peer):
        return pltpu.make_async_remote_copy(
            src_ref=pz.at[z], dst_ref=pz.at[z], send_sem=pz_s.at[0], recv_sem=pz_r.at[0],
            device_id=(me, peer), device_id_type=MESH,
        )

    def all_but_one(ref, count, ssem, rsem, device):
        rest = ref.at[pl.ds(0, count - 1)]
        return pltpu.make_async_remote_copy(
            src_ref=rest, dst_ref=rest, send_sem=ssem.at[0], recv_sem=rsem.at[0],
            device_id=device, device_id_type=MESH,
        )

    def point_first():
        left = gk_ref[...]
        total = jnp.zeros((channels, K), F32)
        for part in range(3):
            term = left.astype(BF16)
            left = left - term.astype(F32)
            turned = dot_nt(eye_ref[0:K, 0:K], term).astype(BF16)
            for k in range(4):
                total += dot_nt(turned[k * channels : (k + 1) * channels], pi[k, 0:K, 0:K])
        pa[me] = total

        def send(d, carry):
            pa_copy(lax.rem(me + d, nb)).start()
            return carry

        lax.fori_loop(1, nb, send, 0)

    def point_second():
        all_but_one(pa, nb, pa_s, pa_r, (lax.rem(me + 1, nb), z)).wait_recv()
        pz[z] = jnp.sum(pa[...], axis=0)

        def send(d, carry):
            pz_copy(lax.rem(z + d, nz)).start()
            return carry

        lax.fori_loop(1, nz, send, 0)

    def point_third():
        all_but_one(pz, nz, pz_s, pz_r, (me, lax.rem(z + 1, nz))).wait_recv()
        pg_ref[...] = jnp.sum(pz[...], axis=0)

    def slot_gradients():
        for i in range(slots):
            g_all = jnp.concatenate([slot_rows(gr, s, i) for s in range(S)], axis=0)
            x_all = jnp.concatenate([slot_rows(xr, s, i) for s in range(S)], axis=0)
            g_turned = dot_nt(eye_ref[...], g_all.astype(BF16)).astype(BF16)
            bigw[i] = dot(g_turned, x_all.astype(BF16)).astype(BF16)

        dw_ref[...] = jnp.zeros_like(dw_ref)

        def fold(kq, carry):
            rows = pl.ds(pl.multiple_of(kq * channels, channels), channels)
            block = jnp.concatenate([bigw[i, rows, :] for i in range(slots)], axis=0)
            dw_ref[...] += dot_nt(block, pi[kq]).reshape(slots, channels, wide)
            return carry

        lax.fori_loop(0, 8, fold, 0)

    rs1 = (pb1, rb1, rs1_s, rs1_r)
    rs2 = (pb2, rb2, rs2_s, rs2_r)
    ag1 = (gb1, ag1_s, ag1_r)
    ag2 = (gb2, ag2_s, ag2_r)

    schedule = []
    schedule += [(2, lambda s: ag_hop(1, s, ag1)), (3, lambda s: rs_hop(1, s, rs2)), (5, lambda s: ag_hop(2, s, ag2))]
    schedule += [(0, stage_a), (0, lambda s: rs_hop(0, s, rs1)), (4, stage_d)]
    schedule += [(2, lambda s: ag_hop(2, s, ag1)), (3, lambda s: rs_hop(2, s, rs2)), (0, lambda s: rs_hop(1, s, rs1))]
    schedule += [(1, stage_b), (5, lambda s: ag_hop(3, s, ag2))]
    schedule += [(0, lambda s: rs_hop(2, s, rs1)), (3, lambda s: stage_f(s, rs2, 2, gs, gr, 2))]
    schedule += [(4, lambda s: stage_u(s, ag2, 3, hs, hr, 3)), (2, lambda s: ag_hop(3, s, ag1)), (2, lambda s: stage_c(s, 0))]
    schedule += [(0, lambda s: stage_f(s, rs1, 0, xs, xr, 0)), (1, lambda s: stage_u(s, ag1, 1, ps, pr, 1))]
    schedule += [(4, lambda s: ag_hop(1, s, ag2)), (2, lambda s: stage_c(s, 1)), (2, lambda s: rs_hop(0, s, rs2))]
    steps = S + max(lag for lag, _ in schedule)
    at_step = {S + 2: point_first, S + 3: point_second, S + 4: slot_gradients}

    pl.semaphore_wait(barrier, nb + nz - 2)

    def iteration(t, carry):
        for lag, stage in schedule:
            s = t - lag
            pl.when((s >= 0) & (s < S))(functools.partial(stage, s))
        for step, work in at_step.items():
            pl.when(t == step)(work)
        return carry

    lax.fori_loop(0, steps, iteration, 0)
    point_third()

    def finish(s, carry):
        for j in range(last):
            rs_hop(j, s, rs1, True)
            rs_hop(j, s, rs2, True)
            ag_hop(j, s, ag1, True)
            ag_hop(j, s, ag2, True)
        for which, (src, dst) in enumerate(((xs, xr), (ps, pr), (gs, gr), (hs, hr))):
            exchanged(s, src, dst, which).wait_send()
        g_copy(s).wait()
        return carry

    lax.fori_loop(0, S, finish, 0)
    all_but_one(pa, nb, pa_s, pa_r, (lax.rem(me + 1, nb), z)).wait_send()
    all_but_one(pz, nz, pz_s, pz_r, (me, lax.rem(z + 1, nz))).wait_send()
    out_copy(S - 1).wait()


def field_gradient_kernel(
    sizes, rk_hbm, kk_ref, eye_ref, cblk_ref, gb2_ref, g_ref, ct_ref, ig_ref, rk, left, l2, sem
):
    nz, H, K, W, M, parts = sizes
    wide = 2 * K
    part = pl.program_id(1)
    z = lax.axis_index("row")

    @pl.when((pl.program_id(0) == 0) & (part == 0))
    def _():
        load = pltpu.make_async_copy(rk_hbm.at[z], rk, sem.at[0])
        load.start()
        load.wait()

    @pl.when(part == 0)
    def _():
        spread = dot_nt(eye_ref[...], gb2_ref[0].reshape(nz * M, wide)).astype(BF16)
        left[:, 0 : nz * M] = spread[0:K]
        left[:, nz * M :] = spread[K:]

    high = lax.broadcasted_iota(jnp.int32, (K, 128), 1) >= 64
    keep = kk_ref[:, 128:256]
    first = kk_ref[:, 0:128].astype(BF16)
    quads = H // 4 // parts
    span = quads * 128
    across = dot(left[...], rk[:, pl.ds(pl.multiple_of(part * span, span), span)])
    for n in range(quads // 2):
        cut = across[:, n * 256 : (n + 1) * 256]
        turned = pltpu.roll(cut, 64, 1)
        for half in range(2):
            lanes = slice(half * 128, half * 128 + 128)
            l2[4 * n + 2 * half] = jnp.where(high, turned[:, lanes], keep).astype(BF16)
            l2[4 * n + 2 * half + 1] = jnp.where(high, cut[:, lanes], keep).astype(BF16)

    for p in range(H // 2 // parts):
        pair = jnp.concatenate([g_ref[0, 2 * p], g_ref[0, 2 * p + 1]], axis=1)
        both = jnp.concatenate([pair, cblk_ref[...]], axis=0)
        y = dot(jnp.concatenate([first, l2[p]], axis=1), both)
        c2 = jnp.concatenate([ct_ref[0, 2 * p], ct_ref[0, 2 * p + 1]], axis=1)
        y = (y + c2.astype(F32)).astype(BF16)
        ig_ref[0, 2 * p] = y[:, 0:W]
        ig_ref[0, 2 * p + 1] = y[:, W : 2 * W]


def orthogonalize(matrices):
    norm_size = jnp.sqrt(jnp.sum(matrices * matrices, axis=(-2, -1), keepdims=True))
    current = matrices / (norm_size + 1e-07)
    for repeat in range(5):
        gram_matrix = jnp.einsum("...ij,...kj->...ik", current, current, precision=PRECISE)
        polynomial = QUINTIC_SECOND * gram_matrix + QUINTIC_THIRD * jnp.einsum(
            "...ij,...jk->...ik", gram_matrix, gram_matrix, precision=PRECISE
        )
        current = QUINTIC_FIRST * current + jnp.einsum(
            "...ij,...jk->...ik", polynomial, current, precision=PRECISE
        )
    return current


def per_device(
    input_field,
    cotangent,
    sample_scale,
    scale_table,
    owner_map,
    spectral_master,
    spectral_momentum,
    pointwise_master,
    pointwise_momentum,
):
    S, H, K, W = input_field.shape
    nz = lax.axis_size("row")
    nb = lax.axis_size("batch")
    z = lax.axis_index("row")
    slots = spectral_master.shape[0]
    channels = K // 4
    wide = 2 * K
    local_columns = COLUMN_MODES // nz
    M = ROW_MODES * local_columns
    grid = H * nz

    group_mode = lax.dynamic_index_in_dim(owner_map.reshape(nb, nz, slots), z, 1, False).reshape(nb * slots)
    group_local = group_mode // COLUMN_MODES * local_columns + group_mode % local_columns
    local_ids = jnp.arange(M, dtype=jnp.int32)
    to_slots = (group_local[:, None] == local_ids[None, :]).astype(F32)
    column = z * local_columns + local_ids % local_columns
    weight = jnp.where(column == 0, 1.0, 2.0) / (grid * grid)
    to_modes = (group_local[None, :] == local_ids[:, None]).astype(F32)
    perms = jnp.stack(
        [to_slots, to_modes * weight[:, None], to_slots * weight[None, :], to_modes]
    ).astype(BF16)
    factors = jnp.take(scale_table, sample_scale)

    anywhere = pl.BlockSpec(memory_space=pl.ANY)
    vmem = pl.BlockSpec(memory_space=pltpu.VMEM)
    exchange_shape = (S, wide // 128, nb * slots, 128) if slots % 8 == 0 else (S, nb, slots, wide)
    dma = pltpu.SemaphoreType.DMA
    row_table = jnp.asarray(row_blocks(grid, nz))
    column_rows = jnp.asarray(column_block(W))
    unit = jnp.asarray(np.eye(wide).astype(ml_dtypes.bfloat16))
    output_field, grad_branch, spectral_grad, pointwise_grad, kernel_back, grad_spectra = pl.pallas_call(
        functools.partial(layer_kernel, (nb, nz, S, H, K, W, slots, M)),
        out_shape=(
            jax.ShapeDtypeStruct(input_field.shape, BF16),
            jax.ShapeDtypeStruct(input_field.shape, BF16),
            jax.ShapeDtypeStruct(spectral_master.shape, F32),
            jax.ShapeDtypeStruct(pointwise_master.shape, F32),
            jax.ShapeDtypeStruct((K, 256), F32),
            jax.ShapeDtypeStruct((S, nz, M, wide), BF16),
        ),
        in_specs=[
            anywhere, anywhere, pl.BlockSpec(memory_space=pltpu.SMEM), anywhere, anywhere,
            vmem, vmem, vmem, vmem, vmem,
        ],
        out_specs=(anywhere, anywhere, vmem, vmem, vmem, vmem),
        scratch_shapes=[
            pltpu.VMEM((S, H, K, W), BF16),
            pltpu.VMEM((2, H, K, W), BF16),
            pltpu.VMEM((2 * nz * M, H * 2 * COLUMN_MODES), BF16),
            pltpu.VMEM((8, wide, wide), BF16),
            pltpu.VMEM((slots, wide, wide), BF16),
            pltpu.VMEM((H * 2 * COLUMN_MODES, 256), BF16),
            pltpu.VMEM((2 * nz * M, 256), F32),
            pltpu.VMEM((H // 2, K, 128), BF16),
            pltpu.VMEM((K, 128), BF16),
            pltpu.VMEM((K, 128), F32),
            pltpu.VMEM((M, wide), F32),
            pltpu.VMEM((K, K), F32),
            pltpu.VMEM((nb, channels, K), F32),
            pltpu.VMEM((nz, channels, K), F32),
            pltpu.VMEM((S, nz, M, wide), BF16),
            pltpu.VMEM((S, 2, nz, M, wide), BF16),
            pltpu.VMEM((S, nz, M, wide), BF16),
            pltpu.VMEM((S, nz, M, wide), BF16),
            pltpu.VMEM((S, 2, nz, M, wide), BF16),
        ]
        + [pltpu.VMEM(exchange_shape, F32)] * 8
        + [dma((S,)), dma((S,)), dma((2,)), dma((2,)), dma((2,))]
        + [dma((1,))] * 4
        + [dma((S, 2, nz))] * 4
        + [dma((S, 2, nz)), dma((S, nz))] * 2
        + [dma((4, S))] * 2,
        compiler_params=pltpu.CompilerParams(
            collective_id=0, has_side_effects=True, vmem_limit_bytes=62 * 1024 * 1024
        ),
    )(
        input_field,
        cotangent,
        factors,
        row_table,
        jnp.asarray(product_signs(channels)),
        column_rows,
        unit,
        perms,
        spectral_master,
        pointwise_master,
    )

    parts = 2
    rows_block = pl.BlockSpec((1, H // parts, K, W), lambda s, p: (s, p, 0, 0))
    input_grad = pl.pallas_call(
        functools.partial(field_gradient_kernel, (nz, H, K, W, M, parts)),
        out_shape=jax.ShapeDtypeStruct(input_field.shape, BF16),
        grid=(S, parts),
        in_specs=[
            anywhere, vmem, vmem, vmem,
            pl.BlockSpec((1, nz, M, wide), lambda s, p: (s, 0, 0, 0)), rows_block, rows_block,
        ],
        out_specs=rows_block,
        scratch_shapes=[
            pltpu.VMEM((2 * nz * M, H * 2 * COLUMN_MODES), BF16),
            pltpu.VMEM((K, 2 * nz * M), BF16),
            pltpu.VMEM((H // 2 // parts, K, 128), BF16),
            dma((1,)),
        ],
        compiler_params=pltpu.CompilerParams(vmem_limit_bytes=48 * 1024 * 1024),
    )(row_table, kernel_back, unit, column_rows, grad_spectra, grad_branch, cotangent)

    spectral_moment = MOMENTUM_DECAY * spectral_momentum + spectral_grad
    spectral_weight = spectral_master - SPECTRAL_RATE * orthogonalize(spectral_moment)
    pointwise_moment = MOMENTUM_DECAY * pointwise_momentum + pointwise_grad
    pointwise_weight = pointwise_master - POINTWISE_RATE * orthogonalize(pointwise_moment)
    return (
        output_field,
        input_grad,
        spectral_grad,
        spectral_moment,
        spectral_weight,
        spectral_weight.astype(BF16),
        pointwise_grad,
        pointwise_moment,
        pointwise_weight,
        pointwise_weight.astype(BF16),
    )


def solution(mesh):
    return jax.shard_map(
        per_device,
        mesh=mesh,
        in_specs=(
            P("batch", "row", None, None),
            P("batch", "row", None, None),
            P("batch"),
            P(),
            P(),
            P(("batch", "row"), None, None),
            P(("batch", "row"), None, None),
            P(),
            P(),
        ),
        out_specs=(
            P("batch", "row", None, None),
            P("batch", "row", None, None),
            P(("batch", "row"), None, None),
            P(("batch", "row"), None, None),
            P(("batch", "row"), None, None),
            P(("batch", "row"), None, None),
            P(),
            P(),
            P(),
            P(),
        ),
        check_vma=False,
    )
```

```python
import functools
import math

import jax
import jax.numpy as jnp
import ml_dtypes
import numpy as np
from jax import lax
from jax.experimental import pallas as pl
from jax.experimental.pallas import tpu as pltpu
from jax.sharding import PartitionSpec as P

ROW_MODES = 16
COLUMN_MODES = 16

BLADE_SIGNS = np.array([[1, 1, 1, 1], [1, 1, 1, 1], [1, -1, 1, -1], [1, -1, 1, -1]], np.float32)
QUINTIC_FIRST = 3.4445
QUINTIC_SECOND = -4.775
QUINTIC_THIRD = 2.0315
SPECTRAL_RATE = 4.0
POINTWISE_RATE = 0.8
MOMENTUM_DECAY = 0.5
MESH = pl.DeviceIdType.MESH
F32 = jnp.float32
BF16 = jnp.bfloat16
GELU_A = math.sqrt(2.0 / math.pi)
GELU_B = GELU_A * 0.044715


MATRIX_SIGNS = np.zeros((2, 2, 4), np.float32)
MATRIX_SIGNS[0, 0, 0] = MATRIX_SIGNS[0, 0, 1] = MATRIX_SIGNS[1, 1, 0] = 1.0
MATRIX_SIGNS[1, 1, 1] = MATRIX_SIGNS[1, 0, 3] = -1.0
MATRIX_SIGNS[0, 1, 2] = MATRIX_SIGNS[0, 1, 3] = MATRIX_SIGNS[1, 0, 2] = 1.0


def column_block(grid_size, row_count):
    angles = 2.0 * np.pi / grid_size * (np.arange(COLUMN_MODES)[:, None] * np.arange(grid_size)[None] % grid_size)
    table = np.stack([np.cos(angles), -np.sin(angles)], 0).reshape(2, row_count, -1, grid_size)
    full = np.einsum("pclw,hg->chplgw", table, np.eye(2))
    return full.reshape(4 * COLUMN_MODES, 2 * grid_size).astype(ml_dtypes.bfloat16)


def row_blocks(grid_size, row_count):
    rows = grid_size // row_count
    local = COLUMN_MODES // row_count
    r = np.arange(ROW_MODES)
    frequency = np.where(r < ROW_MODES // 2, r, grid_size - ROW_MODES + r)
    angles = 2.0 * np.pi / grid_size * (frequency[:, None] * np.arange(grid_size)[None] % grid_size)
    cosine, sine = np.cos(angles), np.sin(angles)
    table = np.stack([np.stack([cosine, sine], -1), np.stack([-sine, cosine], -1)], 0)
    table = table.reshape(2, ROW_MODES, row_count, rows, 2)
    single = np.einsum("qrzhp,cd->zqrchpd", table, np.eye(local))
    single = single.reshape(row_count, 2 * ROW_MODES * local, rows * 2 * local).astype(ml_dtypes.bfloat16)
    parts = single.reshape(row_count, 2 * ROW_MODES * local, rows // 2, 4 * local)
    every = np.zeros((row_count, row_count, parts.shape[1], rows // 2, row_count, 4 * local), ml_dtypes.bfloat16)
    for group in range(row_count):
        every[:, group, :, :, group, :] = parts
    return single, every.reshape(row_count, 4 * ROW_MODES * COLUMN_MODES // 2, rows * 2 * COLUMN_MODES)


def lanes_of_columns(channels):
    half = 4 * channels
    place = np.arange(2 * half)
    cut = half // 128 * 128
    first = np.arange(half)
    second = np.where(first < cut, half + (half - cut) + first, half + first - cut)
    return place[first], place[second]


def product_signs(channels):
    unit = np.eye(channels, dtype=np.float32)
    psi = np.zeros((2, 2, 2, 4, 2, 2), np.float32)
    for q in range(2):
        for p in range(2):
            part = -1.0 if (q == 0 and p == 1) else 1.0
            for row in range(2):
                for inner in range(2):
                    psi[q, row, p ^ q, :, p, inner] = part * MATRIX_SIGNS[row, inner]
    psi = np.einsum("qrwapn,ij->qrwaipnj", psi, unit).reshape(4, 8 * channels, 4 * channels)
    psi = np.pad(psi, ((0, 0), (0, 0), (0, 256 - 4 * channels)))
    spread = np.einsum("pt,ncb,ij->pbictnj", np.eye(2), MATRIX_SIGNS, unit)
    spread = spread.reshape(8 * channels, 2, 4 * channels)
    turn = np.zeros((8 * channels, 8 * channels), np.float32)
    for col, lanes in enumerate(lanes_of_columns(channels)):
        turn[:, lanes] = spread[:, col]
    point = np.zeros((4, 4, 4), np.float32)
    for k in range(4):
        for b in range(4):
            point[k, k ^ b, b] = BLADE_SIGNS[k ^ b, b]
    point = np.einsum("kab,ij->kaibj", point, unit).reshape(4, 4 * channels, 4 * channels)
    point = np.pad(point, ((0, 0), (0, 0), (0, 256 - 4 * channels)))
    return (one.astype(ml_dtypes.bfloat16) for one in (psi, turn, point))


def dot(a, b):
    return lax.dot_general(a, b, (((1,), (0,)), ((), ())), preferred_element_type=F32)


def dot_nt(a, b):
    return lax.dot_general(a, b, (((1,), (1,)), ((), ())), preferred_element_type=F32)


def layer_kernel(
    sizes,
    x_hbm, ct_hbm, scale_ref, table_ref, owner_ref, single_hbm, every_hbm, psi_hbm, master_hbm, momentum_hbm,
    turn_ref, sign_ref, cblk_ref, eye_ref, point_ref, point_momentum_ref,
    ob, xb, dw_ref, pg_ref, turned_ref, point_turned_ref,
    eb, single, every, psi, master_ref, momentum_ref, wm, cols, l2, kt1, ktb, kk1, kkb, acc, gk_ref, pa, pz,
    lows, highs, perm_ref, back_ref,
    pb1, rb1, gb1, pb2, rb2, gb2,
    xs, xr, ps, pr, gs, gr, hs, hr,
    x_sem, ct_sem, ld_sem, ei_sem, pa_s, pa_r, pz_s, pz_r,
    rs1_s, rs1_r, rs2_s, rs2_r, ag1_s, ag1_r, ag2_s, ag2_r, a2a_s, a2a_r,
):
    nb, nz, S, H, K, W, slots, M = sizes
    wide = 2 * K
    channels = K // 4
    pairs = H // 2
    me = lax.axis_index("batch")
    z = lax.axis_index("row")
    last = nz - 1

    loads = [
        pltpu.make_async_copy(psi_hbm, psi, ld_sem.at[0]),
        pltpu.make_async_copy(single_hbm.at[z], single, ld_sem.at[1]),
        pltpu.make_async_copy(every_hbm.at[z], every, ld_sem.at[2]),
        pltpu.make_async_copy(master_hbm, master_ref, ld_sem.at[3]),
        pltpu.make_async_copy(momentum_hbm, momentum_ref, ld_sem.at[4]),
    ]
    x_copy = lambda s: pltpu.make_async_copy(x_hbm.at[s], xb.at[s], x_sem.at[s])
    ct_copy = lambda s: pltpu.make_async_copy(ct_hbm.at[s], ob.at[s], ct_sem.at[s])
    ect_copy = lambda s: pltpu.make_async_copy(ct_hbm.at[s], eb.at[lax.rem(s, 2)], ei_sem.at[lax.rem(s, 2)])

    barrier = pltpu.get_barrier_semaphore()

    def greet(d, carry):
        peer = lax.rem(me + d, nb)
        pl.semaphore_signal(barrier, inc=1, device_id=(peer, z), device_id_type=MESH)
        return carry

    lax.fori_loop(1, nb, greet, 0)

    def greet_z(d, carry):
        pl.semaphore_signal(barrier, inc=1, device_id=(me, lax.rem(z + d, nz)), device_id_type=MESH)
        return carry

    lax.fori_loop(1, nz, greet_z, 0)
    for one in loads:
        one.start()

    def load_x(s, carry):
        x_copy(s).start()
        return carry

    def load_ct(s, carry):
        ct_copy(s).start()
        return carry

    lax.fori_loop(0, S, load_x, 0)
    lax.fori_loop(0, S, load_ct, 0)
    ect_copy(0).start()
    cols[...] = jnp.zeros_like(cols)
    gk_ref[...] = jnp.zeros_like(gk_ref)
    wm[...] = jnp.zeros_like(wm)

    local = COLUMN_MODES // nz
    lane = lax.broadcasted_iota(jnp.int32, (1, 2 * M), 1)

    def place(d, carry):
        for i in range(slots):
            mode = owner_ref[(d * nz + z) * slots + i]
            at = lax.div(mode, COLUMN_MODES) * local + lax.rem(mode, local)
            lows[pl.ds(d * slots + i, 1), :] = jnp.where(lane == at, 1.0, 0.0)
            highs[pl.ds(d * slots + i, 1), :] = jnp.where(lane == at + M, 1.0, 0.0)
        return carry

    lax.fori_loop(0, nb, place, 0)
    inner = 1.0 / (H * nz * H * nz)
    weigh = jnp.where(z * local + lax.rem(lane, local) == 0, 0.5 * inner, inner)
    for table, pick in enumerate((lambda v: v[...], lambda v: v[...] * weigh)):
        perm_ref[table] = pick(lows)[:, 0:M].astype(BF16)
        back_ref[1 - table, 0] = pick(lows).astype(BF16)
        back_ref[1 - table, 1] = pick(highs).astype(BF16)

    weight = point_ref[...].astype(BF16)
    kernel_t = jnp.concatenate([dot(weight, sign_ref[k]) for k in range(4)], axis=0)
    kt1[...] = kernel_t[:, 0:128].astype(BF16)
    ktb[...] = kernel_t[:, 128:256]
    padded = jnp.concatenate([kernel_t.astype(BF16), jnp.zeros((256 - K, 256), BF16)], axis=0)
    kernel_n = dot_nt(eye_ref[0:K], padded)
    kk1[...] = kernel_n[:, 0:128].astype(BF16)
    kkb[...] = kernel_n[:, 128:256]
    for one in loads:
        one.wait()
    masters = master_ref[...].reshape(slots * channels, wide).astype(BF16)
    for part in range(4):
        block = dot(masters, psi[part]).astype(BF16)
        for i in range(slots):
            wm[i, part * channels : (part + 1) * channels, :] = block[i * channels : (i + 1) * channels]

    def rs_copy(s, up, c, pb, rb, ssem, rsem):
        way = 0 if up else 1
        return pltpu.make_async_remote_copy(
            src_ref=pb.at[s, c], dst_ref=rb.at[s, way, c],
            send_sem=ssem.at[s, way, c], recv_sem=rsem.at[s, way, c],
            device_id=(me, z + 1 if up else z - 1), device_id_type=MESH,
        )

    def rs_hop(j, s, bufs, finish=False):
        pb, rb = bufs[0], bufs[1]
        for up in (True, False):
            place = z if up else last - z
            c = (last - j + z) if up else (z - (last - j))

            @pl.when(place <= j)
            def _():
                copy = rs_copy(s, up, c, *bufs)
                if finish:
                    copy.wait_send()
                else:
                    @pl.when(place > 0)
                    def _():
                        way = 0 if up else 1
                        copy.wait_recv()
                        pb[s, c] = (pb[s, c].astype(F32) + rb[s, way, c].astype(F32)).astype(BF16)

                    copy.start()

    def rs_final(s, bufs):
        pb, rb = bufs[0], bufs[1]
        acc[...] = pb[s, z].astype(F32)

        @pl.when(z > 0)
        def _():
            rs_copy(s, True, z, *bufs).wait_recv()
            acc[...] += rb[s, 0, z].astype(F32)

        @pl.when(z < last)
        def _():
            rs_copy(s, False, z, *bufs).wait_recv()
            acc[...] += rb[s, 1, z].astype(F32)

        return acc[...].astype(BF16)

    def ag_copy(s, up, c, gb, ssem, rsem):
        way = 0 if up else 1
        return pltpu.make_async_remote_copy(
            src_ref=gb.at[s, c], dst_ref=gb.at[s, c],
            send_sem=ssem.at[s, way, c], recv_sem=rsem.at[s, c],
            device_id=(me, z + 1 if up else z - 1), device_id_type=MESH,
        )

    def ag_hop(j, s, bufs, finish=False):
        for up in (True, False):
            c = z - j if up else z + j
            more = z < last if up else z > 0

            @pl.when((c >= 0) if up else (c <= last))
            def _():
                copy = ag_copy(s, up, c, *bufs)
                if j > 0 and not finish:
                    copy.wait_recv()

                if j < last:
                    @pl.when(more)
                    def _():
                        if finish:
                            copy.wait_send()
                        else:
                            copy.start()

    tiled = slots % 8 == 0

    def block_of(ref, s, d):
        if tiled:
            return ref.at[s, :, pl.ds(pl.multiple_of(d * slots, slots), slots)]
        return ref.at[s, d]

    def blocks_of(ref, s):
        if tiled:
            return ref.at[s, :, pl.ds(0, (nb - 1) * slots)]
        return ref.at[s, pl.ds(0, nb - 1)]

    def whole_of(ref, s):
        if tiled:
            return jnp.concatenate([ref[s, g] for g in range(wide // 128)], axis=1)
        return ref[s].reshape(nb * slots, wide)

    def put_whole(ref, s, value):
        if tiled:
            for g in range(wide // 128):
                ref[s, g] = value[:, g * 128 : (g + 1) * 128]
        else:
            ref[s] = value.reshape(nb, slots, wide)

    def slot_rows(ref, s, i):
        if tiled:
            return jnp.concatenate([ref[s, g, pl.ds(i, nb, stride=slots), :] for g in range(wide // 128)], axis=1)
        return ref[s, :, i, :]

    def put_slot_rows(ref, s, i, value):
        if tiled:
            for g in range(wide // 128):
                ref[s, g, pl.ds(i, nb, stride=slots), :] = value[:, g * 128 : (g + 1) * 128]
        else:
            ref[s, :, i, :] = value

    def exchange(s, src, dst, which):
        def send(d, carry):
            peer = lax.rem(me + d, nb)
            pltpu.make_async_remote_copy(
                src_ref=block_of(src, s, peer), dst_ref=block_of(dst, s, me),
                send_sem=a2a_s.at[which, s], recv_sem=a2a_r.at[which, s],
                device_id=(peer, z), device_id_type=MESH,
            ).start()
            return carry

        lax.fori_loop(1, nb, send, 0)
        block_of(dst, s, me)[...] = block_of(src, s, me)[...]

    def exchanged(s, src, dst, which):
        return pltpu.make_async_remote_copy(
            src_ref=blocks_of(src, s), dst_ref=blocks_of(dst, s),
            send_sem=a2a_s.at[which, s], recv_sem=a2a_r.at[which, s],
            device_id=(lax.rem(me + 1, nb), z), device_id_type=MESH,
        )

    def forward_rows(s, pb):
        for c in range(nz):
            part = dot(single[...], cols[c])
            first = part[0:M]
            second = pltpu.roll(part[M:], 64, 1)
            pb[s, c, :, 0:128] = first[:, 0:128].astype(BF16)
            pb[s, c, :, 128:256] = (first[:, 128:256] + second[:, 0:128]).astype(BF16)
            pb[s, c, :, 256:384] = second[:, 128:256].astype(BF16)

    def put_columns(p, value):
        step = 4 * COLUMN_MODES // nz
        for c in range(nz):
            cols[c, pl.ds(pl.multiple_of(p * step, step), step), 0:K] = value[c * step : (c + 1) * step]

    def pair_of(ref, s, p):
        return jnp.concatenate([ref[s, 2 * p], ref[s, 2 * p + 1]], axis=1)

    def stage_a(s):
        x_copy(s).wait()

        def some(blk, carry):
            for u in range(4):
                p = blk * 4 + u
                part = dot_nt(cblk_ref[...], pair_of(xb, s, p))
                put_columns(p, part.astype(BF16))
            return carry

        lax.fori_loop(0, pairs // 4, some, 0)
        forward_rows(s, pb1)
        rs_hop(0, s, rs1)

    def by_column(ref, s, i):
        rows = slot_rows(ref, s, i)
        low, mid, top = rows[:, 0:128], rows[:, 128:256], rows[:, 256:384]
        first = jnp.concatenate([low, mid], axis=1)
        second = jnp.concatenate([top, pltpu.roll(mid, 64, 1)], axis=1)
        return jnp.concatenate([first, second], axis=0).astype(BF16)

    def put_by_column(ref, s, i, value):
        first, second = value[0:nb], value[nb:]
        mid = first[:, 128:256] + pltpu.roll(second[:, 128:256], 64, 1)
        put_slot_rows(ref, s, i, jnp.concatenate([first[:, 0:128], mid, second[:, 0:128]], axis=1))

    def stage_b(s):
        exchanged(s, xs, xr, 0).wait_recv()
        for i in range(slots):
            put_by_column(ps, s, i, dot_nt(by_column(xr, s, i), wm[i]))
        exchange(s, ps, pr, 1)

    def stage_d(s):
        exchanged(s, gs, gr, 2).wait_recv()
        for i in range(slots):
            put_by_column(hs, s, i, dot(by_column(gr, s, i), wm[i]))
        exchange(s, hs, hr, 3)

    def stage_f(s, bufs, table, src, dst, which):
        placed = dot(perm_ref[table], rs_final(s, bufs)).astype(BF16)
        put_whole(src, s, dot(placed, turn_ref[...]))
        exchange(s, src, dst, which)

    def stage_u(s, bufs, table, src, dst, which):
        exchanged(s, src, dst, which).wait_recv()
        turned = jnp.transpose(whole_of(dst, s))
        cut = K // 128 * 128
        first = turned[0:K]
        second = jnp.concatenate([turned[2 * K - cut :], turned[K : 2 * K - cut]], axis=0)
        parts = []
        for q in range(2):
            base = 2 * q * channels
            at = lambda col, row: col[base + row * channels : base + (row + 1) * channels]
            m00, m10, m01, m11 = at(first, 0), at(first, 1), at(second, 0), at(second, 1)
            parts.append(jnp.concatenate([m00 + m11, m00 - m11, m01 + m10, m01 - m10], axis=0).astype(BF16))
        both = dot(parts[0], back_ref[table, 0]) + dot(parts[1], back_ref[table, 1])
        bufs[0][s, z] = both.astype(BF16)
        ag_hop(0, s, bufs)

    def inverse_rows(s, gb, base):
        left = jnp.concatenate([gb[s, c] for c in range(nz)], axis=1)
        keep = base[...]
        high = lax.broadcasted_iota(jnp.int32, (K, 128), 1) >= 64
        for n in range(pairs // 4):
            part = dot(left, every[:, n * 256 : (n + 1) * 256])
            turned = pltpu.roll(part, 64, 1)
            for half in range(2):
                cut = slice(half * 128, half * 128 + 128)
                l2[4 * n + 2 * half] = jnp.where(high, turned[:, cut], keep).astype(BF16)
                l2[4 * n + 2 * half + 1] = jnp.where(high, part[:, cut], keep).astype(BF16)

    def stage_c(s):
        ag_hop(last, s, ag1)
        inverse_rows(s, gb1, ktb)
        ct_copy(s).wait()
        f = table_ref[scale_ref[s]]

        def some(blk, carry):
            for u in range(4):
                p = blk * 4 + u
                x2 = pair_of(xb, s, p)
                both = jnp.concatenate([x2, cblk_ref[...]], axis=0)
                branch = dot(jnp.concatenate([kt1[...], l2[p]], axis=1), both)
                v = f * branch
                square = v * v
                rise = 0.5 + 0.5 * jnp.tanh(v * (GELU_A + GELU_B * square))
                y = x2.astype(F32) + v * rise
                slope = rise + rise * (1.0 - rise) * (v * (2.0 * GELU_A + 6.0 * GELU_B * square))
                c2 = pair_of(ob, s, p).astype(F32)
                g2 = (f * c2 * slope).astype(BF16)
                y = y.astype(BF16)
                for e in range(2):
                    ob[s, 2 * p + e] = y[:, e * W : (e + 1) * W]
                    xb[s, 2 * p + e] = g2[:, e * W : (e + 1) * W]
                back = dot_nt(both, g2)
                gk_ref[...] += back[0:K]
                put_columns(p, back[K:].astype(BF16))
            return carry

        lax.fori_loop(0, pairs // 4, some, 0)
        forward_rows(s, pb2)
        rs_hop(0, s, rs2)

    def stage_e(s):
        slot = lax.rem(s, 2)

        @pl.when(s + 1 < S)
        def _():
            ect_copy(s + 1).start()

        ag_hop(last, s, ag2)
        inverse_rows(s, gb2, kkb)
        ect_copy(s).wait()

        def some(blk, carry):
            for u in range(4):
                p = blk * 4 + u
                both = jnp.concatenate([pair_of(xb, s, p), cblk_ref[...]], axis=0)
                y = dot(jnp.concatenate([kk1[...], l2[p]], axis=1), both)
                y = (y + pair_of(eb, slot, p).astype(F32)).astype(BF16)
                for e in range(2):
                    xb[s, 2 * p + e] = y[:, e * W : (e + 1) * W]
            return carry

        lax.fori_loop(0, pairs // 4, some, 0)

    def pa_copy(peer):
        return pltpu.make_async_remote_copy(
            src_ref=pa.at[me], dst_ref=pa.at[me], send_sem=pa_s.at[0], recv_sem=pa_r.at[0],
            device_id=(peer, z), device_id_type=MESH,
        )

    def pz_copy(peer):
        return pltpu.make_async_remote_copy(
            src_ref=pz.at[z], dst_ref=pz.at[z], send_sem=pz_s.at[0], recv_sem=pz_r.at[0],
            device_id=(me, peer), device_id_type=MESH,
        )

    def all_but_one(ref, count, ssem, rsem, device):
        rest = ref.at[pl.ds(0, count - 1)]
        return pltpu.make_async_remote_copy(
            src_ref=rest, dst_ref=rest, send_sem=ssem.at[0], recv_sem=rsem.at[0],
            device_id=device, device_id_type=MESH,
        )

    def point_first():
        left = gk_ref[...]
        total = jnp.zeros((channels, K), F32)
        for part in range(3):
            term = left.astype(BF16)
            left = left - term.astype(F32)
            turned = dot_nt(eye_ref[0:K, 0:K], term).astype(BF16)
            for k in range(4):
                total += dot_nt(turned[k * channels : (k + 1) * channels], sign_ref[k, :, 0:K])
        pa[me] = total

        def send(d, carry):
            pa_copy(lax.rem(me + d, nb)).start()
            return carry

        lax.fori_loop(1, nb, send, 0)

    def point_second():
        all_but_one(pa, nb, pa_s, pa_r, (lax.rem(me + 1, nb), z)).wait_recv()
        pz[z] = jnp.sum(pa[...], axis=0)

        def send(d, carry):
            pz_copy(lax.rem(z + d, nz)).start()
            return carry

        lax.fori_loop(1, nz, send, 0)

    def slot_gradients():
        for i in range(slots):
            g_all = jnp.concatenate([by_column(gr, s, i) for s in range(S)], axis=0)
            x_all = jnp.concatenate([by_column(xr, s, i) for s in range(S)], axis=0)
            g_turned = dot_nt(eye_ref[...], g_all).astype(BF16)
            wm[i] = dot(g_turned, x_all).astype(BF16)

        total = jnp.zeros((slots * channels, wide), F32)
        for part in range(4):
            rows = slice(part * channels, (part + 1) * channels)
            block = jnp.concatenate([wm[i, rows, :] for i in range(slots)], axis=0)
            total += dot_nt(block, psi[part])
        dw_ref[...] = total.reshape(slots, channels, wide)

    def orthogonal(moments):
        def split(v):
            high = v.astype(BF16)
            return high, (v - high.astype(F32)).astype(BF16)

        def product(a, b, mul):
            (ah, al), (bh, bl) = a, b
            return mul(ah, bh) + (mul(ah, bl) + mul(al, bh))

        current = [m / (jnp.sqrt(jnp.sum(m * m)) + 1e-07) for m in moments]
        for repeat in range(5):
            parts = [split(v) for v in current]
            grams = [product(v, v, dot_nt) for v in parts]
            gram_parts = [split(v) for v in grams]
            squares = [product(v, v, dot) for v in gram_parts]
            polynomials = [split(QUINTIC_SECOND * g + QUINTIC_THIRD * q) for g, q in zip(grams, squares)]
            current = [
                QUINTIC_FIRST * v + product(p, w, dot) for v, p, w in zip(current, polynomials, parts)
            ]
        return current

    def slot_updates(chosen):
        moments = [MOMENTUM_DECAY * momentum_ref[i] + dw_ref[i] for i in chosen]
        for i, value in zip(chosen, orthogonal(moments)):
            turned_ref[i] = value

    def point_update():
        all_but_one(pz, nz, pz_s, pz_r, (me, lax.rem(z + 1, nz))).wait_recv()
        total = jnp.sum(pz[...], axis=0)
        pg_ref[...] = total
        (point_turned_ref[...],) = orthogonal([MOMENTUM_DECAY * point_momentum_ref[...] + total])

    rs1 = (pb1, rb1, rs1_s, rs1_r)
    rs2 = (pb2, rb2, rs2_s, rs2_r)
    ag1 = (gb1, ag1_s, ag1_r)
    ag2 = (gb2, ag2_s, ag2_r)

    schedule = [
        (0, stage_a),
        (3, lambda s: stage_f(s, rs1, 0, xs, xr, 0)),
        (11, lambda s: stage_f(s, rs2, 1, gs, gr, 2)),
        (2, lambda s: rs_hop(2, s, rs1)),
        (10, lambda s: rs_hop(2, s, rs2)),
        (1, lambda s: rs_hop(1, s, rs1)),
        (9, lambda s: rs_hop(1, s, rs2)),
        (7, lambda s: ag_hop(2, s, ag1)),
        (15, lambda s: ag_hop(2, s, ag2)),
        (6, lambda s: ag_hop(1, s, ag1)),
        (14, lambda s: ag_hop(1, s, ag2)),
        (5, lambda s: stage_u(s, ag1, 0, ps, pr, 1)),
        (13, lambda s: stage_u(s, ag2, 1, hs, hr, 3)),
        (4, stage_b),
        (12, stage_d),
        (8, stage_c),
        (16, stage_e),
    ]
    steps = S + max(lag for lag, _ in schedule)
    at_step = {S + 8: point_first, S + 9: point_second, S + 11: point_update, S + 12: slot_gradients}
    groups = [range(slots)[: slots // 2], range(slots)[slots // 2 :]]
    for step, group in enumerate(groups):
        if group:
            at_step[S + 13 + step] = functools.partial(slot_updates, group)

    pl.semaphore_wait(barrier, nb + nz - 2)

    def iteration(t, carry):
        for lag, stage in schedule:
            s = t - lag
            pl.when((s >= 0) & (s < S))(functools.partial(stage, s))
        for step, work in at_step.items():
            pl.when(t == step)(work)
        return carry

    lax.fori_loop(0, steps, iteration, 0)

    def finish(s, carry):
        for j in range(last):
            rs_hop(j, s, rs1, True)
            rs_hop(j, s, rs2, True)
            ag_hop(j, s, ag1, True)
            ag_hop(j, s, ag2, True)
        for which, (src, dst) in enumerate(((xs, xr), (ps, pr), (gs, gr), (hs, hr))):
            exchanged(s, src, dst, which).wait_send()
        return carry

    lax.fori_loop(0, S, finish, 0)
    all_but_one(pa, nb, pa_s, pa_r, (lax.rem(me + 1, nb), z)).wait_send()
    all_but_one(pz, nz, pz_s, pz_r, (me, lax.rem(z + 1, nz))).wait_send()


def store_kernel(
    ob, xb, dw_ref, pg_ref, turned_ref, point_turned_ref, master_ref, momentum_ref, point_ref, point_momentum_ref,
    out_hbm, ig_hbm, grad_ref, moment_ref, weight_ref, low_ref,
    point_grad_ref, point_moment_ref, point_weight_ref, point_low_ref, sem,
):
    S = ob.shape[0]
    copies = []
    for s in range(S):
        copies.append(pltpu.make_async_copy(ob.at[s], out_hbm.at[s], sem.at[0, s]))
        copies.append(pltpu.make_async_copy(xb.at[s], ig_hbm.at[s], sem.at[1, s]))
    for copy in copies:
        copy.start()
    point_grad_ref[...] = pg_ref[...]
    point_moment_ref[...] = MOMENTUM_DECAY * point_momentum_ref[...] + pg_ref[...]
    point_weight = point_ref[...] - POINTWISE_RATE * point_turned_ref[...]
    point_weight_ref[...] = point_weight
    point_low_ref[...] = point_weight.astype(BF16)
    grad_ref[...] = dw_ref[...]
    moment_ref[...] = MOMENTUM_DECAY * momentum_ref[...] + dw_ref[...]
    weight = master_ref[...] - SPECTRAL_RATE * turned_ref[...]
    weight_ref[...] = weight
    low_ref[...] = weight.astype(BF16)
    for copy in copies:
        copy.wait()


def per_device(
    input_field,
    cotangent,
    sample_scale,
    scale_table,
    owner_map,
    spectral_master,
    spectral_momentum,
    pointwise_master,
    pointwise_momentum,
):
    S, H, K, W = input_field.shape
    nz = lax.axis_size("row")
    nb = lax.axis_size("batch")
    slots = spectral_master.shape[0]
    channels = K // 4
    wide = 2 * K
    local_columns = COLUMN_MODES // nz
    M = ROW_MODES * local_columns
    grid = H * nz

    anywhere = pl.BlockSpec(memory_space=pltpu.HBM)
    smem = pl.BlockSpec(memory_space=pltpu.SMEM)
    vmem = pl.BlockSpec(memory_space=pltpu.VMEM)
    exchange_shape = (S, wide // 128, nb * slots, 128) if slots % 8 == 0 else (S, nb, slots, wide)
    dma = pltpu.SemaphoreType.DMA
    single, every = (jnp.asarray(one) for one in row_blocks(grid, nz))
    psi, turn, signs = (jnp.asarray(one) for one in product_signs(channels))
    column_rows = jnp.asarray(column_block(W, nz))
    unit = jnp.asarray(np.eye(256).astype(ml_dtypes.bfloat16))
    slot_shape, point_shape = spectral_master.shape, pointwise_master.shape
    kept = pl.pallas_call(
        functools.partial(layer_kernel, (nb, nz, S, H, K, W, slots, M)),
        out_shape=(
            pltpu.VMEM(input_field.shape, BF16),
            pltpu.VMEM(input_field.shape, BF16),
            pltpu.VMEM(slot_shape, F32),
            pltpu.VMEM(point_shape, F32),
            pltpu.VMEM(slot_shape, F32),
            pltpu.VMEM(point_shape, F32),
        ),
        in_specs=[anywhere, anywhere, smem, smem, smem] + [anywhere] * 5 + [vmem] * 6,
        out_specs=(vmem,) * 6,
        scratch_shapes=[
            pltpu.VMEM((2, H, K, W), BF16),
            pltpu.VMEM(single.shape[1:], BF16),
            pltpu.VMEM(every.shape[1:], BF16),
            pltpu.VMEM(psi.shape, BF16),
            pltpu.VMEM(spectral_master.shape, F32),
            pltpu.VMEM(spectral_master.shape, F32),
            pltpu.VMEM((slots, 256, 256), BF16),
            pltpu.VMEM((nz, single.shape[2], 256), BF16),
            pltpu.VMEM((H // 2, K, 128), BF16),
            pltpu.VMEM((K, 128), BF16),
            pltpu.VMEM((K, 128), F32),
            pltpu.VMEM((K, 128), BF16),
            pltpu.VMEM((K, 128), F32),
            pltpu.VMEM((M, wide), F32),
            pltpu.VMEM((K, K), F32),
            pltpu.VMEM((nb, channels, K), F32),
            pltpu.VMEM((nz, channels, K), F32),
            pltpu.VMEM((M, 2 * M), F32),
            pltpu.VMEM((M, 2 * M), F32),
            pltpu.VMEM((2, M, M), BF16),
            pltpu.VMEM((2, 2, M, 2 * M), BF16),
            pltpu.VMEM((S, nz, M, wide), BF16),
            pltpu.VMEM((S, 2, nz, M, wide), BF16),
            pltpu.VMEM((S, nz, K, 2 * M), BF16),
            pltpu.VMEM((S, nz, M, wide), BF16),
            pltpu.VMEM((S, 2, nz, M, wide), BF16),
            pltpu.VMEM((S, nz, K, 2 * M), BF16),
        ]
        + [pltpu.VMEM(exchange_shape, F32)] * 8
        + [dma((S,)), dma((S,)), dma((5,)), dma((2,))]
        + [dma((1,))] * 4
        + [dma((S, 2, nz))] * 4
        + [dma((S, 2, nz)), dma((S, nz))] * 2
        + [dma((4, S))] * 2,
        compiler_params=pltpu.CompilerParams(
            collective_id=0, has_side_effects=True, vmem_limit_bytes=37 * 1024 * 1024
        ),
    )(
        input_field, cotangent, sample_scale, scale_table, owner_map, single, every, psi,
        spectral_master, spectral_momentum, turn, signs, column_rows, unit, pointwise_master, pointwise_momentum,
    )

    held = [pltpu.with_memory_space_constraint(one, pltpu.VMEM) for one in kept]
    input_shape = jax.ShapeDtypeStruct(input_field.shape, BF16)
    results = pl.pallas_call(
        store_kernel,
        out_shape=(
            input_shape,
            input_shape,
            jax.ShapeDtypeStruct(slot_shape, F32),
            jax.ShapeDtypeStruct(slot_shape, F32),
            jax.ShapeDtypeStruct(slot_shape, F32),
            jax.ShapeDtypeStruct(slot_shape, BF16),
            jax.ShapeDtypeStruct(point_shape, F32),
            jax.ShapeDtypeStruct(point_shape, F32),
            jax.ShapeDtypeStruct(point_shape, F32),
            jax.ShapeDtypeStruct(point_shape, BF16),
        ),
        in_specs=[vmem] * 10,
        out_specs=(anywhere, anywhere) + (vmem,) * 8,
        scratch_shapes=[dma((2, S))],
        compiler_params=pltpu.CompilerParams(vmem_limit_bytes=6 * 1024 * 1024),
    )(*held, spectral_master, spectral_momentum, pointwise_master, pointwise_momentum)
    return tuple(results)


def solution(mesh):
    return jax.shard_map(
        per_device,
        mesh=mesh,
        in_specs=(
            P("batch", "row", None, None),
            P("batch", "row", None, None),
            P("batch"),
            P(),
            P(),
            P(("batch", "row"), None, None),
            P(("batch", "row"), None, None),
            P(),
            P(),
        ),
        out_specs=(
            P("batch", "row", None, None),
            P("batch", "row", None, None),
            P(("batch", "row"), None, None),
            P(("batch", "row"), None, None),
            P(("batch", "row"), None, None),
            P(("batch", "row"), None, None),
            P(),
            P(),
            P(),
            P(),
        ),
        check_vma=False,
    )
```

```python
import functools
import math

import jax
import jax.numpy as jnp
import ml_dtypes
import numpy as np
from jax import lax
from jax.experimental import pallas as pl
from jax.experimental.pallas import tpu as pltpu
from jax.sharding import PartitionSpec as P

ROW_MODES = 16
COLUMN_MODES = 16

BLADE_SIGNS = np.array([[1, 1, 1, 1], [1, 1, 1, 1], [1, -1, 1, -1], [1, -1, 1, -1]], np.float32)
QUINTIC_FIRST = 3.4445
QUINTIC_SECOND = -4.775
QUINTIC_THIRD = 2.0315
SPECTRAL_RATE = 4.0
POINTWISE_RATE = 0.8
MOMENTUM_DECAY = 0.5
MESH = pl.DeviceIdType.MESH
F32 = jnp.float32
BF16 = jnp.bfloat16
GELU_A = math.sqrt(2.0 / math.pi)
GELU_B = GELU_A * 0.044715


MATRIX_SIGNS = np.zeros((2, 2, 4), np.float32)
MATRIX_SIGNS[0, 0, 0] = MATRIX_SIGNS[0, 0, 1] = MATRIX_SIGNS[1, 1, 0] = 1.0
MATRIX_SIGNS[1, 1, 1] = MATRIX_SIGNS[1, 0, 3] = -1.0
MATRIX_SIGNS[0, 1, 2] = MATRIX_SIGNS[0, 1, 3] = MATRIX_SIGNS[1, 0, 2] = 1.0


def column_block(grid_size, row_count):
    angles = 2.0 * np.pi / grid_size * (np.arange(COLUMN_MODES)[:, None] * np.arange(grid_size)[None] % grid_size)
    table = np.stack([np.cos(angles), -np.sin(angles)], 0).reshape(2, row_count, -1, grid_size)
    full = np.einsum("pclw,hg->chplgw", table, np.eye(2))
    return full.reshape(4 * COLUMN_MODES, 2 * grid_size).astype(ml_dtypes.bfloat16)


def row_blocks(grid_size, row_count):
    rows = grid_size // row_count
    local = COLUMN_MODES // row_count
    r = np.arange(ROW_MODES)
    frequency = np.where(r < ROW_MODES // 2, r, grid_size - ROW_MODES + r)
    angles = 2.0 * np.pi / grid_size * (frequency[:, None] * np.arange(grid_size)[None] % grid_size)
    cosine, sine = np.cos(angles), np.sin(angles)
    table = np.stack([np.stack([cosine, sine], -1), np.stack([-sine, cosine], -1)], 0)
    table = table.reshape(2, ROW_MODES, row_count, rows, 2)
    full = np.einsum("qrzhp,cd->zqrchpd", table, np.eye(local))
    return full.reshape(row_count, 2 * ROW_MODES * local, rows * 2 * local).astype(ml_dtypes.bfloat16)


def lanes_of_columns(channels):
    half = 4 * channels
    place = np.arange(2 * half)
    cut = half // 128 * 128
    first = np.arange(half)
    second = np.where(first < cut, half + (half - cut) + first, half + first - cut)
    return place[first], place[second]


def product_signs(channels):
    unit = np.eye(channels, dtype=np.float32)
    psi = np.zeros((2, 2, 2, 4, 2, 2), np.float32)
    for q in range(2):
        for p in range(2):
            part = -1.0 if (q == 0 and p == 1) else 1.0
            for row in range(2):
                for inner in range(2):
                    psi[q, row, p ^ q, :, p, inner] = part * MATRIX_SIGNS[row, inner]
    psi = np.einsum("qrwapn,ij->qrwaipnj", psi, unit).reshape(4, 8 * channels, 4 * channels)
    psi = np.pad(psi, ((0, 0), (0, 0), (0, 256 - 4 * channels)))
    spread = np.einsum("pt,ncb,ij->pbictnj", np.eye(2), MATRIX_SIGNS, unit)
    spread = spread.reshape(8 * channels, 2, 4 * channels)
    turn = np.zeros((8 * channels, 8 * channels), np.float32)
    for col, lanes in enumerate(lanes_of_columns(channels)):
        turn[:, lanes] = spread[:, col]
    point = np.zeros((4, 4, 4), np.float32)
    for k in range(4):
        for b in range(4):
            point[k, k ^ b, b] = BLADE_SIGNS[k ^ b, b]
    point = np.einsum("kab,ij->kaibj", point, unit).reshape(4, 4 * channels, 4 * channels)
    point = np.pad(point, ((0, 0), (0, 0), (0, 256 - 4 * channels)))
    return (one.astype(ml_dtypes.bfloat16) for one in (psi, turn, point))


def dot(a, b):
    return lax.dot_general(a, b, (((1,), (0,)), ((), ())), preferred_element_type=F32)


def dot_nt(a, b):
    return lax.dot_general(a, b, (((1,), (1,)), ((), ())), preferred_element_type=F32)


def layer_kernel(
    sizes,
    x_hbm, ct_hbm, scale_ref, table_ref, owner_ref, single_hbm, psi_hbm, master_hbm, momentum_hbm,
    turn_ref, sign_ref, cblk_ref, eye_ref, point_ref, point_momentum_ref,
    ob, xb, dw_ref, pg_ref, turned_ref, point_turned_ref,
    eb, single, psi, master_ref, momentum_ref, wm, cols, l2, kt1, ktb, kk1, kkb, acc, gk_ref, pa, pz,
    lows, highs, perm_ref, back_ref,
    pb1, rb1, gb1, pb2, rb2, gb2,
    xs, xr, ps, pr, gs, gr, hs, hr,
    x_sem, ct_sem, ld_sem, ei_sem, pa_s, pa_r, pz_s, pz_r,
    rs1_s, rs1_r, rs2_s, rs2_r, ag1_s, ag1_r, ag2_s, ag2_r, a2a_s, a2a_r,
):
    nb, nz, S, H, K, W, slots, M = sizes
    wide = 2 * K
    channels = K // 4
    pairs = H // 2
    me = lax.axis_index("batch")
    z = lax.axis_index("row")
    last = nz - 1

    loads = [
        pltpu.make_async_copy(psi_hbm, psi, ld_sem.at[0]),
        pltpu.make_async_copy(single_hbm.at[z], single, ld_sem.at[1]),
        pltpu.make_async_copy(master_hbm, master_ref, ld_sem.at[2]),
        pltpu.make_async_copy(momentum_hbm, momentum_ref, ld_sem.at[3]),
    ]
    x_copy = lambda s: pltpu.make_async_copy(x_hbm.at[s], xb.at[s], x_sem.at[s])
    ct_copy = lambda s: pltpu.make_async_copy(ct_hbm.at[s], ob.at[s], ct_sem.at[s])
    ect_copy = lambda s: pltpu.make_async_copy(ct_hbm.at[s], eb.at[lax.rem(s, 2)], ei_sem.at[lax.rem(s, 2)])

    barrier = pltpu.get_barrier_semaphore()

    def greet(d, carry):
        peer = lax.rem(me + d, nb)
        pl.semaphore_signal(barrier, inc=1, device_id=(peer, z), device_id_type=MESH)
        return carry

    lax.fori_loop(1, nb, greet, 0)

    def greet_z(d, carry):
        pl.semaphore_signal(barrier, inc=1, device_id=(me, lax.rem(z + d, nz)), device_id_type=MESH)
        return carry

    lax.fori_loop(1, nz, greet_z, 0)
    for one in loads:
        one.start()

    def load_x(s, carry):
        x_copy(s).start()
        return carry

    def load_ct(s, carry):
        ct_copy(s).start()
        return carry

    lax.fori_loop(0, S, load_x, 0)
    lax.fori_loop(0, S, load_ct, 0)
    ect_copy(0).start()
    cols[...] = jnp.zeros_like(cols)
    gk_ref[...] = jnp.zeros_like(gk_ref)
    wm[...] = jnp.zeros_like(wm)

    local = COLUMN_MODES // nz
    lane = lax.broadcasted_iota(jnp.int32, (1, 2 * M), 1)

    def place(d, carry):
        for i in range(slots):
            mode = owner_ref[(d * nz + z) * slots + i]
            at = lax.div(mode, COLUMN_MODES) * local + lax.rem(mode, local)
            lows[pl.ds(d * slots + i, 1), :] = jnp.where(lane == at, 1.0, 0.0)
            highs[pl.ds(d * slots + i, 1), :] = jnp.where(lane == at + M, 1.0, 0.0)
        return carry

    lax.fori_loop(0, nb, place, 0)
    inner = 1.0 / (H * nz * H * nz)
    weigh = jnp.where(z * local + lax.rem(lane, local) == 0, 0.5 * inner, inner)
    for table, pick in enumerate((lambda v: v[...], lambda v: v[...] * weigh)):
        perm_ref[table] = pick(lows)[:, 0:M].astype(BF16)
        back_ref[1 - table, 0] = pick(lows).astype(BF16)
        back_ref[1 - table, 1] = pick(highs).astype(BF16)

    weight = point_ref[...].astype(BF16)
    kernel_t = jnp.concatenate([dot(weight, sign_ref[k]) for k in range(4)], axis=0)
    kt1[...] = kernel_t[:, 0:128].astype(BF16)
    for turn in range(8):
        ktb[turn] = pltpu.roll(kernel_t[:, 128:256], (64 + 16 * turn) % 128, 1)
    padded = jnp.concatenate([kernel_t.astype(BF16), jnp.zeros((256 - K, 256), BF16)], axis=0)
    kernel_n = dot_nt(eye_ref[0:K], padded)
    kk1[...] = kernel_n[:, 0:128].astype(BF16)
    for turn in range(8):
        kkb[turn] = pltpu.roll(kernel_n[:, 128:256], (64 + 16 * turn) % 128, 1)
    for one in loads:
        one.wait()
    masters = master_ref[...].reshape(slots * channels, wide).astype(BF16)
    for part in range(4):
        block = dot(masters, psi[part]).astype(BF16)
        for i in range(slots):
            wm[i, part * channels : (part + 1) * channels, :] = block[i * channels : (i + 1) * channels]

    def rs_copy(s, up, c, pb, rb, ssem, rsem):
        way = 0 if up else 1
        return pltpu.make_async_remote_copy(
            src_ref=pb.at[s, c], dst_ref=rb.at[s, way, c],
            send_sem=ssem.at[s, way, c], recv_sem=rsem.at[s, way, c],
            device_id=(me, z + 1 if up else z - 1), device_id_type=MESH,
        )

    def rs_hop(j, s, bufs, finish=False):
        pb, rb = bufs[0], bufs[1]
        for up in (True, False):
            place = z if up else last - z
            c = (last - j + z) if up else (z - (last - j))

            @pl.when(place <= j)
            def _():
                copy = rs_copy(s, up, c, *bufs)
                if finish:
                    copy.wait_send()
                else:
                    @pl.when(place > 0)
                    def _():
                        way = 0 if up else 1
                        copy.wait_recv()
                        pb[s, c] = (pb[s, c].astype(F32) + rb[s, way, c].astype(F32)).astype(BF16)

                    copy.start()

    def rs_final(s, bufs):
        pb, rb = bufs[0], bufs[1]
        acc[...] = pb[s, z].astype(F32)

        @pl.when(z > 0)
        def _():
            rs_copy(s, True, z, *bufs).wait_recv()
            acc[...] += rb[s, 0, z].astype(F32)

        @pl.when(z < last)
        def _():
            rs_copy(s, False, z, *bufs).wait_recv()
            acc[...] += rb[s, 1, z].astype(F32)

        return acc[...].astype(BF16)

    def ag_copy(s, up, c, gb, ssem, rsem):
        way = 0 if up else 1
        return pltpu.make_async_remote_copy(
            src_ref=gb.at[s, c], dst_ref=gb.at[s, c],
            send_sem=ssem.at[s, way, c], recv_sem=rsem.at[s, c],
            device_id=(me, z + 1 if up else z - 1), device_id_type=MESH,
        )

    def ag_hop(j, s, bufs, finish=False):
        for up in (True, False):
            c = z - j if up else z + j
            more = z < last if up else z > 0

            @pl.when((c >= 0) if up else (c <= last))
            def _():
                copy = ag_copy(s, up, c, *bufs)
                if j > 0 and not finish:
                    copy.wait_recv()

                if j < last:
                    @pl.when(more)
                    def _():
                        if finish:
                            copy.wait_send()
                        else:
                            copy.start()

    tiled = slots % 8 == 0

    def block_of(ref, s, d):
        if tiled:
            return ref.at[s, :, pl.ds(pl.multiple_of(d * slots, slots), slots)]
        return ref.at[s, d]

    def blocks_of(ref, s):
        if tiled:
            return ref.at[s, :, pl.ds(0, (nb - 1) * slots)]
        return ref.at[s, pl.ds(0, nb - 1)]

    def whole_of(ref, s):
        if tiled:
            return jnp.concatenate([ref[s, g] for g in range(wide // 128)], axis=1)
        return ref[s].reshape(nb * slots, wide)

    def put_whole(ref, s, value):
        if tiled:
            for g in range(wide // 128):
                ref[s, g] = value[:, g * 128 : (g + 1) * 128]
        else:
            ref[s] = value.reshape(nb, slots, wide)

    def slot_rows(ref, s, i):
        if tiled:
            return jnp.concatenate([ref[s, g, pl.ds(i, nb, stride=slots), :] for g in range(wide // 128)], axis=1)
        return ref[s, :, i, :]

    def put_slot_rows(ref, s, i, value):
        if tiled:
            for g in range(wide // 128):
                ref[s, g, pl.ds(i, nb, stride=slots), :] = value[:, g * 128 : (g + 1) * 128]
        else:
            ref[s, :, i, :] = value

    def exchange(s, src, dst, which):
        def send(d, carry):
            peer = lax.rem(me + d, nb)
            pltpu.make_async_remote_copy(
                src_ref=block_of(src, s, peer), dst_ref=block_of(dst, s, me),
                send_sem=a2a_s.at[which, s], recv_sem=a2a_r.at[which, s],
                device_id=(peer, z), device_id_type=MESH,
            ).start()
            return carry

        lax.fori_loop(1, nb, send, 0)
        block_of(dst, s, me)[...] = block_of(src, s, me)[...]

    def exchanged(s, src, dst, which):
        return pltpu.make_async_remote_copy(
            src_ref=blocks_of(src, s), dst_ref=blocks_of(dst, s),
            send_sem=a2a_s.at[which, s], recv_sem=a2a_r.at[which, s],
            device_id=(lax.rem(me + 1, nb), z), device_id_type=MESH,
        )

    def forward_rows(s, pb):
        for c in range(nz):
            part = dot(single[...], cols[c])
            first = part[0:M]
            second = pltpu.roll(part[M:], 64, 1)
            pb[s, c, :, 0:128] = first[:, 0:128].astype(BF16)
            pb[s, c, :, 128:256] = (first[:, 128:256] + second[:, 0:128]).astype(BF16)
            pb[s, c, :, 256:384] = second[:, 128:256].astype(BF16)

    def put_columns(p, value):
        step = 4 * COLUMN_MODES // nz
        for c in range(nz):
            cols[c, pl.ds(pl.multiple_of(p * step, step), step), 0:K] = value[c * step : (c + 1) * step]

    def pair_of(ref, s, p):
        return jnp.concatenate([ref[s, 2 * p], ref[s, 2 * p + 1]], axis=1)

    def stage_a(s):
        x_copy(s).wait()

        def some(blk, carry):
            for u in range(8):
                p = blk * 8 + u
                part = dot_nt(cblk_ref[...], pair_of(xb, s, p))
                put_columns(p, part.astype(BF16))
            return carry

        lax.fori_loop(0, pairs // 8, some, 0)
        forward_rows(s, pb1)
        rs_hop(0, s, rs1)

    def by_column(ref, s, i):
        rows = slot_rows(ref, s, i)
        low, mid, top = rows[:, 0:128], rows[:, 128:256], rows[:, 256:384]
        first = jnp.concatenate([low, mid], axis=1)
        second = jnp.concatenate([top, pltpu.roll(mid, 64, 1)], axis=1)
        return jnp.concatenate([first, second], axis=0).astype(BF16)

    def put_by_column(ref, s, i, value):
        first, second = value[0:nb], value[nb:]
        mid = first[:, 128:256] + pltpu.roll(second[:, 128:256], 64, 1)
        put_slot_rows(ref, s, i, jnp.concatenate([first[:, 0:128], mid, second[:, 0:128]], axis=1))

    def stage_b(s):
        exchanged(s, xs, xr, 0).wait_recv()
        for i in range(slots):
            put_by_column(ps, s, i, dot_nt(by_column(xr, s, i), wm[i]))
        exchange(s, ps, pr, 1)

    def stage_d(s):
        exchanged(s, gs, gr, 2).wait_recv()
        for i in range(slots):
            put_by_column(hs, s, i, dot(by_column(gr, s, i), wm[i]))
        exchange(s, hs, hr, 3)

    def stage_f(s, bufs, table, src, dst, which):
        placed = dot(perm_ref[table], rs_final(s, bufs)).astype(BF16)
        put_whole(src, s, dot(placed, turn_ref[...]))
        exchange(s, src, dst, which)

    def stage_u(s, bufs, table, src, dst, which):
        exchanged(s, src, dst, which).wait_recv()
        turned = jnp.transpose(whole_of(dst, s))
        cut = K // 128 * 128
        first = turned[0:K]
        second = jnp.concatenate([turned[2 * K - cut :], turned[K : 2 * K - cut]], axis=0)
        parts = []
        for q in range(2):
            base = 2 * q * channels
            at = lambda col, row: col[base + row * channels : base + (row + 1) * channels]
            m00, m10, m01, m11 = at(first, 0), at(first, 1), at(second, 0), at(second, 1)
            parts.append(jnp.concatenate([m00 + m11, m00 - m11, m01 + m10, m01 - m10], axis=0).astype(BF16))
        both = dot(parts[0], back_ref[table, 0]) + dot(parts[1], back_ref[table, 1])
        bufs[0][s, z] = both.astype(BF16)
        ag_hop(0, s, bufs)

    def inverse_rows(s, gb, base):
        spread = dot(gb[s].reshape(nz * K, 2 * M), single[...])
        group = lax.broadcasted_iota(jnp.int32, (K, 128), 1) // 16
        for col in range(pairs // 8):
            cut = slice(col * 128, col * 128 + 128)
            parts = [spread[c * K : (c + 1) * K, cut] for c in range(nz)]
            parts = [parts[0]] + [pltpu.roll(parts[c], 16 * c, 1) for c in range(1, nz)]
            for first in range(4):
                which = (group + (8 - first)) % 4
                mixed = jnp.where(which == 0, parts[0], jnp.where(which == 1, parts[1], jnp.where(which == 2, parts[2], parts[3])))
                for turn in (first, first + 4):
                    inside = (group + (8 - turn)) % 8 < 4
                    l2[col * 8 + turn] = jnp.where(inside, mixed, base[turn]).astype(BF16)

    def with_columns(x2, turn):
        rows = [x2[0:128]]
        for g in range(8):
            i = (g - turn) % 8
            rows.append(cblk_ref[16 * i : 16 * i + 16, :] if i < 4 else x2[64 + 16 * i : 80 + 16 * i])
        return jnp.concatenate(rows, axis=0)

    def stage_c(s):
        ag_hop(last, s, ag1)
        inverse_rows(s, gb1, ktb)
        ct_copy(s).wait()
        f = table_ref[scale_ref[s]]

        def some(blk, carry):
            for u in range(8):
                p = blk * 8 + u
                x2 = pair_of(xb, s, p)
                both = with_columns(x2, u)
                half = (0.5 * f) * dot(jnp.concatenate([kt1[...], l2[p]], axis=1), both)
                square = half * half
                rise = 1.0 + jnp.tanh(half * (2.0 * GELU_A + 8.0 * GELU_B * square))
                y = (x2.astype(F32) + half * rise).astype(BF16)
                slope = rise + (rise * (2.0 - rise)) * (half * (2.0 * GELU_A + 24.0 * GELU_B * square))
                c2 = pair_of(ob, s, p).astype(F32)
                g2 = (((0.5 * f) * c2) * slope).astype(BF16)
                for e in range(2):
                    ob[s, 2 * p + e] = y[:, e * W : (e + 1) * W]
                    xb[s, 2 * p + e] = g2[:, e * W : (e + 1) * W]
                back = dot_nt(both, g2)
                gk_ref[0:128] += back[0:128]
                for g in range(8):
                    i = (g - u) % 8
                    piece = back[128 + 16 * g : 144 + 16 * g]
                    if i < 4:
                        cols[i, pl.ds(pl.multiple_of(p * 16, 16), 16), 0:K] = piece.astype(BF16)
                    else:
                        gk_ref[64 + 16 * i : 80 + 16 * i] += piece
            return carry

        lax.fori_loop(0, pairs // 8, some, 0)
        forward_rows(s, pb2)
        rs_hop(0, s, rs2)

    def stage_e(s):
        slot = lax.rem(s, 2)

        @pl.when(s + 1 < S)
        def _():
            ect_copy(s + 1).start()

        ag_hop(last, s, ag2)
        inverse_rows(s, gb2, kkb)
        ect_copy(s).wait()

        def some(blk, carry):
            for u in range(8):
                p = blk * 8 + u
                both = with_columns(pair_of(xb, s, p), u)
                y = dot(jnp.concatenate([kk1[...], l2[p]], axis=1), both)
                y = (y + pair_of(eb, slot, p).astype(F32)).astype(BF16)
                for e in range(2):
                    xb[s, 2 * p + e] = y[:, e * W : (e + 1) * W]
            return carry

        lax.fori_loop(0, pairs // 8, some, 0)

    def pa_copy(peer):
        return pltpu.make_async_remote_copy(
            src_ref=pa.at[me], dst_ref=pa.at[me], send_sem=pa_s.at[0], recv_sem=pa_r.at[0],
            device_id=(peer, z), device_id_type=MESH,
        )

    def pz_copy(peer):
        return pltpu.make_async_remote_copy(
            src_ref=pz.at[z], dst_ref=pz.at[z], send_sem=pz_s.at[0], recv_sem=pz_r.at[0],
            device_id=(me, peer), device_id_type=MESH,
        )

    def all_but_one(ref, count, ssem, rsem, device):
        rest = ref.at[pl.ds(0, count - 1)]
        return pltpu.make_async_remote_copy(
            src_ref=rest, dst_ref=rest, send_sem=ssem.at[0], recv_sem=rsem.at[0],
            device_id=device, device_id_type=MESH,
        )

    def point_first():
        left = gk_ref[...]
        total = jnp.zeros((channels, K), F32)
        for part in range(3):
            term = left.astype(BF16)
            left = left - term.astype(F32)
            turned = dot_nt(eye_ref[0:K, 0:K], term).astype(BF16)
            for k in range(4):
                total += dot_nt(turned[k * channels : (k + 1) * channels], sign_ref[k, :, 0:K])
        pa[me] = total

        def send(d, carry):
            pa_copy(lax.rem(me + d, nb)).start()
            return carry

        lax.fori_loop(1, nb, send, 0)

    def point_second():
        all_but_one(pa, nb, pa_s, pa_r, (lax.rem(me + 1, nb), z)).wait_recv()
        pz[z] = jnp.sum(pa[...], axis=0)

        def send(d, carry):
            pz_copy(lax.rem(z + d, nz)).start()
            return carry

        lax.fori_loop(1, nz, send, 0)

    def slot_gradients():
        for i in range(slots):
            g_all = jnp.concatenate([by_column(gr, s, i) for s in range(S)], axis=0)
            x_all = jnp.concatenate([by_column(xr, s, i) for s in range(S)], axis=0)
            g_turned = dot_nt(eye_ref[...], g_all).astype(BF16)
            wm[i] = dot(g_turned, x_all).astype(BF16)

        total = jnp.zeros((slots * channels, wide), F32)
        for part in range(4):
            rows = slice(part * channels, (part + 1) * channels)
            block = jnp.concatenate([wm[i, rows, :] for i in range(slots)], axis=0)
            total += dot_nt(block, psi[part])
        dw_ref[...] = total.reshape(slots, channels, wide)

    def orthogonal(moments):
        def split(v):
            high = v.astype(BF16)
            return high, (v - high.astype(F32)).astype(BF16)

        def product(a, b, mul):
            (ah, al), (bh, bl) = a, b
            return mul(ah, bh) + (mul(ah, bl) + mul(al, bh))

        current = [m / (jnp.sqrt(jnp.sum(m * m)) + 1e-07) for m in moments]
        for repeat in range(5):
            parts = [split(v) for v in current]
            grams = [product(v, v, dot_nt) for v in parts]
            gram_parts = [split(v) for v in grams]
            squares = [product(v, v, dot) for v in gram_parts]
            polynomials = [split(QUINTIC_SECOND * g + QUINTIC_THIRD * q) for g, q in zip(grams, squares)]
            current = [
                QUINTIC_FIRST * v + product(p, w, dot) for v, p, w in zip(current, polynomials, parts)
            ]
        return current

    def slot_updates(chosen):
        moments = [MOMENTUM_DECAY * momentum_ref[i] + dw_ref[i] for i in chosen]
        for i, value in zip(chosen, orthogonal(moments)):
            turned_ref[i] = value

    def point_update():
        all_but_one(pz, nz, pz_s, pz_r, (me, lax.rem(z + 1, nz))).wait_recv()
        total = jnp.sum(pz[...], axis=0)
        pg_ref[...] = total
        (point_turned_ref[...],) = orthogonal([MOMENTUM_DECAY * point_momentum_ref[...] + total])

    rs1 = (pb1, rb1, rs1_s, rs1_r)
    rs2 = (pb2, rb2, rs2_s, rs2_r)
    ag1 = (gb1, ag1_s, ag1_r)
    ag2 = (gb2, ag2_s, ag2_r)

    schedule = [
        (0, stage_a),
        (3, lambda s: stage_f(s, rs1, 0, xs, xr, 0)),
        (11, lambda s: stage_f(s, rs2, 1, gs, gr, 2)),
        (2, lambda s: rs_hop(2, s, rs1)),
        (10, lambda s: rs_hop(2, s, rs2)),
        (1, lambda s: rs_hop(1, s, rs1)),
        (9, lambda s: rs_hop(1, s, rs2)),
        (7, lambda s: ag_hop(2, s, ag1)),
        (15, lambda s: ag_hop(2, s, ag2)),
        (6, lambda s: ag_hop(1, s, ag1)),
        (14, lambda s: ag_hop(1, s, ag2)),
        (5, lambda s: stage_u(s, ag1, 0, ps, pr, 1)),
        (13, lambda s: stage_u(s, ag2, 1, hs, hr, 3)),
        (4, stage_b),
        (12, stage_d),
        (8, stage_c),
        (16, stage_e),
    ]
    steps = S + max(lag for lag, _ in schedule)
    at_step = {S + 8: point_first, S + 9: point_second, S + 11: point_update, S + 12: slot_gradients}
    groups = [range(slots)[: slots // 2], range(slots)[slots // 2 :]]
    for step, group in enumerate(groups):
        if group:
            at_step[S + 13 + step] = functools.partial(slot_updates, group)

    pl.semaphore_wait(barrier, nb + nz - 2)

    def iteration(t, carry):
        for lag, stage in schedule:
            s = t - lag
            pl.when((s >= 0) & (s < S))(functools.partial(stage, s))
        for step, work in at_step.items():
            pl.when(t == step)(work)
        return carry

    lax.fori_loop(0, steps, iteration, 0)

    def finish(s, carry):
        for j in range(last):
            rs_hop(j, s, rs1, True)
            rs_hop(j, s, rs2, True)
            ag_hop(j, s, ag1, True)
            ag_hop(j, s, ag2, True)
        for which, (src, dst) in enumerate(((xs, xr), (ps, pr), (gs, gr), (hs, hr))):
            exchanged(s, src, dst, which).wait_send()
        return carry

    lax.fori_loop(0, S, finish, 0)
    all_but_one(pa, nb, pa_s, pa_r, (lax.rem(me + 1, nb), z)).wait_send()
    all_but_one(pz, nz, pz_s, pz_r, (me, lax.rem(z + 1, nz))).wait_send()


def store_kernel(
    ob, xb, dw_ref, pg_ref, turned_ref, point_turned_ref, master_ref, momentum_ref, point_ref, point_momentum_ref,
    out_hbm, ig_hbm, grad_ref, moment_ref, weight_ref, low_ref,
    point_grad_ref, point_moment_ref, point_weight_ref, point_low_ref, sem,
):
    S = ob.shape[0]
    copies = []
    for s in range(S):
        copies.append(pltpu.make_async_copy(ob.at[s], out_hbm.at[s], sem.at[0, s]))
        copies.append(pltpu.make_async_copy(xb.at[s], ig_hbm.at[s], sem.at[1, s]))
    for copy in copies:
        copy.start()
    point_grad_ref[...] = pg_ref[...]
    point_moment_ref[...] = MOMENTUM_DECAY * point_momentum_ref[...] + pg_ref[...]
    point_weight = point_ref[...] - POINTWISE_RATE * point_turned_ref[...]
    point_weight_ref[...] = point_weight
    point_low_ref[...] = point_weight.astype(BF16)
    grad_ref[...] = dw_ref[...]
    moment_ref[...] = MOMENTUM_DECAY * momentum_ref[...] + dw_ref[...]
    weight = master_ref[...] - SPECTRAL_RATE * turned_ref[...]
    weight_ref[...] = weight
    low_ref[...] = weight.astype(BF16)
    for copy in copies:
        copy.wait()


def per_device(
    input_field,
    cotangent,
    sample_scale,
    scale_table,
    owner_map,
    spectral_master,
    spectral_momentum,
    pointwise_master,
    pointwise_momentum,
):
    S, H, K, W = input_field.shape
    nz = lax.axis_size("row")
    nb = lax.axis_size("batch")
    slots = spectral_master.shape[0]
    channels = K // 4
    wide = 2 * K
    local_columns = COLUMN_MODES // nz
    M = ROW_MODES * local_columns
    grid = H * nz

    anywhere = pl.BlockSpec(memory_space=pltpu.HBM)
    smem = pl.BlockSpec(memory_space=pltpu.SMEM)
    vmem = pl.BlockSpec(memory_space=pltpu.VMEM)
    exchange_shape = (S, wide // 128, nb * slots, 128) if slots % 8 == 0 else (S, nb, slots, wide)
    dma = pltpu.SemaphoreType.DMA
    single = jnp.asarray(row_blocks(grid, nz))
    psi, turn, signs = (jnp.asarray(one) for one in product_signs(channels))
    column_rows = jnp.asarray(column_block(W, nz))
    unit = jnp.asarray(np.eye(256).astype(ml_dtypes.bfloat16))
    slot_shape, point_shape = spectral_master.shape, pointwise_master.shape
    kept = pl.pallas_call(
        functools.partial(layer_kernel, (nb, nz, S, H, K, W, slots, M)),
        out_shape=(
            pltpu.VMEM(input_field.shape, BF16),
            pltpu.VMEM(input_field.shape, BF16),
            pltpu.VMEM(slot_shape, F32),
            pltpu.VMEM(point_shape, F32),
            pltpu.VMEM(slot_shape, F32),
            pltpu.VMEM(point_shape, F32),
        ),
        in_specs=[anywhere, anywhere, smem, smem, smem] + [anywhere] * 4 + [vmem] * 6,
        out_specs=(vmem,) * 6,
        scratch_shapes=[
            pltpu.VMEM((2, H, K, W), BF16),
            pltpu.VMEM(single.shape[1:], BF16),
            pltpu.VMEM(psi.shape, BF16),
            pltpu.VMEM(spectral_master.shape, F32),
            pltpu.VMEM(spectral_master.shape, F32),
            pltpu.VMEM((slots, 256, 256), BF16),
            pltpu.VMEM((nz, single.shape[2], 256), BF16),
            pltpu.VMEM((H // 2, K, 128), BF16),
            pltpu.VMEM((K, 128), BF16),
            pltpu.VMEM((8, K, 128), F32),
            pltpu.VMEM((K, 128), BF16),
            pltpu.VMEM((8, K, 128), F32),
            pltpu.VMEM((M, wide), F32),
            pltpu.VMEM((K, K), F32),
            pltpu.VMEM((nb, channels, K), F32),
            pltpu.VMEM((nz, channels, K), F32),
            pltpu.VMEM((M, 2 * M), F32),
            pltpu.VMEM((M, 2 * M), F32),
            pltpu.VMEM((2, M, M), BF16),
            pltpu.VMEM((2, 2, M, 2 * M), BF16),
            pltpu.VMEM((S, nz, M, wide), BF16),
            pltpu.VMEM((S, 2, nz, M, wide), BF16),
            pltpu.VMEM((S, nz, K, 2 * M), BF16),
            pltpu.VMEM((S, nz, M, wide), BF16),
            pltpu.VMEM((S, 2, nz, M, wide), BF16),
            pltpu.VMEM((S, nz, K, 2 * M), BF16),
        ]
        + [pltpu.VMEM(exchange_shape, F32)] * 8
        + [dma((S,)), dma((S,)), dma((4,)), dma((2,))]
        + [dma((1,))] * 4
        + [dma((S, 2, nz))] * 4
        + [dma((S, 2, nz)), dma((S, nz))] * 2
        + [dma((4, S))] * 2,
        compiler_params=pltpu.CompilerParams(
            collective_id=0, has_side_effects=True, vmem_limit_bytes=37 * 1024 * 1024
        ),
    )(
        input_field, cotangent, sample_scale, scale_table, owner_map, single, psi,
        spectral_master, spectral_momentum, turn, signs, column_rows, unit, pointwise_master, pointwise_momentum,
    )

    held = [pltpu.with_memory_space_constraint(one, pltpu.VMEM) for one in kept]
    input_shape = jax.ShapeDtypeStruct(input_field.shape, BF16)
    results = pl.pallas_call(
        store_kernel,
        out_shape=(
            input_shape,
            input_shape,
            jax.ShapeDtypeStruct(slot_shape, F32),
            jax.ShapeDtypeStruct(slot_shape, F32),
            jax.ShapeDtypeStruct(slot_shape, F32),
            jax.ShapeDtypeStruct(slot_shape, BF16),
            jax.ShapeDtypeStruct(point_shape, F32),
            jax.ShapeDtypeStruct(point_shape, F32),
            jax.ShapeDtypeStruct(point_shape, F32),
            jax.ShapeDtypeStruct(point_shape, BF16),
        ),
        in_specs=[vmem] * 10,
        out_specs=(anywhere, anywhere) + (vmem,) * 8,
        scratch_shapes=[dma((2, S))],
        compiler_params=pltpu.CompilerParams(vmem_limit_bytes=6 * 1024 * 1024),
    )(*held, spectral_master, spectral_momentum, pointwise_master, pointwise_momentum)
    return tuple(results)


def solution(mesh):
    return jax.shard_map(
        per_device,
        mesh=mesh,
        in_specs=(
            P("batch", "row", None, None),
            P("batch", "row", None, None),
            P("batch"),
            P(),
            P(),
            P(("batch", "row"), None, None),
            P(("batch", "row"), None, None),
            P(),
            P(),
        ),
        out_specs=(
            P("batch", "row", None, None),
            P("batch", "row", None, None),
            P(("batch", "row"), None, None),
            P(("batch", "row"), None, None),
            P(("batch", "row"), None, None),
            P(("batch", "row"), None, None),
            P(),
            P(),
            P(),
            P(),
        ),
        check_vma=False,
    )
```

```python
import functools
import math

import jax
import jax.numpy as jnp
import ml_dtypes
import numpy as np
from jax import lax
from jax.experimental import pallas as pl
from jax.experimental.pallas import tpu as pltpu
from jax.sharding import PartitionSpec as P

ROW_MODES = 16
COLUMN_MODES = 16

BLADE_SIGNS = np.array([[1, 1, 1, 1], [1, 1, 1, 1], [1, -1, 1, -1], [1, -1, 1, -1]], np.float32)
QUINTIC_FIRST = 3.4445
QUINTIC_SECOND = -4.775
QUINTIC_THIRD = 2.0315
SPECTRAL_RATE = 4.0
POINTWISE_RATE = 0.8
MOMENTUM_DECAY = 0.5
MESH = pl.DeviceIdType.MESH
F32 = jnp.float32
BF16 = jnp.bfloat16
GELU_A = math.sqrt(2.0 / math.pi)
GELU_B = GELU_A * 0.044715


MATRIX_SIGNS = np.zeros((2, 2, 4), np.float32)
MATRIX_SIGNS[0, 0, 0] = MATRIX_SIGNS[0, 0, 1] = MATRIX_SIGNS[1, 1, 0] = 1.0
MATRIX_SIGNS[1, 1, 1] = MATRIX_SIGNS[1, 0, 3] = -1.0
MATRIX_SIGNS[0, 1, 2] = MATRIX_SIGNS[0, 1, 3] = MATRIX_SIGNS[1, 0, 2] = 1.0


def column_block(grid_size, row_count):
    angles = 2.0 * np.pi / grid_size * (np.arange(COLUMN_MODES)[:, None] * np.arange(grid_size)[None] % grid_size)
    table = np.stack([np.cos(angles), -np.sin(angles)], 0).reshape(2, row_count, -1, grid_size)
    full = np.einsum("pclw,hg->chplgw", table, np.eye(2))
    return full.reshape(4 * COLUMN_MODES, 2 * grid_size).astype(ml_dtypes.bfloat16)


def row_blocks(grid_size, row_count):
    rows = grid_size // row_count
    local = COLUMN_MODES // row_count
    r = np.arange(ROW_MODES)
    frequency = np.where(r < ROW_MODES // 2, r, grid_size - ROW_MODES + r)
    angles = 2.0 * np.pi / grid_size * (frequency[:, None] * np.arange(grid_size)[None] % grid_size)
    cosine, sine = np.cos(angles), np.sin(angles)
    table = np.stack([np.stack([cosine, sine], -1), np.stack([-sine, cosine], -1)], 0)
    table = table.reshape(2, ROW_MODES, row_count, rows, 2)
    full = np.einsum("qrzhp,cd->zqrchpd", table, np.eye(local))
    return full.reshape(row_count, 2 * ROW_MODES * local, rows * 2 * local).astype(ml_dtypes.bfloat16)


def lanes_of_columns(channels):
    half = 4 * channels
    place = np.arange(2 * half)
    cut = half // 128 * 128
    first = np.arange(half)
    second = np.where(first < cut, half + (half - cut) + first, half + first - cut)
    return place[first], place[second]


def product_signs(channels):
    unit = np.eye(channels, dtype=np.float32)
    psi = np.zeros((2, 2, 2, 4, 2, 2), np.float32)
    for q in range(2):
        for p in range(2):
            part = -1.0 if (q == 0 and p == 1) else 1.0
            for row in range(2):
                for inner in range(2):
                    psi[q, row, p ^ q, :, p, inner] = part * MATRIX_SIGNS[row, inner]
    psi = np.einsum("qrwapn,ij->qrwaipnj", psi, unit).reshape(4, 8 * channels, 4 * channels)
    psi = np.pad(psi, ((0, 0), (0, 0), (0, 256 - 4 * channels)))
    spread = np.einsum("pt,ncb,ij->pbictnj", np.eye(2), MATRIX_SIGNS, unit)
    spread = spread.reshape(8 * channels, 2, 4 * channels)
    turn = np.zeros((8 * channels, 8 * channels), np.float32)
    for col, lanes in enumerate(lanes_of_columns(channels)):
        turn[:, lanes] = spread[:, col]
    point = np.zeros((4, 4, 4), np.float32)
    for k in range(4):
        for b in range(4):
            point[k, k ^ b, b] = BLADE_SIGNS[k ^ b, b]
    point = np.einsum("kab,ij->kaibj", point, unit).reshape(4, 4 * channels, 4 * channels)
    point = np.pad(point, ((0, 0), (0, 0), (0, 256 - 4 * channels)))
    return (one.astype(ml_dtypes.bfloat16) for one in (psi, turn, point))


def dot(a, b):
    return lax.dot_general(a, b, (((1,), (0,)), ((), ())), preferred_element_type=F32)


def dot_nt(a, b):
    return lax.dot_general(a, b, (((1,), (1,)), ((), ())), preferred_element_type=F32)


def layer_kernel(
    sizes,
    x_hbm, ct_hbm, scale_ref, table_ref, owner_ref, single_hbm, psi_hbm, master_hbm, momentum_hbm,
    turn_ref, sign_ref, cblk_ref, eye_ref, point_ref, point_momentum_ref,
    ob, xb, dw_ref, pg_ref, turned_ref, point_turned_ref,
    eb, single, psi, master_ref, momentum_ref, wm, cols, l2, kt1, ktb, kk1, kkb, acc, gk_ref, pa, pz,
    lows, highs, perm_ref, back_ref,
    pb, rb, gb, given, taken, made, back,
    x_sem, ct_sem, ld_sem, ei_sem, pa_s, pa_r, pz_s, pz_r,
    rs_s, rs_r, ag_s, ag_r, a2a_s, a2a_r,
):
    nb, nz, S, H, K, W, slots, M = sizes
    wide = 2 * K
    channels = K // 4
    pairs = H // 2
    me = lax.axis_index("batch")
    z = lax.axis_index("row")
    last = nz - 1

    loads = [
        pltpu.make_async_copy(psi_hbm, psi, ld_sem.at[0]),
        pltpu.make_async_copy(single_hbm.at[z], single, ld_sem.at[1]),
        pltpu.make_async_copy(master_hbm, master_ref, ld_sem.at[2]),
        pltpu.make_async_copy(momentum_hbm, momentum_ref, ld_sem.at[3]),
    ]
    x_copy = lambda s: pltpu.make_async_copy(x_hbm.at[s], xb.at[s], x_sem.at[s])
    ct_copy = lambda s: pltpu.make_async_copy(ct_hbm.at[s], ob.at[s], ct_sem.at[s])
    ect_copy = lambda s: pltpu.make_async_copy(ct_hbm.at[s], eb.at[lax.rem(s, 2)], ei_sem.at[lax.rem(s, 2)])

    barrier = pltpu.get_barrier_semaphore()

    def greet(d, carry):
        peer = lax.rem(me + d, nb)
        pl.semaphore_signal(barrier, inc=1, device_id=(peer, z), device_id_type=MESH)
        return carry

    lax.fori_loop(1, nb, greet, 0)

    def greet_z(d, carry):
        pl.semaphore_signal(barrier, inc=1, device_id=(me, lax.rem(z + d, nz)), device_id_type=MESH)
        return carry

    lax.fori_loop(1, nz, greet_z, 0)
    for one in loads:
        one.start()

    def load_x(s, carry):
        x_copy(s).start()
        return carry

    def load_ct(s, carry):
        ct_copy(s).start()
        return carry

    lax.fori_loop(0, S, load_x, 0)
    lax.fori_loop(0, S, load_ct, 0)
    ect_copy(0).start()
    cols[...] = jnp.zeros_like(cols)
    gk_ref[...] = jnp.zeros_like(gk_ref)
    wm[...] = jnp.zeros_like(wm)

    local = COLUMN_MODES // nz
    lane = lax.broadcasted_iota(jnp.int32, (1, 2 * M), 1)

    def place(d, carry):
        for i in range(slots):
            mode = owner_ref[(d * nz + z) * slots + i]
            at = lax.div(mode, COLUMN_MODES) * local + lax.rem(mode, local)
            lows[pl.ds(d * slots + i, 1), :] = jnp.where(lane == at, 1.0, 0.0)
            highs[pl.ds(d * slots + i, 1), :] = jnp.where(lane == at + M, 1.0, 0.0)
        return carry

    lax.fori_loop(0, nb, place, 0)
    inner = 1.0 / (H * nz * H * nz)
    weigh = jnp.where(z * local + lax.rem(lane, local) == 0, 0.5 * inner, inner)
    for table, pick in enumerate((lambda v: v[...], lambda v: v[...] * weigh)):
        perm_ref[table] = pick(lows)[:, 0:M].astype(BF16)
        back_ref[1 - table, 0] = pick(lows).astype(BF16)
        back_ref[1 - table, 1] = pick(highs).astype(BF16)

    weight = point_ref[...].astype(BF16)
    kernel_t = jnp.concatenate([dot(weight, sign_ref[k]) for k in range(4)], axis=0)
    kt1[...] = kernel_t[:, 0:128].astype(BF16)
    for turn in range(8):
        ktb[turn] = pltpu.roll(kernel_t[:, 128:256], (64 + 16 * turn) % 128, 1)
    padded = jnp.concatenate([kernel_t.astype(BF16), jnp.zeros((256 - K, 256), BF16)], axis=0)
    kernel_n = dot_nt(eye_ref[0:K], padded)
    kk1[...] = kernel_n[:, 0:128].astype(BF16)
    for turn in range(8):
        kkb[turn] = pltpu.roll(kernel_n[:, 128:256], (64 + 16 * turn) % 128, 1)
    for one in loads:
        one.wait()
    masters = master_ref[...].reshape(slots * channels, wide).astype(BF16)
    for part in range(4):
        block = dot(masters, psi[part]).astype(BF16)
        for i in range(slots):
            wm[1, i, part * channels : (part + 1) * channels, :] = block[i * channels : (i + 1) * channels]
    for i in range(slots):
        wm[0, i] = dot_nt(eye_ref[...], wm[1, i]).astype(BF16)

    def rs_copy(n, up, c):
        way = 0 if up else 1
        return pltpu.make_async_remote_copy(
            src_ref=pb.at[n, c], dst_ref=rb.at[n, way, c],
            send_sem=rs_s.at[n, way, c], recv_sem=rs_r.at[n, way, c],
            device_id=(me, z + 1 if up else z - 1), device_id_type=MESH,
        )

    def rs_hop(j, n, finish=False):
        for up in (True, False):
            place = z if up else last - z
            c = (last - j + z) if up else (z - (last - j))

            @pl.when(place <= j)
            def _():
                copy = rs_copy(n, up, c)
                if finish:
                    copy.wait_send()
                else:
                    if j > 0:
                        @pl.when(place > 0)
                        def _():
                            way = 0 if up else 1
                            copy.wait_recv()
                            pb[n, c] = (pb[n, c].astype(F32) + rb[n, way, c].astype(F32)).astype(BF16)

                    copy.start()

    def rs_final(n):
        acc[...] = pb[n, z].astype(F32)

        @pl.when(z > 0)
        def _():
            rs_copy(n, True, z).wait_recv()
            acc[...] += rb[n, 0, z].astype(F32)

        @pl.when(z < last)
        def _():
            rs_copy(n, False, z).wait_recv()
            acc[...] += rb[n, 1, z].astype(F32)

    def ag_copy(n, up, c):
        way = 0 if up else 1
        return pltpu.make_async_remote_copy(
            src_ref=gb.at[n, c], dst_ref=gb.at[n, c],
            send_sem=ag_s.at[n, way, c], recv_sem=ag_r.at[n, c],
            device_id=(me, z + 1 if up else z - 1), device_id_type=MESH,
        )

    def ag_hop(j, n, finish=False):
        for up in (True, False):
            c = z - j if up else z + j
            more = z < last if up else z > 0

            @pl.when((c >= 0) if up else (c <= last))
            def _():
                copy = ag_copy(n, up, c)
                if j > 0 and not finish:
                    copy.wait_recv()

                if j < last:
                    @pl.when(more)
                    def _():
                        if finish:
                            copy.wait_send()
                        else:
                            copy.start()

    tiled = slots % 8 == 0

    def block_of(ref, s, d):
        if tiled:
            return ref.at[s, :, pl.ds(pl.multiple_of(d * slots, slots), slots)]
        return ref.at[s, d]

    def blocks_of(ref, s):
        if tiled:
            return ref.at[s, :, pl.ds(0, (nb - 1) * slots)]
        return ref.at[s, pl.ds(0, nb - 1)]

    def whole_of(ref, s):
        if tiled:
            return jnp.concatenate([ref[s, g] for g in range(wide // 128)], axis=1)
        return ref[s].reshape(nb * slots, wide)

    def put_whole(ref, s, value):
        if tiled:
            for g in range(wide // 128):
                ref[s, g] = value[:, g * 128 : (g + 1) * 128]
        else:
            ref[s] = value.reshape(nb, slots, wide)

    def slot_rows(ref, s, i):
        if tiled:
            return jnp.concatenate([ref[s, g, pl.ds(i, nb, stride=slots), :] for g in range(wide // 128)], axis=1)
        return ref[s, :, i, :]

    def put_slot_rows(ref, s, i, value):
        if tiled:
            for g in range(wide // 128):
                ref[s, g, pl.ds(i, nb, stride=slots), :] = value[:, g * 128 : (g + 1) * 128]
        else:
            ref[s, :, i, :] = value

    def exchange(s, src, dst, which):
        def send(d, carry):
            peer = lax.rem(me + d, nb)
            pltpu.make_async_remote_copy(
                src_ref=block_of(src, s, peer), dst_ref=block_of(dst, s, me),
                send_sem=a2a_s.at[which, s], recv_sem=a2a_r.at[which, s],
                device_id=(peer, z), device_id_type=MESH,
            ).start()
            return carry

        lax.fori_loop(1, nb, send, 0)
        block_of(dst, s, me)[...] = block_of(src, s, me)[...]

    def exchanged(s, src, dst, which):
        return pltpu.make_async_remote_copy(
            src_ref=blocks_of(src, s), dst_ref=blocks_of(dst, s),
            send_sem=a2a_s.at[which, s], recv_sem=a2a_r.at[which, s],
            device_id=(lax.rem(me + 1, nb), z), device_id_type=MESH,
        )

    def forward_rows(n):
        for c in range(nz):
            part = dot(single[...], cols[c])
            first = part[0:M]
            second = pltpu.roll(part[M:], 64, 1)
            pb[n, c, :, 0:128] = first[:, 0:128].astype(BF16)
            pb[n, c, :, 128:256] = (first[:, 128:256] + second[:, 0:128]).astype(BF16)
            pb[n, c, :, 256:384] = second[:, 128:256].astype(BF16)

    def put_columns(p, value):
        step = 4 * COLUMN_MODES // nz
        for c in range(nz):
            cols[c, pl.ds(pl.multiple_of(p * step, step), step), 0:K] = value[c * step : (c + 1) * step]

    def pair_of(ref, s, p):
        return jnp.concatenate([ref[s, 2 * p], ref[s, 2 * p + 1]], axis=1)

    def by_column(ref, s, i):
        rows = slot_rows(ref, s, i)
        low, mid, top = rows[:, 0:128], rows[:, 128:256], rows[:, 256:384]
        first = jnp.concatenate([low, mid], axis=1)
        second = jnp.concatenate([top, pltpu.roll(mid, 64, 1)], axis=1)
        return jnp.concatenate([first, second], axis=0).astype(BF16)

    def put_by_column(ref, s, i, value):
        first, second = value[0:nb], value[nb:]
        mid = first[:, 128:256] + pltpu.roll(second[:, 128:256], 64, 1)
        put_slot_rows(ref, s, i, jnp.concatenate([first[:, 0:128], mid, second[:, 0:128]], axis=1))

    def stage_f(n):
        placed = dot(perm_ref[lax.div(n, S)], acc[...].astype(BF16)).astype(BF16)
        put_whole(given, n, dot(placed, turn_ref[...]))

    def stage_b(n):
        way = lax.div(n, S)
        for i in range(slots):
            put_by_column(made, n, i, dot(by_column(taken, n, i), wm[way, i]))

    def stage_u(n):
        table = lax.div(n, S)
        turned = jnp.transpose(whole_of(back, n))
        cut = K // 128 * 128
        first = turned[0:K]
        second = jnp.concatenate([turned[2 * K - cut :], turned[K : 2 * K - cut]], axis=0)
        parts = []
        for q in range(2):
            base = 2 * q * channels
            at = lambda col, row: col[base + row * channels : base + (row + 1) * channels]
            m00, m10, m01, m11 = at(first, 0), at(first, 1), at(second, 0), at(second, 1)
            parts.append(jnp.concatenate([m00 + m11, m00 - m11, m01 + m10, m01 - m10], axis=0).astype(BF16))
        both = dot(parts[0], back_ref[table, 0]) + dot(parts[1], back_ref[table, 1])
        gb[n, z] = both.astype(BF16)

    def inverse_rows(n, base):
        spread = dot(gb[n].reshape(nz * K, 2 * M), single[...])
        group = lax.broadcasted_iota(jnp.int32, (K, 128), 1) // 16
        for col in range(pairs // 8):
            cut = slice(col * 128, col * 128 + 128)
            parts = [spread[c * K : (c + 1) * K, cut] for c in range(nz)]
            parts = [parts[0]] + [pltpu.roll(parts[c], 16 * c, 1) for c in range(1, nz)]
            for first in range(4):
                which = (group + (8 - first)) % 4
                mixed = jnp.where(which == 0, parts[0], jnp.where(which == 1, parts[1], jnp.where(which == 2, parts[2], parts[3])))
                for turn in (first, first + 4):
                    inside = (group + (8 - turn)) % 8 < 4
                    l2[col * 8 + turn] = jnp.where(inside, mixed, base[turn]).astype(BF16)

    def with_columns(x2, turn):
        rows = [x2[0:128]]
        for g in range(8):
            i = (g - turn) % 8
            rows.append(cblk_ref[16 * i : 16 * i + 16, :] if i < 4 else x2[64 + 16 * i : 80 + 16 * i])
        return jnp.concatenate(rows, axis=0)

    def columns_of(s, blk):
        for u in range(8):
            p = blk * 8 + u
            part = dot_nt(cblk_ref[...], pair_of(xb, s, p))
            put_columns(p, part.astype(BF16))

    def activate(s, blk):
        f = table_ref[scale_ref[s]]
        for u in range(8):
            p = blk * 8 + u
            x2 = pair_of(xb, s, p)
            both = with_columns(x2, u)
            half = (0.5 * f) * dot(jnp.concatenate([kt1[...], l2[p]], axis=1), both)
            square = half * half
            rise = 1.0 + jnp.tanh(half * (2.0 * GELU_A + 8.0 * GELU_B * square))
            y = (x2.astype(F32) + half * rise).astype(BF16)
            slope = rise + (rise * (2.0 - rise)) * (half * (2.0 * GELU_A + 24.0 * GELU_B * square))
            c2 = pair_of(ob, s, p).astype(F32)
            g2 = (((0.5 * f) * c2) * slope).astype(BF16)
            for e in range(2):
                ob[s, 2 * p + e] = y[:, e * W : (e + 1) * W]
                xb[s, 2 * p + e] = g2[:, e * W : (e + 1) * W]
            down = dot_nt(both, g2)
            gk_ref[0:128] += down[0:128]
            for g in range(8):
                i = (g - u) % 8
                piece = down[128 + 16 * g : 144 + 16 * g]
                if i < 4:
                    cols[i, pl.ds(p * 16, 16), 0:K] = piece.astype(BF16)
                else:
                    gk_ref[64 + 16 * i : 80 + 16 * i] += piece

    def field_gradient(s, blk):
        slot = lax.rem(s, 2)
        for u in range(8):
            p = blk * 8 + u
            both = with_columns(pair_of(xb, s, p), u)
            y = dot(jnp.concatenate([kk1[...], l2[p]], axis=1), both)
            y = (y + pair_of(eb, slot, p).astype(F32)).astype(BF16)
            for e in range(2):
                xb[s, 2 * p + e] = y[:, e * W : (e + 1) * W]

    def pa_copy(peer):
        return pltpu.make_async_remote_copy(
            src_ref=pa.at[me], dst_ref=pa.at[me], send_sem=pa_s.at[0], recv_sem=pa_r.at[0],
            device_id=(peer, z), device_id_type=MESH,
        )

    def pz_copy(peer):
        return pltpu.make_async_remote_copy(
            src_ref=pz.at[z], dst_ref=pz.at[z], send_sem=pz_s.at[0], recv_sem=pz_r.at[0],
            device_id=(me, peer), device_id_type=MESH,
        )

    def all_but_one(ref, count, ssem, rsem, device):
        rest = ref.at[pl.ds(0, count - 1)]
        return pltpu.make_async_remote_copy(
            src_ref=rest, dst_ref=rest, send_sem=ssem.at[0], recv_sem=rsem.at[0],
            device_id=device, device_id_type=MESH,
        )

    def point_first():
        left = gk_ref[...]
        total = jnp.zeros((channels, K), F32)
        for part in range(3):
            term = left.astype(BF16)
            left = left - term.astype(F32)
            turned = dot_nt(eye_ref[0:K, 0:K], term).astype(BF16)
            for k in range(4):
                total += dot_nt(turned[k * channels : (k + 1) * channels], sign_ref[k, :, 0:K])
        pa[me] = total

        def send(d, carry):
            pa_copy(lax.rem(me + d, nb)).start()
            return carry

        lax.fori_loop(1, nb, send, 0)

    def point_second():
        all_but_one(pa, nb, pa_s, pa_r, (lax.rem(me + 1, nb), z)).wait_recv()
        pz[z] = jnp.sum(pa[...], axis=0)

        def send(d, carry):
            pz_copy(lax.rem(z + d, nz)).start()
            return carry

        lax.fori_loop(1, nz, send, 0)

    def slot_gradients():
        for i in range(slots):
            g_all = jnp.concatenate([by_column(taken, S + s, i) for s in range(S)], axis=0)
            x_all = jnp.concatenate([by_column(taken, s, i) for s in range(S)], axis=0)
            g_turned = dot_nt(eye_ref[...], g_all).astype(BF16)
            wm[1, i] = dot(g_turned, x_all).astype(BF16)

        total = jnp.zeros((slots * channels, wide), F32)
        for part in range(4):
            rows = slice(part * channels, (part + 1) * channels)
            block = jnp.concatenate([wm[1, i, rows, :] for i in range(slots)], axis=0)
            total += dot_nt(block, psi[part])
        dw_ref[...] = total.reshape(slots, channels, wide)

    def orthogonal(moments):
        def split(v):
            high = v.astype(BF16)
            return high, (v - high.astype(F32)).astype(BF16)

        def product(a, b, mul):
            (ah, al), (bh, bl) = a, b
            return mul(ah, bh) + (mul(ah, bl) + mul(al, bh))

        current = [m / (jnp.sqrt(jnp.sum(m * m)) + 1e-07) for m in moments]
        for repeat in range(5):
            parts = [split(v) for v in current]
            grams = [product(v, v, dot_nt) for v in parts]
            gram_parts = [split(v) for v in grams]
            squares = [product(v, v, dot) for v in gram_parts]
            polynomials = [split(QUINTIC_SECOND * g + QUINTIC_THIRD * q) for g, q in zip(grams, squares)]
            current = [
                QUINTIC_FIRST * v + product(p, w, dot) for v, p, w in zip(current, polynomials, parts)
            ]
        return current

    def slot_updates(chosen):
        moments = [MOMENTUM_DECAY * momentum_ref[i] + dw_ref[i] for i in chosen]
        for i, value in zip(chosen, orthogonal(moments)):
            turned_ref[i] = value

    def point_update():
        all_but_one(pz, nz, pz_s, pz_r, (me, lax.rem(z + 1, nz))).wait_recv()
        total = jnp.sum(pz[...], axis=0)
        pg_ref[...] = total
        (point_turned_ref[...],) = orthogonal([MOMENTUM_DECAY * point_momentum_ref[...] + total])

    at_step = {2 * S: point_first, 2 * S + 1: point_second, 2 * S + 3: slot_gradients, 2 * S + 6: point_update}
    groups = [range(slots)[: slots // 2], range(slots)[slots // 2 :]]
    for step, group in enumerate(groups):
        if group:
            at_step[2 * S + 4 + step] = functools.partial(slot_updates, group)
    half = pairs // 8 // 2

    def on(n):
        return (n >= 0) & (n < 2 * S)

    def blocks(work, s, part):
        for blk in range(part * half, (part + 1) * half):
            work(s, blk)

    def iteration(t, carry):
        starts, turns, ends = t < S, (t >= S) & (t < 2 * S), t >= 2 * S
        pl.when(on(t - 2))(lambda: rs_hop(2, t - 2))
        pl.when(on(t - 6))(lambda: ag_hop(2, t - 6))

        @pl.when(starts)
        def _():
            x_copy(t).wait()
            blocks(columns_of, t, 0)

        @pl.when(turns)
        def _():
            ag_hop(last, t - S)
            inverse_rows(t - S, ktb)
            ct_copy(t - S).wait()
            blocks(activate, t - S, 0)

        @pl.when(ends)
        def _():
            s = t - 2 * S

            @pl.when(s + 1 < S)
            def _():
                ect_copy(s + 1).start()

            ag_hop(last, t - S)
            inverse_rows(t - S, kkb)
            ect_copy(s).wait()
            blocks(field_gradient, s, 0)

        pl.when(on(t - 1))(lambda: rs_hop(1, t - 1))
        pl.when(on(t - 5))(lambda: ag_hop(1, t - 5))
        pl.when(on(t - 3))(lambda: exchanged(t - 3, given, taken, 0).wait_recv())
        pl.when(on(t - 4))(lambda: exchanged(t - 4, made, back, 1).wait_recv())

        @pl.when(turns)
        def _():
            stage_u(t - 4)
            stage_b(t - 3)
            blocks(activate, t - S, 1)

        pl.when(starts)(lambda: blocks(columns_of, t, 1))
        pl.when(on(t - 4) & ~turns)(lambda: stage_u(t - 4))
        pl.when(on(t - 4))(lambda: ag_hop(0, t - 4))
        pl.when(on(t - 3) & ~turns)(lambda: stage_b(t - 3))
        pl.when(on(t - 3))(lambda: exchange(t - 3, made, back, 1))
        pl.when(ends)(lambda: blocks(field_gradient, t - 2 * S, 1))
        pl.when(on(t - 2))(lambda: rs_final(t - 2))

        @pl.when(turns)
        def _():
            stage_f(t - 2)
            forward_rows(t)

        pl.when(starts)(lambda: forward_rows(t))
        pl.when(~ends)(lambda: rs_hop(0, t))
        pl.when(on(t - 2) & ~turns)(lambda: stage_f(t - 2))
        pl.when(on(t - 2))(lambda: exchange(t - 2, given, taken, 0))
        for step, work in at_step.items():
            pl.when(t == step)(work)
        return carry

    pl.semaphore_wait(barrier, nb + nz - 2)

    lax.fori_loop(0, 3 * S, iteration, 0)

    def finish(n, carry):
        for j in range(last):
            rs_hop(j, n, True)
            ag_hop(j, n, True)
        exchanged(n, given, taken, 0).wait_send()
        exchanged(n, made, back, 1).wait_send()
        return carry

    lax.fori_loop(0, 2 * S, finish, 0)
    all_but_one(pa, nb, pa_s, pa_r, (lax.rem(me + 1, nb), z)).wait_send()
    all_but_one(pz, nz, pz_s, pz_r, (me, lax.rem(z + 1, nz))).wait_send()


def store_kernel(
    ob, xb, dw_ref, pg_ref, turned_ref, point_turned_ref, master_ref, momentum_ref, point_ref, point_momentum_ref,
    out_hbm, ig_hbm, grad_ref, moment_ref, weight_ref, low_ref,
    point_grad_ref, point_moment_ref, point_weight_ref, point_low_ref, sem,
):
    S = ob.shape[0]
    copies = []
    for s in range(S):
        copies.append(pltpu.make_async_copy(ob.at[s], out_hbm.at[s], sem.at[0, s]))
        copies.append(pltpu.make_async_copy(xb.at[s], ig_hbm.at[s], sem.at[1, s]))
    for copy in copies:
        copy.start()
    point_grad_ref[...] = pg_ref[...]
    point_moment_ref[...] = MOMENTUM_DECAY * point_momentum_ref[...] + pg_ref[...]
    point_weight = point_ref[...] - POINTWISE_RATE * point_turned_ref[...]
    point_weight_ref[...] = point_weight
    point_low_ref[...] = point_weight.astype(BF16)
    grad_ref[...] = dw_ref[...]
    moment_ref[...] = MOMENTUM_DECAY * momentum_ref[...] + dw_ref[...]
    weight = master_ref[...] - SPECTRAL_RATE * turned_ref[...]
    weight_ref[...] = weight
    low_ref[...] = weight.astype(BF16)
    for copy in copies:
        copy.wait()


def per_device(
    input_field,
    cotangent,
    sample_scale,
    scale_table,
    owner_map,
    spectral_master,
    spectral_momentum,
    pointwise_master,
    pointwise_momentum,
):
    S, H, K, W = input_field.shape
    nz = lax.axis_size("row")
    nb = lax.axis_size("batch")
    slots = spectral_master.shape[0]
    channels = K // 4
    wide = 2 * K
    local_columns = COLUMN_MODES // nz
    M = ROW_MODES * local_columns
    grid = H * nz

    anywhere = pl.BlockSpec(memory_space=pltpu.HBM)
    smem = pl.BlockSpec(memory_space=pltpu.SMEM)
    vmem = pl.BlockSpec(memory_space=pltpu.VMEM)
    exchange_shape = (2 * S, wide // 128, nb * slots, 128) if slots % 8 == 0 else (2 * S, nb, slots, wide)
    dma = pltpu.SemaphoreType.DMA
    single = jnp.asarray(row_blocks(grid, nz))
    psi, turn, signs = (jnp.asarray(one) for one in product_signs(channels))
    column_rows = jnp.asarray(column_block(W, nz))
    unit = jnp.asarray(np.eye(256).astype(ml_dtypes.bfloat16))
    slot_shape, point_shape = spectral_master.shape, pointwise_master.shape
    kept = pl.pallas_call(
        functools.partial(layer_kernel, (nb, nz, S, H, K, W, slots, M)),
        out_shape=(
            pltpu.VMEM(input_field.shape, BF16),
            pltpu.VMEM(input_field.shape, BF16),
            pltpu.VMEM(slot_shape, F32),
            pltpu.VMEM(point_shape, F32),
            pltpu.VMEM(slot_shape, F32),
            pltpu.VMEM(point_shape, F32),
        ),
        in_specs=[anywhere, anywhere, smem, smem, smem] + [anywhere] * 4 + [vmem] * 6,
        out_specs=(vmem,) * 6,
        scratch_shapes=[
            pltpu.VMEM((2, H, K, W), BF16),
            pltpu.VMEM(single.shape[1:], BF16),
            pltpu.VMEM(psi.shape, BF16),
            pltpu.VMEM(spectral_master.shape, F32),
            pltpu.VMEM(spectral_master.shape, F32),
            pltpu.VMEM((2, slots, 256, 256), BF16),
            pltpu.VMEM((nz, single.shape[2], 256), BF16),
            pltpu.VMEM((H // 2, K, 128), BF16),
            pltpu.VMEM((K, 128), BF16),
            pltpu.VMEM((8, K, 128), F32),
            pltpu.VMEM((K, 128), BF16),
            pltpu.VMEM((8, K, 128), F32),
            pltpu.VMEM((M, wide), F32),
            pltpu.VMEM((K, K), F32),
            pltpu.VMEM((nb, channels, K), F32),
            pltpu.VMEM((nz, channels, K), F32),
            pltpu.VMEM((M, 2 * M), F32),
            pltpu.VMEM((M, 2 * M), F32),
            pltpu.VMEM((2, M, M), BF16),
            pltpu.VMEM((2, 2, M, 2 * M), BF16),
            pltpu.VMEM((2 * S, nz, M, wide), BF16),
            pltpu.VMEM((2 * S, 2, nz, M, wide), BF16),
            pltpu.VMEM((2 * S, nz, K, 2 * M), BF16),
        ]
        + [pltpu.VMEM(exchange_shape, F32)] * 4
        + [dma((S,)), dma((S,)), dma((4,)), dma((2,))]
        + [dma((1,))] * 4
        + [dma((2 * S, 2, nz)), dma((2 * S, 2, nz)), dma((2 * S, 2, nz)), dma((2 * S, nz))]
        + [dma((2, 2 * S))] * 2,
        compiler_params=pltpu.CompilerParams(
            collective_id=0, has_side_effects=True, vmem_limit_bytes=37 * 1024 * 1024
        ),
    )(
        input_field, cotangent, sample_scale, scale_table, owner_map, single, psi,
        spectral_master, spectral_momentum, turn, signs, column_rows, unit, pointwise_master, pointwise_momentum,
    )

    held = [pltpu.with_memory_space_constraint(one, pltpu.VMEM) for one in kept]
    input_shape = jax.ShapeDtypeStruct(input_field.shape, BF16)
    results = pl.pallas_call(
        store_kernel,
        out_shape=(
            input_shape,
            input_shape,
            jax.ShapeDtypeStruct(slot_shape, F32),
            jax.ShapeDtypeStruct(slot_shape, F32),
            jax.ShapeDtypeStruct(slot_shape, F32),
            jax.ShapeDtypeStruct(slot_shape, BF16),
            jax.ShapeDtypeStruct(point_shape, F32),
            jax.ShapeDtypeStruct(point_shape, F32),
            jax.ShapeDtypeStruct(point_shape, F32),
            jax.ShapeDtypeStruct(point_shape, BF16),
        ),
        in_specs=[vmem] * 10,
        out_specs=(anywhere, anywhere) + (vmem,) * 8,
        scratch_shapes=[dma((2, S))],
        compiler_params=pltpu.CompilerParams(vmem_limit_bytes=6 * 1024 * 1024),
    )(*held, spectral_master, spectral_momentum, pointwise_master, pointwise_momentum)
    return tuple(results)


def solution(mesh):
    return jax.shard_map(
        per_device,
        mesh=mesh,
        in_specs=(
            P("batch", "row", None, None),
            P("batch", "row", None, None),
            P("batch"),
            P(),
            P(),
            P(("batch", "row"), None, None),
            P(("batch", "row"), None, None),
            P(),
            P(),
        ),
        out_specs=(
            P("batch", "row", None, None),
            P("batch", "row", None, None),
            P(("batch", "row"), None, None),
            P(("batch", "row"), None, None),
            P(("batch", "row"), None, None),
            P(("batch", "row"), None, None),
            P(),
            P(),
            P(),
            P(),
        ),
        check_vma=False,
    )
```

```python
import functools
import math

import jax
import jax.numpy as jnp
import ml_dtypes
import numpy as np
from jax import lax
from jax.experimental import pallas as pl
from jax.experimental.pallas import tpu as pltpu
from jax.sharding import PartitionSpec as P

ROW_MODES = 16
COLUMN_MODES = 16

BLADE_SIGNS = np.array([[1, 1, 1, 1], [1, 1, 1, 1], [1, -1, 1, -1], [1, -1, 1, -1]], np.float32)
QUINTIC_FIRST = 3.4445
QUINTIC_SECOND = -4.775
QUINTIC_THIRD = 2.0315
SPECTRAL_RATE = 4.0
POINTWISE_RATE = 0.8
MOMENTUM_DECAY = 0.5
MESH = pl.DeviceIdType.MESH
F32 = jnp.float32
BF16 = jnp.bfloat16
GELU_A = math.sqrt(2.0 / math.pi)
GELU_B = GELU_A * 0.044715


MATRIX_SIGNS = np.zeros((2, 2, 4), np.float32)
MATRIX_SIGNS[0, 0, 0] = MATRIX_SIGNS[0, 0, 1] = MATRIX_SIGNS[1, 1, 0] = 1.0
MATRIX_SIGNS[1, 1, 1] = MATRIX_SIGNS[1, 0, 3] = -1.0
MATRIX_SIGNS[0, 1, 2] = MATRIX_SIGNS[0, 1, 3] = MATRIX_SIGNS[1, 0, 2] = 1.0


def column_block(grid_size, row_count):
    angles = 2.0 * np.pi / grid_size * (np.arange(COLUMN_MODES)[:, None] * np.arange(grid_size)[None] % grid_size)
    table = np.stack([np.cos(angles), -np.sin(angles)], 0).reshape(2, row_count, -1, grid_size)
    full = np.einsum("pclw,hg->chplgw", table, np.eye(2))
    return full.reshape(4 * COLUMN_MODES, 2 * grid_size).astype(ml_dtypes.bfloat16)


def row_blocks(grid_size, row_count):
    rows = grid_size // row_count
    local = COLUMN_MODES // row_count
    r = np.arange(ROW_MODES)
    frequency = np.where(r < ROW_MODES // 2, r, grid_size - ROW_MODES + r)
    angles = 2.0 * np.pi / grid_size * (frequency[:, None] * np.arange(grid_size)[None] % grid_size)
    cosine, sine = np.cos(angles), np.sin(angles)
    table = np.stack([np.stack([cosine, sine], -1), np.stack([-sine, cosine], -1)], 0)
    table = table.reshape(2, ROW_MODES, row_count, rows, 2)
    full = np.einsum("qrzhp,cd->zqrchpd", table, np.eye(local))
    return full.reshape(row_count, 2 * ROW_MODES * local, rows * 2 * local).astype(ml_dtypes.bfloat16)


def lanes_of_columns(channels):
    half = 4 * channels
    place = np.arange(2 * half)
    cut = half // 128 * 128
    first = np.arange(half)
    second = np.where(first < cut, half + (half - cut) + first, half + first - cut)
    return place[first], place[second]


def product_signs(channels):
    unit = np.eye(channels, dtype=np.float32)
    psi = np.zeros((2, 2, 2, 4, 2, 2), np.float32)
    for q in range(2):
        for p in range(2):
            part = -1.0 if (q == 0 and p == 1) else 1.0
            for row in range(2):
                for inner in range(2):
                    psi[q, row, p ^ q, :, p, inner] = part * MATRIX_SIGNS[row, inner]
    psi = np.einsum("qrwapn,ij->qrwaipnj", psi, unit).reshape(4, 8 * channels, 4 * channels)
    psi = np.pad(psi, ((0, 0), (0, 0), (0, 256 - 4 * channels)))
    spread = np.einsum("pt,ncb,ij->pbictnj", np.eye(2), MATRIX_SIGNS, unit)
    spread = spread.reshape(8 * channels, 2, 4 * channels)
    turn = np.zeros((8 * channels, 8 * channels), np.float32)
    for col, lanes in enumerate(lanes_of_columns(channels)):
        turn[:, lanes] = spread[:, col]
    point = np.zeros((4, 4, 4), np.float32)
    for k in range(4):
        for b in range(4):
            point[k, k ^ b, b] = BLADE_SIGNS[k ^ b, b]
    point = np.einsum("kab,ij->kaibj", point, unit).reshape(4, 4 * channels, 4 * channels)
    point = np.pad(point, ((0, 0), (0, 0), (0, 256 - 4 * channels)))
    return (one.astype(ml_dtypes.bfloat16) for one in (psi, turn, point))


def dot(a, b):
    return lax.dot_general(a, b, (((1,), (0,)), ((), ())), preferred_element_type=F32)


def dot_nt(a, b):
    return lax.dot_general(a, b, (((1,), (1,)), ((), ())), preferred_element_type=F32)


def layer_kernel(
    sizes,
    x_hbm, ct_hbm, scale_ref, table_ref, owner_ref, single_hbm, psi_hbm, master_hbm, momentum_hbm,
    turn_ref, sign_ref, cblk_ref, eye_ref, point_ref, point_momentum_ref,
    ob, xb, dw_ref, pg_ref, turned_ref, point_turned_ref,
    eb, single, psi, master_ref, momentum_ref, wm, cols, l2, kt1, ktb, kk1, kkb, acc, gk_ref, pa, pz,
    lows, highs, perm_ref, back_ref,
    pb1, rb1, gb1, pb2, rb2, gb2,
    xs, xr, ps, pr, gs, gr, hs, hr,
    x_sem, ct_sem, ld_sem, ei_sem, pa_s, pa_r, pz_s, pz_r,
    rs1_s, rs1_r, rs2_s, rs2_r, ag1_s, ag1_r, ag2_s, ag2_r, a2a_s, a2a_r,
):
    nb, nz, S, H, K, W, slots, M = sizes
    wide = 2 * K
    channels = K // 4
    pairs = H // 2
    me = lax.axis_index("batch")
    z = lax.axis_index("row")
    last = nz - 1

    loads = [
        pltpu.make_async_copy(psi_hbm, psi, ld_sem.at[0]),
        pltpu.make_async_copy(single_hbm.at[z], single, ld_sem.at[1]),
        pltpu.make_async_copy(master_hbm, master_ref, ld_sem.at[2]),
        pltpu.make_async_copy(momentum_hbm, momentum_ref, ld_sem.at[3]),
    ]
    x_copy = lambda s: pltpu.make_async_copy(x_hbm.at[s], xb.at[s], x_sem.at[s])
    ct_copy = lambda s: pltpu.make_async_copy(ct_hbm.at[s], ob.at[s], ct_sem.at[s])
    ect_copy = lambda s: pltpu.make_async_copy(ct_hbm.at[s], eb.at[lax.rem(s, 2)], ei_sem.at[lax.rem(s, 2)])

    barrier = pltpu.get_barrier_semaphore()

    def greet(d, carry):
        peer = lax.rem(me + d, nb)
        pl.semaphore_signal(barrier, inc=1, device_id=(peer, z), device_id_type=MESH)
        return carry

    lax.fori_loop(1, nb, greet, 0)

    def greet_z(d, carry):
        pl.semaphore_signal(barrier, inc=1, device_id=(me, lax.rem(z + d, nz)), device_id_type=MESH)
        return carry

    lax.fori_loop(1, nz, greet_z, 0)
    x_copy(0).start()
    loads[1].start()
    x_copy(1).start()
    loads[0].start()
    loads[2].start()
    x_copy(2).start()
    loads[3].start()
    cols[...] = jnp.zeros_like(cols)
    gk_ref[...] = jnp.zeros_like(gk_ref)

    def place_modes():
        local = COLUMN_MODES // nz
        lane = lax.broadcasted_iota(jnp.int32, (1, 2 * M), 1)

        def place(d, carry):
            for i in range(slots):
                mode = owner_ref[(d * nz + z) * slots + i]
                at = lax.div(mode, COLUMN_MODES) * local + lax.rem(mode, local)
                lows[pl.ds(d * slots + i, 1), :] = jnp.where(lane == at, 1.0, 0.0)
                highs[pl.ds(d * slots + i, 1), :] = jnp.where(lane == at + M, 1.0, 0.0)
            return carry

        lax.fori_loop(0, nb, place, 0)
        inner = 1.0 / (H * nz * H * nz)
        weigh = jnp.where(z * local + lax.rem(lane, local) == 0, 0.5 * inner, inner)
        for table, pick in enumerate((lambda v: v[...], lambda v: v[...] * weigh)):
            perm_ref[table] = pick(lows)[:, 0:M].astype(BF16)
            back_ref[1 - table, 0] = pick(lows).astype(BF16)
            back_ref[1 - table, 1] = pick(highs).astype(BF16)

    def point_kernels():
        weight = point_ref[...].astype(BF16)
        kernel_t = jnp.concatenate([dot(weight, sign_ref[k]) for k in range(4)], axis=0)
        kt1[...] = kernel_t[:, 0:128].astype(BF16)
        for turn in range(8):
            ktb[turn] = pltpu.roll(kernel_t[:, 128:256], (64 + 16 * turn) % 128, 1)
        padded = jnp.concatenate([kernel_t.astype(BF16), jnp.zeros((256 - K, 256), BF16)], axis=0)
        kernel_n = dot_nt(eye_ref[0:K], padded)
        kk1[...] = kernel_n[:, 0:128].astype(BF16)
        for turn in range(8):
            kkb[turn] = pltpu.roll(kernel_n[:, 128:256], (64 + 16 * turn) % 128, 1)

    def expand_weights():
        loads[0].wait()
        loads[2].wait()
        wm[...] = jnp.zeros_like(wm)
        masters = master_ref[...].reshape(slots * channels, wide).astype(BF16)
        for part in range(4):
            block = dot(masters, psi[part]).astype(BF16)
            for i in range(slots):
                wm[i, part * channels : (part + 1) * channels, :] = block[i * channels : (i + 1) * channels]

    def rs_copy(s, up, c, pb, rb, ssem, rsem):
        way = 0 if up else 1
        return pltpu.make_async_remote_copy(
            src_ref=pb.at[s, c], dst_ref=rb.at[s, way, c],
            send_sem=ssem.at[s, way, c], recv_sem=rsem.at[s, way, c],
            device_id=(me, z + 1 if up else z - 1), device_id_type=MESH,
        )

    def rs_hop(j, s, bufs, finish=False):
        pb, rb = bufs[0], bufs[1]
        for up in (True, False):
            place = z if up else last - z
            c = (last - j + z) if up else (z - (last - j))

            @pl.when(place <= j)
            def _():
                copy = rs_copy(s, up, c, *bufs)
                if finish:
                    copy.wait_send()
                else:
                    @pl.when(place > 0)
                    def _():
                        way = 0 if up else 1
                        copy.wait_recv()
                        pb[s, c] = (pb[s, c].astype(F32) + rb[s, way, c].astype(F32)).astype(BF16)

                    copy.start()

    def rs_final(s, bufs):
        pb, rb = bufs[0], bufs[1]
        acc[...] = pb[s, z].astype(F32)

        @pl.when(z > 0)
        def _():
            rs_copy(s, True, z, *bufs).wait_recv()
            acc[...] += rb[s, 0, z].astype(F32)

        @pl.when(z < last)
        def _():
            rs_copy(s, False, z, *bufs).wait_recv()
            acc[...] += rb[s, 1, z].astype(F32)

        return acc[...].astype(BF16)

    def ag_copy(s, up, c, gb, ssem, rsem):
        way = 0 if up else 1
        return pltpu.make_async_remote_copy(
            src_ref=gb.at[s, c], dst_ref=gb.at[s, c],
            send_sem=ssem.at[s, way, c], recv_sem=rsem.at[s, c],
            device_id=(me, z + 1 if up else z - 1), device_id_type=MESH,
        )

    def ag_hop(j, s, bufs, finish=False):
        for up in (True, False):
            c = z - j if up else z + j
            more = z < last if up else z > 0

            @pl.when((c >= 0) if up else (c <= last))
            def _():
                copy = ag_copy(s, up, c, *bufs)
                if j > 0 and not finish:
                    copy.wait_recv()

                if j < last:
                    @pl.when(more)
                    def _():
                        if finish:
                            copy.wait_send()
                        else:
                            copy.start()

    tiled = slots % 8 == 0

    def block_of(ref, s, d):
        if tiled:
            return ref.at[s, :, pl.ds(pl.multiple_of(d * slots, slots), slots)]
        return ref.at[s, d]

    def blocks_of(ref, s):
        if tiled:
            return ref.at[s, :, pl.ds(0, (nb - 1) * slots)]
        return ref.at[s, pl.ds(0, nb - 1)]

    def whole_of(ref, s):
        if tiled:
            return jnp.concatenate([ref[s, g] for g in range(wide // 128)], axis=1)
        return ref[s].reshape(nb * slots, wide)

    def put_whole(ref, s, value):
        if tiled:
            for g in range(wide // 128):
                ref[s, g] = value[:, g * 128 : (g + 1) * 128]
        else:
            ref[s] = value.reshape(nb, slots, wide)

    def slot_rows(ref, s, i):
        if tiled:
            return jnp.concatenate([ref[s, g, pl.ds(i, nb, stride=slots), :] for g in range(wide // 128)], axis=1)
        return ref[s, :, i, :]

    def put_slot_rows(ref, s, i, value):
        if tiled:
            for g in range(wide // 128):
                ref[s, g, pl.ds(i, nb, stride=slots), :] = value[:, g * 128 : (g + 1) * 128]
        else:
            ref[s, :, i, :] = value

    def exchange(s, src, dst, which):
        def send(d, carry):
            peer = lax.rem(me + d, nb)
            pltpu.make_async_remote_copy(
                src_ref=block_of(src, s, peer), dst_ref=block_of(dst, s, me),
                send_sem=a2a_s.at[which, s], recv_sem=a2a_r.at[which, s],
                device_id=(peer, z), device_id_type=MESH,
            ).start()
            return carry

        lax.fori_loop(1, nb, send, 0)
        block_of(dst, s, me)[...] = block_of(src, s, me)[...]

    def exchanged(s, src, dst, which):
        return pltpu.make_async_remote_copy(
            src_ref=blocks_of(src, s), dst_ref=blocks_of(dst, s),
            send_sem=a2a_s.at[which, s], recv_sem=a2a_r.at[which, s],
            device_id=(lax.rem(me + 1, nb), z), device_id_type=MESH,
        )

    def forward_rows(s, pb):
        for c in range(nz):
            part = dot(single[...], cols[c])
            first = part[0:M]
            second = pltpu.roll(part[M:], 64, 1)
            pb[s, c, :, 0:128] = first[:, 0:128].astype(BF16)
            pb[s, c, :, 128:256] = (first[:, 128:256] + second[:, 0:128]).astype(BF16)
            pb[s, c, :, 256:384] = second[:, 128:256].astype(BF16)

    def put_columns(p, value):
        step = 4 * COLUMN_MODES // nz
        for c in range(nz):
            cols[c, pl.ds(pl.multiple_of(p * step, step), step), 0:K] = value[c * step : (c + 1) * step]

    def pair_of(ref, s, p):
        return jnp.concatenate([ref[s, 2 * p], ref[s, 2 * p + 1]], axis=1)

    def stage_a(s):
        x_copy(s).wait()

        def some(blk, carry):
            for u in range(8):
                p = blk * 8 + u
                part = dot_nt(cblk_ref[...], pair_of(xb, s, p))
                put_columns(p, part.astype(BF16))
            return carry

        lax.fori_loop(0, pairs // 8, some, 0)
        forward_rows(s, pb1)
        rs_hop(0, s, rs1)

    def by_column(ref, s, i):
        rows = slot_rows(ref, s, i)
        low, mid, top = rows[:, 0:128], rows[:, 128:256], rows[:, 256:384]
        first = jnp.concatenate([low, mid], axis=1)
        second = jnp.concatenate([top, pltpu.roll(mid, 64, 1)], axis=1)
        return jnp.concatenate([first, second], axis=0).astype(BF16)

    def put_by_column(ref, s, i, value):
        first, second = value[0:nb], value[nb:]
        mid = first[:, 128:256] + pltpu.roll(second[:, 128:256], 64, 1)
        put_slot_rows(ref, s, i, jnp.concatenate([first[:, 0:128], mid, second[:, 0:128]], axis=1))

    def stage_b(s):
        exchanged(s, xs, xr, 0).wait_recv()
        for i in range(slots):
            put_by_column(ps, s, i, dot_nt(by_column(xr, s, i), wm[i]))
        exchange(s, ps, pr, 1)

    def stage_d(s):
        exchanged(s, gs, gr, 2).wait_recv()
        for i in range(slots):
            put_by_column(hs, s, i, dot(by_column(gr, s, i), wm[i]))
        exchange(s, hs, hr, 3)

    def stage_f(s, bufs, table, src, dst, which):
        placed = dot(perm_ref[table], rs_final(s, bufs)).astype(BF16)
        put_whole(src, s, dot(placed, turn_ref[...]))
        exchange(s, src, dst, which)

    def stage_u(s, bufs, table, src, dst, which):
        exchanged(s, src, dst, which).wait_recv()
        turned = jnp.transpose(whole_of(dst, s))
        cut = K // 128 * 128
        first = turned[0:K]
        second = jnp.concatenate([turned[2 * K - cut :], turned[K : 2 * K - cut]], axis=0)
        parts = []
        for q in range(2):
            base = 2 * q * channels
            at = lambda col, row: col[base + row * channels : base + (row + 1) * channels]
            m00, m10, m01, m11 = at(first, 0), at(first, 1), at(second, 0), at(second, 1)
            parts.append(jnp.concatenate([m00 + m11, m00 - m11, m01 + m10, m01 - m10], axis=0).astype(BF16))
        both = dot(parts[0], back_ref[table, 0]) + dot(parts[1], back_ref[table, 1])
        bufs[0][s, z] = both.astype(BF16)
        ag_hop(0, s, bufs)

    def inverse_rows(s, gb, base):
        spread = dot(gb[s].reshape(nz * K, 2 * M), single[...])
        group = lax.broadcasted_iota(jnp.int32, (K, 128), 1) // 16
        for col in range(pairs // 8):
            cut = slice(col * 128, col * 128 + 128)
            parts = [spread[c * K : (c + 1) * K, cut] for c in range(nz)]
            parts = [parts[0]] + [pltpu.roll(parts[c], 16 * c, 1) for c in range(1, nz)]
            for first in range(4):
                which = (group + (8 - first)) % 4
                mixed = jnp.where(which == 0, parts[0], jnp.where(which == 1, parts[1], jnp.where(which == 2, parts[2], parts[3])))
                for turn in (first, first + 4):
                    inside = (group + (8 - turn)) % 8 < 4
                    l2[col * 8 + turn] = jnp.where(inside, mixed, base[turn]).astype(BF16)

    def with_columns(x2, turn):
        rows = [x2[0:128]]
        for g in range(8):
            i = (g - turn) % 8
            rows.append(cblk_ref[16 * i : 16 * i + 16, :] if i < 4 else x2[64 + 16 * i : 80 + 16 * i])
        return jnp.concatenate(rows, axis=0)

    def stage_c(s):
        ag_hop(last, s, ag1)
        inverse_rows(s, gb1, ktb)
        ct_copy(s).wait()
        f = table_ref[scale_ref[s]]

        def some(blk, carry):
            for u in range(8):
                p = blk * 8 + u
                x2 = pair_of(xb, s, p)
                both = with_columns(x2, u)
                half = (0.5 * f) * dot(jnp.concatenate([kt1[...], l2[p]], axis=1), both)
                square = half * half
                rise = 1.0 + jnp.tanh(half * (2.0 * GELU_A + 8.0 * GELU_B * square))
                y = (x2.astype(F32) + half * rise).astype(BF16)
                slope = rise + (rise * (2.0 - rise)) * (half * (2.0 * GELU_A + 24.0 * GELU_B * square))
                c2 = pair_of(ob, s, p).astype(F32)
                g2 = (((0.5 * f) * c2) * slope).astype(BF16)
                for e in range(2):
                    ob[s, 2 * p + e] = y[:, e * W : (e + 1) * W]
                    xb[s, 2 * p + e] = g2[:, e * W : (e + 1) * W]
                back = dot_nt(both, g2)
                gk_ref[0:128] += back[0:128]
                for g in range(8):
                    i = (g - u) % 8
                    piece = back[128 + 16 * g : 144 + 16 * g]
                    if i < 4:
                        cols[i, pl.ds(pl.multiple_of(p * 16, 16), 16), 0:K] = piece.astype(BF16)
                    else:
                        gk_ref[64 + 16 * i : 80 + 16 * i] += piece
            return carry

        lax.fori_loop(0, pairs // 8, some, 0)
        forward_rows(s, pb2)
        rs_hop(0, s, rs2)

    def stage_e(s):
        slot = lax.rem(s, 2)

        @pl.when(s + 1 < S)
        def _():
            ect_copy(s + 1).start()

        ag_hop(last, s, ag2)
        inverse_rows(s, gb2, kkb)
        ect_copy(s).wait()

        def some(blk, carry):
            for u in range(8):
                p = blk * 8 + u
                both = with_columns(pair_of(xb, s, p), u)
                y = dot(jnp.concatenate([kk1[...], l2[p]], axis=1), both)
                y = (y + pair_of(eb, slot, p).astype(F32)).astype(BF16)
                for e in range(2):
                    xb[s, 2 * p + e] = y[:, e * W : (e + 1) * W]
            return carry

        lax.fori_loop(0, pairs // 8, some, 0)

    def pa_copy(peer):
        return pltpu.make_async_remote_copy(
            src_ref=pa.at[me], dst_ref=pa.at[me], send_sem=pa_s.at[0], recv_sem=pa_r.at[0],
            device_id=(peer, z), device_id_type=MESH,
        )

    def pz_copy(peer):
        return pltpu.make_async_remote_copy(
            src_ref=pz.at[z], dst_ref=pz.at[z], send_sem=pz_s.at[0], recv_sem=pz_r.at[0],
            device_id=(me, peer), device_id_type=MESH,
        )

    def all_but_one(ref, count, ssem, rsem, device):
        rest = ref.at[pl.ds(0, count - 1)]
        return pltpu.make_async_remote_copy(
            src_ref=rest, dst_ref=rest, send_sem=ssem.at[0], recv_sem=rsem.at[0],
            device_id=device, device_id_type=MESH,
        )

    def point_first():
        left = gk_ref[...]
        total = jnp.zeros((channels, K), F32)
        for part in range(3):
            term = left.astype(BF16)
            left = left - term.astype(F32)
            turned = dot_nt(eye_ref[0:K, 0:K], term).astype(BF16)
            for k in range(4):
                total += dot_nt(turned[k * channels : (k + 1) * channels], sign_ref[k, :, 0:K])
        pa[me] = total

        def send(d, carry):
            pa_copy(lax.rem(me + d, nb)).start()
            return carry

        lax.fori_loop(1, nb, send, 0)

    def point_second():
        all_but_one(pa, nb, pa_s, pa_r, (lax.rem(me + 1, nb), z)).wait_recv()
        pz[z] = jnp.sum(pa[...], axis=0)

        def send(d, carry):
            pz_copy(lax.rem(z + d, nz)).start()
            return carry

        lax.fori_loop(1, nz, send, 0)

    def slot_gradients():
        loads[3].wait()
        for i in range(slots):
            g_all = jnp.concatenate([by_column(gr, s, i) for s in range(S)], axis=0)
            x_all = jnp.concatenate([by_column(xr, s, i) for s in range(S)], axis=0)
            g_turned = dot_nt(eye_ref[...], g_all).astype(BF16)
            wm[i] = dot(g_turned, x_all).astype(BF16)

        total = jnp.zeros((slots * channels, wide), F32)
        for part in range(4):
            rows = slice(part * channels, (part + 1) * channels)
            block = jnp.concatenate([wm[i, rows, :] for i in range(slots)], axis=0)
            total += dot_nt(block, psi[part])
        dw_ref[...] = total.reshape(slots, channels, wide)

    def orthogonal(moments):
        def split(v):
            high = v.astype(BF16)
            return high, (v - high.astype(F32)).astype(BF16)

        def product(a, b, mul):
            (ah, al), (bh, bl) = a, b
            return mul(ah, bh) + (mul(ah, bl) + mul(al, bh))

        current = [m / (jnp.sqrt(jnp.sum(m * m)) + 1e-07) for m in moments]
        for repeat in range(5):
            parts = [split(v) for v in current]
            grams = [product(v, v, dot_nt) for v in parts]
            gram_parts = [split(v) for v in grams]
            squares = [product(v, v, dot) for v in gram_parts]
            polynomials = [split(QUINTIC_SECOND * g + QUINTIC_THIRD * q) for g, q in zip(grams, squares)]
            current = [
                QUINTIC_FIRST * v + product(p, w, dot) for v, p, w in zip(current, polynomials, parts)
            ]
        return current

    def slot_updates(chosen):
        moments = [MOMENTUM_DECAY * momentum_ref[i] + dw_ref[i] for i in chosen]
        for i, value in zip(chosen, orthogonal(moments)):
            turned_ref[i] = value

    def point_update():
        all_but_one(pz, nz, pz_s, pz_r, (me, lax.rem(z + 1, nz))).wait_recv()
        total = jnp.sum(pz[...], axis=0)
        pg_ref[...] = total
        (point_turned_ref[...],) = orthogonal([MOMENTUM_DECAY * point_momentum_ref[...] + total])

    rs1 = (pb1, rb1, rs1_s, rs1_r)
    rs2 = (pb2, rb2, rs2_s, rs2_r)
    ag1 = (gb1, ag1_s, ag1_r)
    ag2 = (gb2, ag2_s, ag2_r)

    schedule = [
        (0, stage_a),
        (3, lambda s: stage_f(s, rs1, 0, xs, xr, 0)),
        (11, lambda s: stage_f(s, rs2, 1, gs, gr, 2)),
        (2, lambda s: rs_hop(2, s, rs1)),
        (10, lambda s: rs_hop(2, s, rs2)),
        (1, lambda s: rs_hop(1, s, rs1)),
        (9, lambda s: rs_hop(1, s, rs2)),
        (7, lambda s: ag_hop(2, s, ag1)),
        (15, lambda s: ag_hop(2, s, ag2)),
        (6, lambda s: ag_hop(1, s, ag1)),
        (14, lambda s: ag_hop(1, s, ag2)),
        (5, lambda s: stage_u(s, ag1, 0, ps, pr, 1)),
        (13, lambda s: stage_u(s, ag2, 1, hs, hr, 3)),
        (4, stage_b),
        (12, stage_d),
        (8, stage_c),
        (16, stage_e),
    ]
    steps = S + max(lag for lag, _ in schedule)
    at_step = {0: place_modes, 1: expand_weights, 2: point_kernels, S + 8: point_first, S + 9: point_second, S + 11: point_update, S + 12: slot_gradients}
    groups = [range(slots)[: slots // 2], range(slots)[slots // 2 :]]
    for step, group in enumerate(groups):
        if group:
            at_step[S + 13 + step] = functools.partial(slot_updates, group)

    pl.semaphore_wait(barrier, nb + nz - 2)

    loads[1].wait()

    def iteration(t, carry):
        pl.when(t + 3 < S)(lambda: x_copy(t + 3).start())
        pl.when((t >= 5) & (t < S + 5))(lambda: ct_copy(t - 5).start())
        pl.when(t == 14)(lambda: ect_copy(0).start())
        for lag, stage in schedule:
            s = t - lag
            pl.when((s >= 0) & (s < S))(functools.partial(stage, s))
        for step, work in at_step.items():
            pl.when(t == step)(work)
        return carry

    lax.fori_loop(0, steps, iteration, 0)

    def finish(s, carry):
        for j in range(last):
            rs_hop(j, s, rs1, True)
            rs_hop(j, s, rs2, True)
            ag_hop(j, s, ag1, True)
            ag_hop(j, s, ag2, True)
        for which, (src, dst) in enumerate(((xs, xr), (ps, pr), (gs, gr), (hs, hr))):
            exchanged(s, src, dst, which).wait_send()
        return carry

    lax.fori_loop(0, S, finish, 0)
    all_but_one(pa, nb, pa_s, pa_r, (lax.rem(me + 1, nb), z)).wait_send()
    all_but_one(pz, nz, pz_s, pz_r, (me, lax.rem(z + 1, nz))).wait_send()


def store_kernel(
    ob, xb, dw_ref, pg_ref, turned_ref, point_turned_ref, master_ref, momentum_ref, point_ref, point_momentum_ref,
    out_hbm, ig_hbm, grad_ref, moment_ref, weight_ref, low_ref,
    point_grad_ref, point_moment_ref, point_weight_ref, point_low_ref, sem,
):
    S = ob.shape[0]
    copies = []
    for s in range(S):
        copies.append(pltpu.make_async_copy(ob.at[s], out_hbm.at[s], sem.at[0, s]))
        copies.append(pltpu.make_async_copy(xb.at[s], ig_hbm.at[s], sem.at[1, s]))
    for copy in copies:
        copy.start()
    point_grad_ref[...] = pg_ref[...]
    point_moment_ref[...] = MOMENTUM_DECAY * point_momentum_ref[...] + pg_ref[...]
    point_weight = point_ref[...] - POINTWISE_RATE * point_turned_ref[...]
    point_weight_ref[...] = point_weight
    point_low_ref[...] = point_weight.astype(BF16)
    grad_ref[...] = dw_ref[...]
    moment_ref[...] = MOMENTUM_DECAY * momentum_ref[...] + dw_ref[...]
    weight = master_ref[...] - SPECTRAL_RATE * turned_ref[...]
    weight_ref[...] = weight
    low_ref[...] = weight.astype(BF16)
    for copy in copies:
        copy.wait()


def per_device(
    input_field,
    cotangent,
    sample_scale,
    scale_table,
    owner_map,
    spectral_master,
    spectral_momentum,
    pointwise_master,
    pointwise_momentum,
):
    S, H, K, W = input_field.shape
    nz = lax.axis_size("row")
    nb = lax.axis_size("batch")
    slots = spectral_master.shape[0]
    channels = K // 4
    wide = 2 * K
    local_columns = COLUMN_MODES // nz
    M = ROW_MODES * local_columns
    grid = H * nz

    anywhere = pl.BlockSpec(memory_space=pltpu.HBM)
    smem = pl.BlockSpec(memory_space=pltpu.SMEM)
    vmem = pl.BlockSpec(memory_space=pltpu.VMEM)
    exchange_shape = (S, wide // 128, nb * slots, 128) if slots % 8 == 0 else (S, nb, slots, wide)
    dma = pltpu.SemaphoreType.DMA
    single = jnp.asarray(row_blocks(grid, nz))
    psi, turn, signs = (jnp.asarray(one) for one in product_signs(channels))
    column_rows = jnp.asarray(column_block(W, nz))
    unit = jnp.asarray(np.eye(256).astype(ml_dtypes.bfloat16))
    slot_shape, point_shape = spectral_master.shape, pointwise_master.shape
    kept = pl.pallas_call(
        functools.partial(layer_kernel, (nb, nz, S, H, K, W, slots, M)),
        out_shape=(
            pltpu.VMEM(input_field.shape, BF16),
            pltpu.VMEM(input_field.shape, BF16),
            pltpu.VMEM(slot_shape, F32),
            pltpu.VMEM(point_shape, F32),
            pltpu.VMEM(slot_shape, F32),
            pltpu.VMEM(point_shape, F32),
        ),
        in_specs=[anywhere, anywhere, smem, smem, smem] + [anywhere] * 4 + [vmem] * 6,
        out_specs=(vmem,) * 6,
        scratch_shapes=[
            pltpu.VMEM((2, H, K, W), BF16),
            pltpu.VMEM(single.shape[1:], BF16),
            pltpu.VMEM(psi.shape, BF16),
            pltpu.VMEM(spectral_master.shape, F32),
            pltpu.VMEM(spectral_master.shape, F32),
            pltpu.VMEM((slots, 256, 256), BF16),
            pltpu.VMEM((nz, single.shape[2], 256), BF16),
            pltpu.VMEM((H // 2, K, 128), BF16),
            pltpu.VMEM((K, 128), BF16),
            pltpu.VMEM((8, K, 128), F32),
            pltpu.VMEM((K, 128), BF16),
            pltpu.VMEM((8, K, 128), F32),
            pltpu.VMEM((M, wide), F32),
            pltpu.VMEM((K, K), F32),
            pltpu.VMEM((nb, channels, K), F32),
            pltpu.VMEM((nz, channels, K), F32),
            pltpu.VMEM((M, 2 * M), F32),
            pltpu.VMEM((M, 2 * M), F32),
            pltpu.VMEM((2, M, M), BF16),
            pltpu.VMEM((2, 2, M, 2 * M), BF16),
            pltpu.VMEM((S, nz, M, wide), BF16),
            pltpu.VMEM((S, 2, nz, M, wide), BF16),
            pltpu.VMEM((S, nz, K, 2 * M), BF16),
            pltpu.VMEM((S, nz, M, wide), BF16),
            pltpu.VMEM((S, 2, nz, M, wide), BF16),
            pltpu.VMEM((S, nz, K, 2 * M), BF16),
        ]
        + [pltpu.VMEM(exchange_shape, F32)] * 8
        + [dma((S,)), dma((S,)), dma((4,)), dma((2,))]
        + [dma((1,))] * 4
        + [dma((S, 2, nz))] * 4
        + [dma((S, 2, nz)), dma((S, nz))] * 2
        + [dma((4, S))] * 2,
        compiler_params=pltpu.CompilerParams(
            collective_id=0, has_side_effects=True, vmem_limit_bytes=37 * 1024 * 1024
        ),
    )(
        input_field, cotangent, sample_scale, scale_table, owner_map, single, psi,
        spectral_master, spectral_momentum, turn, signs, column_rows, unit, pointwise_master, pointwise_momentum,
    )

    held = [pltpu.with_memory_space_constraint(one, pltpu.VMEM) for one in kept]
    input_shape = jax.ShapeDtypeStruct(input_field.shape, BF16)
    results = pl.pallas_call(
        store_kernel,
        out_shape=(
            input_shape,
            input_shape,
            jax.ShapeDtypeStruct(slot_shape, F32),
            jax.ShapeDtypeStruct(slot_shape, F32),
            jax.ShapeDtypeStruct(slot_shape, F32),
            jax.ShapeDtypeStruct(slot_shape, BF16),
            jax.ShapeDtypeStruct(point_shape, F32),
            jax.ShapeDtypeStruct(point_shape, F32),
            jax.ShapeDtypeStruct(point_shape, F32),
            jax.ShapeDtypeStruct(point_shape, BF16),
        ),
        in_specs=[vmem] * 10,
        out_specs=(anywhere, anywhere) + (vmem,) * 8,
        scratch_shapes=[dma((2, S))],
        compiler_params=pltpu.CompilerParams(vmem_limit_bytes=6 * 1024 * 1024),
    )(*held, spectral_master, spectral_momentum, pointwise_master, pointwise_momentum)
    return tuple(results)


def solution(mesh):
    return jax.shard_map(
        per_device,
        mesh=mesh,
        in_specs=(
            P("batch", "row", None, None),
            P("batch", "row", None, None),
            P("batch"),
            P(),
            P(),
            P(("batch", "row"), None, None),
            P(("batch", "row"), None, None),
            P(),
            P(),
        ),
        out_specs=(
            P("batch", "row", None, None),
            P("batch", "row", None, None),
            P(("batch", "row"), None, None),
            P(("batch", "row"), None, None),
            P(("batch", "row"), None, None),
            P(("batch", "row"), None, None),
            P(),
            P(),
            P(),
            P(),
        ),
        check_vma=False,
    )
```

```python
import functools
import math

import jax
import jax.numpy as jnp
import ml_dtypes
import numpy as np
from jax import lax
from jax.experimental import pallas as pl
from jax.experimental.pallas import tpu as pltpu
from jax.sharding import PartitionSpec as P

ROW_MODES = 16
COLUMN_MODES = 16

BLADE_SIGNS = np.array([[1, 1, 1, 1], [1, 1, 1, 1], [1, -1, 1, -1], [1, -1, 1, -1]], np.float32)
QUINTIC_FIRST = 3.4445
QUINTIC_SECOND = -4.775
QUINTIC_THIRD = 2.0315
SPECTRAL_RATE = 4.0
POINTWISE_RATE = 0.8
MOMENTUM_DECAY = 0.5
MESH = pl.DeviceIdType.MESH
F32 = jnp.float32
BF16 = jnp.bfloat16
GELU_A = math.sqrt(2.0 / math.pi)
GELU_B = GELU_A * 0.044715


MATRIX_SIGNS = np.zeros((2, 2, 4), np.float32)
MATRIX_SIGNS[0, 0, 0] = MATRIX_SIGNS[0, 0, 1] = MATRIX_SIGNS[1, 1, 0] = 1.0
MATRIX_SIGNS[1, 1, 1] = MATRIX_SIGNS[1, 0, 3] = -1.0
MATRIX_SIGNS[0, 1, 2] = MATRIX_SIGNS[0, 1, 3] = MATRIX_SIGNS[1, 0, 2] = 1.0


def column_block(grid_size, row_count):
    angles = 2.0 * np.pi / grid_size * (np.arange(COLUMN_MODES)[:, None] * np.arange(grid_size)[None] % grid_size)
    table = np.stack([np.cos(angles), -np.sin(angles)], 0).reshape(2, row_count, -1, grid_size)
    full = np.einsum("pclw,hg->chplgw", table, np.eye(2))
    return full.reshape(4 * COLUMN_MODES, 2 * grid_size).astype(ml_dtypes.bfloat16)


def row_blocks(grid_size, row_count):
    rows = grid_size // row_count
    local = COLUMN_MODES // row_count
    r = np.arange(ROW_MODES)
    frequency = np.where(r < ROW_MODES // 2, r, grid_size - ROW_MODES + r)
    angles = 2.0 * np.pi / grid_size * (frequency[:, None] * np.arange(grid_size)[None] % grid_size)
    cosine, sine = np.cos(angles), np.sin(angles)
    table = np.stack([np.stack([cosine, sine], -1), np.stack([-sine, cosine], -1)], 0)
    table = table.reshape(2, ROW_MODES, row_count, rows, 2)
    full = np.einsum("qrzhp,cd->zqrchpd", table, np.eye(local))
    return full.reshape(row_count, 2 * ROW_MODES * local, rows * 2 * local).astype(ml_dtypes.bfloat16)


def lanes_of_columns(channels):
    half = 4 * channels
    place = np.arange(2 * half)
    cut = half // 128 * 128
    first = np.arange(half)
    second = np.where(first < cut, half + (half - cut) + first, half + first - cut)
    return place[first], place[second]


def product_signs(channels):
    unit = np.eye(channels, dtype=np.float32)
    psi = np.zeros((2, 2, 2, 4, 2, 2), np.float32)
    for q in range(2):
        for p in range(2):
            part = -1.0 if (q == 0 and p == 1) else 1.0
            for row in range(2):
                for inner in range(2):
                    psi[q, row, p ^ q, :, p, inner] = part * MATRIX_SIGNS[row, inner]
    psi = np.einsum("qrwapn,ij->qrwaipnj", psi, unit).reshape(4, 8 * channels, 4 * channels)
    psi = np.pad(psi, ((0, 0), (0, 0), (0, 256 - 4 * channels)))
    spread = np.einsum("pt,ncb,ij->pbictnj", np.eye(2), MATRIX_SIGNS, unit)
    spread = spread.reshape(8 * channels, 2, 4 * channels)
    turn = np.zeros((8 * channels, 8 * channels), np.float32)
    for col, lanes in enumerate(lanes_of_columns(channels)):
        turn[:, lanes] = spread[:, col]
    point = np.zeros((4, 4, 4), np.float32)
    for k in range(4):
        for b in range(4):
            point[k, k ^ b, b] = BLADE_SIGNS[k ^ b, b]
    point = np.einsum("kab,ij->kaibj", point, unit).reshape(4, 4 * channels, 4 * channels)
    point = np.pad(point, ((0, 0), (0, 0), (0, 256 - 4 * channels)))
    return (one.astype(ml_dtypes.bfloat16) for one in (psi, turn, point))


def dot(a, b):
    return lax.dot_general(a, b, (((1,), (0,)), ((), ())), preferred_element_type=F32)


def dot_nt(a, b):
    return lax.dot_general(a, b, (((1,), (1,)), ((), ())), preferred_element_type=F32)


def layer_kernel(
    sizes,
    x_hbm, ct_hbm, scale_ref, table_ref, owner_ref, single_hbm, psi_hbm, master_hbm, momentum_hbm,
    turn_ref, sign_ref, cblk_ref, eye_ref, point_ref, point_momentum_ref,
    ob, xb, dw_ref, pg_ref, turned_ref, point_turned_ref,
    eb, single, psi, master_ref, momentum_ref, wm, cols, l2, kt1, ktb, kk1, kkb, acc, gk_ref, pa, pz,
    lows, highs, perm_ref, back_ref,
    pb1, rb1, gb1, pb2, rb2, gb2,
    xs, xr, ps, pr, gs, gr, hs, hr,
    x_sem, ct_sem, ld_sem, ei_sem, pa_s, pa_r, pz_s, pz_r,
    rs1_s, rs1_r, rs2_s, rs2_r, ag1_s, ag1_r, ag2_s, ag2_r, a2a_s, a2a_r,
):
    nb, nz, S, H, K, W, slots, M = sizes
    wide = 2 * K
    channels = K // 4
    pairs = H // 2
    me = lax.axis_index("batch")
    z = lax.axis_index("row")
    last = nz - 1

    loads = [
        pltpu.make_async_copy(psi_hbm, psi, ld_sem.at[0]),
        pltpu.make_async_copy(single_hbm.at[z], single, ld_sem.at[1]),
        pltpu.make_async_copy(master_hbm, master_ref, ld_sem.at[2]),
        pltpu.make_async_copy(momentum_hbm, momentum_ref, ld_sem.at[3]),
    ]
    x_copy = lambda s: pltpu.make_async_copy(x_hbm.at[s], xb.at[s], x_sem.at[s])
    ct_copy = lambda s: pltpu.make_async_copy(ct_hbm.at[s], ob.at[s], ct_sem.at[s])
    ect_copy = lambda s: pltpu.make_async_copy(ct_hbm.at[s], eb.at[lax.rem(s, 2)], ei_sem.at[lax.rem(s, 2)])

    barrier = pltpu.get_barrier_semaphore()

    def greet(d, carry):
        peer = lax.rem(me + d, nb)
        pl.semaphore_signal(barrier, inc=1, device_id=(peer, z), device_id_type=MESH)
        return carry

    lax.fori_loop(1, nb, greet, 0)

    def greet_z(d, carry):
        pl.semaphore_signal(barrier, inc=1, device_id=(me, lax.rem(z + d, nz)), device_id_type=MESH)
        return carry

    lax.fori_loop(1, nz, greet_z, 0)
    x_copy(0).start()
    loads[1].start()
    x_copy(1).start()
    loads[0].start()
    loads[2].start()
    x_copy(2).start()
    loads[3].start()
    cols[...] = jnp.zeros_like(cols)
    gk_ref[...] = jnp.zeros_like(gk_ref)

    def place_modes():
        local = COLUMN_MODES // nz
        lane = lax.broadcasted_iota(jnp.int32, (1, 2 * M), 1)

        def place(d, carry):
            for i in range(slots):
                mode = owner_ref[(d * nz + z) * slots + i]
                at = lax.div(mode, COLUMN_MODES) * local + lax.rem(mode, local)
                lows[pl.ds(d * slots + i, 1), :] = jnp.where(lane == at, 1.0, 0.0)
                highs[pl.ds(d * slots + i, 1), :] = jnp.where(lane == at + M, 1.0, 0.0)
            return carry

        lax.fori_loop(0, nb, place, 0)
        inner = 1.0 / (H * nz * H * nz)
        weigh = jnp.where(z * local + lax.rem(lane, local) == 0, 0.5 * inner, inner)
        for table, pick in enumerate((lambda v: v[...], lambda v: v[...] * weigh)):
            perm_ref[table] = pick(lows)[:, 0:M].astype(BF16)
            back_ref[1 - table, 0] = pick(lows).astype(BF16)
            back_ref[1 - table, 1] = pick(highs).astype(BF16)

    def point_kernels():
        weight = point_ref[...].astype(BF16)
        kernel_t = jnp.concatenate([dot(weight, sign_ref[k]) for k in range(4)], axis=0)
        kt1[...] = kernel_t[:, 0:128].astype(BF16)
        for turn in range(8):
            ktb[turn] = pltpu.roll(kernel_t[:, 128:256], (64 + 16 * turn) % 128, 1)
        padded = jnp.concatenate([kernel_t.astype(BF16), jnp.zeros((256 - K, 256), BF16)], axis=0)
        kernel_n = dot_nt(eye_ref[0:K], padded)
        kk1[...] = kernel_n[:, 0:128].astype(BF16)
        for turn in range(8):
            kkb[turn] = pltpu.roll(kernel_n[:, 128:256], (64 + 16 * turn) % 128, 1)

    def expand_weights():
        loads[0].wait()
        loads[2].wait()
        wm[...] = jnp.zeros_like(wm)
        masters = master_ref[...].reshape(slots * channels, wide).astype(BF16)
        for part in range(4):
            block = dot(masters, psi[part]).astype(BF16)
            for i in range(slots):
                wm[i, part * channels : (part + 1) * channels, :] = block[i * channels : (i + 1) * channels]

    pieces = 4

    def rs_copy(s, up, c, pb, rb, ssem, rsem, piece=None):
        way = 0 if up else 1
        rows = slice(None) if piece is None else pl.ds(piece * (M // pieces), M // pieces)
        return pltpu.make_async_remote_copy(
            src_ref=pb.at[s, c, rows], dst_ref=rb.at[s, way, c, rows],
            send_sem=ssem.at[s, way, c], recv_sem=rsem.at[s, way, c],
            device_id=(me, z + 1 if up else z - 1), device_id_type=MESH,
        )

    def rs_hop(j, s, bufs, finish=False):
        pb, rb = bufs[0], bufs[1]
        for up in (True, False):
            place = z if up else last - z
            c = (last - j + z) if up else (z - (last - j))

            @pl.when(place <= j)
            def _():
                copy = rs_copy(s, up, c, *bufs)
                if finish:
                    copy.wait_send()
                else:
                    @pl.when(place > 0)
                    def _():
                        way = 0 if up else 1
                        copy.wait_recv()
                        pb[s, c] = (pb[s, c].astype(F32) + rb[s, way, c].astype(F32)).astype(BF16)

                    for piece in range(pieces):
                        rs_copy(s, up, c, *bufs, piece).start()

    def rs_final(s, bufs):
        pb, rb = bufs[0], bufs[1]
        acc[...] = pb[s, z].astype(F32)

        @pl.when(z > 0)
        def _():
            rs_copy(s, True, z, *bufs).wait_recv()
            acc[...] += rb[s, 0, z].astype(F32)

        @pl.when(z < last)
        def _():
            rs_copy(s, False, z, *bufs).wait_recv()
            acc[...] += rb[s, 1, z].astype(F32)

        return acc[...].astype(BF16)

    def ag_copy(s, up, c, gb, ssem, rsem, piece=None):
        way = 0 if up else 1
        rows = slice(None) if piece is None else pl.ds(piece * (K // pieces), K // pieces)
        return pltpu.make_async_remote_copy(
            src_ref=gb.at[s, c, rows], dst_ref=gb.at[s, c, rows],
            send_sem=ssem.at[s, way, c], recv_sem=rsem.at[s, c],
            device_id=(me, z + 1 if up else z - 1), device_id_type=MESH,
        )

    def ag_hop(j, s, bufs, finish=False):
        for up in (True, False):
            c = z - j if up else z + j
            more = z < last if up else z > 0

            @pl.when((c >= 0) if up else (c <= last))
            def _():
                copy = ag_copy(s, up, c, *bufs)
                if j > 0 and not finish:
                    copy.wait_recv()

                if j < last:
                    @pl.when(more)
                    def _():
                        if finish:
                            copy.wait_send()
                        else:
                            for piece in range(pieces):
                                ag_copy(s, up, c, *bufs, piece).start()

    tiled = slots % 8 == 0

    def block_of(ref, s, d):
        if tiled:
            return ref.at[s, :, pl.ds(pl.multiple_of(d * slots, slots), slots)]
        return ref.at[s, d]

    def blocks_of(ref, s):
        if tiled:
            return ref.at[s, :, pl.ds(0, (nb - 1) * slots)]
        return ref.at[s, pl.ds(0, nb - 1)]

    def whole_of(ref, s):
        if tiled:
            return jnp.concatenate([ref[s, g] for g in range(wide // 128)], axis=1)
        return ref[s].reshape(nb * slots, wide)

    def put_whole(ref, s, value):
        if tiled:
            for g in range(wide // 128):
                ref[s, g] = value[:, g * 128 : (g + 1) * 128]
        else:
            ref[s] = value.reshape(nb, slots, wide)

    def slot_rows(ref, s, i):
        if tiled:
            return jnp.concatenate([ref[s, g, pl.ds(i, nb, stride=slots), :] for g in range(wide // 128)], axis=1)
        return ref[s, :, i, :]

    def put_slot_rows(ref, s, i, value):
        if tiled:
            for g in range(wide // 128):
                ref[s, g, pl.ds(i, nb, stride=slots), :] = value[:, g * 128 : (g + 1) * 128]
        else:
            ref[s, :, i, :] = value

    def exchange(s, src, dst, which):
        def send(d, carry):
            peer = lax.rem(me + d, nb)
            pltpu.make_async_remote_copy(
                src_ref=block_of(src, s, peer), dst_ref=block_of(dst, s, me),
                send_sem=a2a_s.at[which, s], recv_sem=a2a_r.at[which, s],
                device_id=(peer, z), device_id_type=MESH,
            ).start()
            return carry

        lax.fori_loop(1, nb, send, 0)
        block_of(dst, s, me)[...] = block_of(src, s, me)[...]

    def exchanged(s, src, dst, which):
        return pltpu.make_async_remote_copy(
            src_ref=blocks_of(src, s), dst_ref=blocks_of(dst, s),
            send_sem=a2a_s.at[which, s], recv_sem=a2a_r.at[which, s],
            device_id=(lax.rem(me + 1, nb), z), device_id_type=MESH,
        )

    def forward_rows(s, pb):
        for c in range(nz):
            part = dot(single[...], cols[c])
            first = part[0:M]
            second = pltpu.roll(part[M:], 64, 1)
            pb[s, c, :, 0:128] = first[:, 0:128].astype(BF16)
            pb[s, c, :, 128:256] = (first[:, 128:256] + second[:, 0:128]).astype(BF16)
            pb[s, c, :, 256:384] = second[:, 128:256].astype(BF16)

    def put_columns(p, value):
        step = 4 * COLUMN_MODES // nz
        for c in range(nz):
            cols[c, pl.ds(pl.multiple_of(p * step, step), step), 0:K] = value[c * step : (c + 1) * step]

    def pair_of(ref, s, p):
        return jnp.concatenate([ref[s, 2 * p], ref[s, 2 * p + 1]], axis=1)

    def stage_a(s):
        x_copy(s).wait()

        def some(blk, carry):
            for u in range(8):
                p = blk * 8 + u
                part = dot_nt(cblk_ref[...], pair_of(xb, s, p))
                put_columns(p, part.astype(BF16))
            return carry

        lax.fori_loop(0, pairs // 8, some, 0)
        forward_rows(s, pb1)
        rs_hop(0, s, rs1)

    def by_column(ref, s, i):
        rows = slot_rows(ref, s, i)
        low, mid, top = rows[:, 0:128], rows[:, 128:256], rows[:, 256:384]
        first = jnp.concatenate([low, mid], axis=1)
        second = jnp.concatenate([top, pltpu.roll(mid, 64, 1)], axis=1)
        return jnp.concatenate([first, second], axis=0).astype(BF16)

    def put_by_column(ref, s, i, value):
        first, second = value[0:nb], value[nb:]
        mid = first[:, 128:256] + pltpu.roll(second[:, 128:256], 64, 1)
        put_slot_rows(ref, s, i, jnp.concatenate([first[:, 0:128], mid, second[:, 0:128]], axis=1))

    def stage_b(s):
        exchanged(s, xs, xr, 0).wait_recv()
        for i in range(slots):
            put_by_column(ps, s, i, dot_nt(by_column(xr, s, i), wm[i]))
        exchange(s, ps, pr, 1)

    def stage_d(s):
        exchanged(s, gs, gr, 2).wait_recv()
        for i in range(slots):
            put_by_column(hs, s, i, dot(by_column(gr, s, i), wm[i]))
        exchange(s, hs, hr, 3)

    def stage_f(s, bufs, table, src, dst, which):
        placed = dot(perm_ref[table], rs_final(s, bufs)).astype(BF16)
        put_whole(src, s, dot(placed, turn_ref[...]))
        exchange(s, src, dst, which)

    def stage_u(s, bufs, table, src, dst, which):
        exchanged(s, src, dst, which).wait_recv()
        turned = jnp.transpose(whole_of(dst, s))
        cut = K // 128 * 128
        first = turned[0:K]
        second = jnp.concatenate([turned[2 * K - cut :], turned[K : 2 * K - cut]], axis=0)
        parts = []
        for q in range(2):
            base = 2 * q * channels
            at = lambda col, row: col[base + row * channels : base + (row + 1) * channels]
            m00, m10, m01, m11 = at(first, 0), at(first, 1), at(second, 0), at(second, 1)
            parts.append(jnp.concatenate([m00 + m11, m00 - m11, m01 + m10, m01 - m10], axis=0).astype(BF16))
        both = dot(parts[0], back_ref[table, 0]) + dot(parts[1], back_ref[table, 1])
        bufs[0][s, z] = both.astype(BF16)
        ag_hop(0, s, bufs)

    def inverse_rows(s, gb, base):
        spread = dot(gb[s].reshape(nz * K, 2 * M), single[...])
        group = lax.broadcasted_iota(jnp.int32, (K, 128), 1) // 16
        for col in range(pairs // 8):
            cut = slice(col * 128, col * 128 + 128)
            parts = [spread[c * K : (c + 1) * K, cut] for c in range(nz)]
            parts = [parts[0]] + [pltpu.roll(parts[c], 16 * c, 1) for c in range(1, nz)]
            for first in range(4):
                which = (group + (8 - first)) % 4
                mixed = jnp.where(which == 0, parts[0], jnp.where(which == 1, parts[1], jnp.where(which == 2, parts[2], parts[3])))
                for turn in (first, first + 4):
                    inside = (group + (8 - turn)) % 8 < 4
                    l2[col * 8 + turn] = jnp.where(inside, mixed, base[turn]).astype(BF16)

    def with_columns(x2, turn):
        rows = [x2[0:128]]
        for g in range(8):
            i = (g - turn) % 8
            rows.append(cblk_ref[16 * i : 16 * i + 16, :] if i < 4 else x2[64 + 16 * i : 80 + 16 * i])
        return jnp.concatenate(rows, axis=0)

    def stage_c(s):
        ag_hop(last, s, ag1)
        inverse_rows(s, gb1, ktb)
        ct_copy(s).wait()
        f = table_ref[scale_ref[s]]

        def some(blk, carry):
            for u in range(8):
                p = blk * 8 + u
                x2 = pair_of(xb, s, p)
                both = with_columns(x2, u)
                half = (0.5 * f) * dot(jnp.concatenate([kt1[...], l2[p]], axis=1), both)
                square = half * half
                rise = 1.0 + jnp.tanh(half * (2.0 * GELU_A + 8.0 * GELU_B * square))
                y = (x2.astype(F32) + half * rise).astype(BF16)
                slope = rise + (rise * (2.0 - rise)) * (half * (2.0 * GELU_A + 24.0 * GELU_B * square))
                c2 = pair_of(ob, s, p).astype(F32)
                g2 = (((0.5 * f) * c2) * slope).astype(BF16)
                for e in range(2):
                    ob[s, 2 * p + e] = y[:, e * W : (e + 1) * W]
                    xb[s, 2 * p + e] = g2[:, e * W : (e + 1) * W]
                back = dot_nt(both, g2)
                gk_ref[0:128] += back[0:128]
                for g in range(8):
                    i = (g - u) % 8
                    piece = back[128 + 16 * g : 144 + 16 * g]
                    if i < 4:
                        cols[i, pl.ds(pl.multiple_of(p * 16, 16), 16), 0:K] = piece.astype(BF16)
                    else:
                        gk_ref[64 + 16 * i : 80 + 16 * i] += piece
            return carry

        lax.fori_loop(0, pairs // 8, some, 0)
        forward_rows(s, pb2)
        rs_hop(0, s, rs2)

    def stage_e(s):
        slot = lax.rem(s, 2)

        @pl.when(s + 1 < S)
        def _():
            ect_copy(s + 1).start()

        ag_hop(last, s, ag2)
        inverse_rows(s, gb2, kkb)
        ect_copy(s).wait()

        def some(blk, carry):
            for u in range(8):
                p = blk * 8 + u
                both = with_columns(pair_of(xb, s, p), u)
                y = dot(jnp.concatenate([kk1[...], l2[p]], axis=1), both)
                y = (y + pair_of(eb, slot, p).astype(F32)).astype(BF16)
                for e in range(2):
                    xb[s, 2 * p + e] = y[:, e * W : (e + 1) * W]
            return carry

        lax.fori_loop(0, pairs // 8, some, 0)

    def pa_copy(peer):
        return pltpu.make_async_remote_copy(
            src_ref=pa.at[me], dst_ref=pa.at[me], send_sem=pa_s.at[0], recv_sem=pa_r.at[0],
            device_id=(peer, z), device_id_type=MESH,
        )

    def pz_copy(peer):
        return pltpu.make_async_remote_copy(
            src_ref=pz.at[z], dst_ref=pz.at[z], send_sem=pz_s.at[0], recv_sem=pz_r.at[0],
            device_id=(me, peer), device_id_type=MESH,
        )

    def all_but_one(ref, count, ssem, rsem, device):
        rest = ref.at[pl.ds(0, count - 1)]
        return pltpu.make_async_remote_copy(
            src_ref=rest, dst_ref=rest, send_sem=ssem.at[0], recv_sem=rsem.at[0],
            device_id=device, device_id_type=MESH,
        )

    def point_first():
        left = gk_ref[...]
        total = jnp.zeros((channels, K), F32)
        for part in range(3):
            term = left.astype(BF16)
            left = left - term.astype(F32)
            turned = dot_nt(eye_ref[0:K, 0:K], term).astype(BF16)
            for k in range(4):
                total += dot_nt(turned[k * channels : (k + 1) * channels], sign_ref[k, :, 0:K])
        pa[me] = total

        def send(d, carry):
            pa_copy(lax.rem(me + d, nb)).start()
            return carry

        lax.fori_loop(1, nb, send, 0)

    def point_second():
        all_but_one(pa, nb, pa_s, pa_r, (lax.rem(me + 1, nb), z)).wait_recv()
        pz[z] = jnp.sum(pa[...], axis=0)

        def send(d, carry):
            pz_copy(lax.rem(z + d, nz)).start()
            return carry

        lax.fori_loop(1, nz, send, 0)

    def slot_gradients():
        loads[3].wait()
        for i in range(slots):
            g_all = jnp.concatenate([by_column(gr, s, i) for s in range(S)], axis=0)
            x_all = jnp.concatenate([by_column(xr, s, i) for s in range(S)], axis=0)
            g_turned = dot_nt(eye_ref[...], g_all).astype(BF16)
            wm[i] = dot(g_turned, x_all).astype(BF16)

        total = jnp.zeros((slots * channels, wide), F32)
        for part in range(4):
            rows = slice(part * channels, (part + 1) * channels)
            block = jnp.concatenate([wm[i, rows, :] for i in range(slots)], axis=0)
            total += dot_nt(block, psi[part])
        dw_ref[...] = total.reshape(slots, channels, wide)

    def orthogonal(moments):
        def split(v):
            high = v.astype(BF16)
            return high, (v - high.astype(F32)).astype(BF16)

        def product(a, b, mul):
            (ah, al), (bh, bl) = a, b
            return mul(ah, bh) + (mul(ah, bl) + mul(al, bh))

        current = [m / (jnp.sqrt(jnp.sum(m * m)) + 1e-07) for m in moments]
        for repeat in range(5):
            parts = [split(v) for v in current]
            grams = [product(v, v, dot_nt) for v in parts]
            gram_parts = [split(v) for v in grams]
            squares = [product(v, v, dot) for v in gram_parts]
            polynomials = [split(QUINTIC_SECOND * g + QUINTIC_THIRD * q) for g, q in zip(grams, squares)]
            current = [
                QUINTIC_FIRST * v + product(p, w, dot) for v, p, w in zip(current, polynomials, parts)
            ]
        return current

    def slot_updates(chosen):
        moments = [MOMENTUM_DECAY * momentum_ref[i] + dw_ref[i] for i in chosen]
        for i, value in zip(chosen, orthogonal(moments)):
            turned_ref[i] = value

    def point_update():
        all_but_one(pz, nz, pz_s, pz_r, (me, lax.rem(z + 1, nz))).wait_recv()
        total = jnp.sum(pz[...], axis=0)
        pg_ref[...] = total
        (point_turned_ref[...],) = orthogonal([MOMENTUM_DECAY * point_momentum_ref[...] + total])

    rs1 = (pb1, rb1, rs1_s, rs1_r)
    rs2 = (pb2, rb2, rs2_s, rs2_r)
    ag1 = (gb1, ag1_s, ag1_r)
    ag2 = (gb2, ag2_s, ag2_r)

    schedule = [
        (0, stage_a),
        (3, lambda s: stage_f(s, rs1, 0, xs, xr, 0)),
        (11, lambda s: stage_f(s, rs2, 1, gs, gr, 2)),
        (2, lambda s: rs_hop(2, s, rs1)),
        (10, lambda s: rs_hop(2, s, rs2)),
        (1, lambda s: rs_hop(1, s, rs1)),
        (9, lambda s: rs_hop(1, s, rs2)),
        (7, lambda s: ag_hop(2, s, ag1)),
        (15, lambda s: ag_hop(2, s, ag2)),
        (6, lambda s: ag_hop(1, s, ag1)),
        (14, lambda s: ag_hop(1, s, ag2)),
        (5, lambda s: stage_u(s, ag1, 0, ps, pr, 1)),
        (13, lambda s: stage_u(s, ag2, 1, hs, hr, 3)),
        (4, stage_b),
        (12, stage_d),
        (8, stage_c),
        (16, stage_e),
    ]
    steps = S + max(lag for lag, _ in schedule)
    at_step = {0: place_modes, 1: expand_weights, 2: point_kernels, S + 8: point_first, S + 9: point_second, S + 11: point_update, S + 12: slot_gradients}
    groups = [range(slots)[: slots // 2], range(slots)[slots // 2 :]]
    for step, group in enumerate(groups):
        if group:
            at_step[S + 13 + step] = functools.partial(slot_updates, group)

    pl.semaphore_wait(barrier, nb + nz - 2)

    loads[1].wait()

    def iteration(t, carry):
        pl.when(t + 3 < S)(lambda: x_copy(t + 3).start())
        pl.when((t >= 5) & (t < S + 5))(lambda: ct_copy(t - 5).start())
        pl.when(t == 14)(lambda: ect_copy(0).start())
        for lag, stage in schedule:
            s = t - lag
            pl.when((s >= 0) & (s < S))(functools.partial(stage, s))
        for step, work in at_step.items():
            pl.when(t == step)(work)
        return carry

    lax.fori_loop(0, steps, iteration, 0)

    def finish(s, carry):
        for j in range(last):
            rs_hop(j, s, rs1, True)
            rs_hop(j, s, rs2, True)
            ag_hop(j, s, ag1, True)
            ag_hop(j, s, ag2, True)
        for which, (src, dst) in enumerate(((xs, xr), (ps, pr), (gs, gr), (hs, hr))):
            exchanged(s, src, dst, which).wait_send()
        return carry

    lax.fori_loop(0, S, finish, 0)
    all_but_one(pa, nb, pa_s, pa_r, (lax.rem(me + 1, nb), z)).wait_send()
    all_but_one(pz, nz, pz_s, pz_r, (me, lax.rem(z + 1, nz))).wait_send()


def store_kernel(
    ob, xb, dw_ref, pg_ref, turned_ref, point_turned_ref, master_ref, momentum_ref, point_ref, point_momentum_ref,
    out_hbm, ig_hbm, grad_ref, moment_ref, weight_ref, low_ref,
    point_grad_ref, point_moment_ref, point_weight_ref, point_low_ref, sem,
):
    S = ob.shape[0]
    copies = []
    for s in range(S):
        copies.append(pltpu.make_async_copy(ob.at[s], out_hbm.at[s], sem.at[0, s]))
        copies.append(pltpu.make_async_copy(xb.at[s], ig_hbm.at[s], sem.at[1, s]))
    for copy in copies:
        copy.start()
    point_grad_ref[...] = pg_ref[...]
    point_moment_ref[...] = MOMENTUM_DECAY * point_momentum_ref[...] + pg_ref[...]
    point_weight = point_ref[...] - POINTWISE_RATE * point_turned_ref[...]
    point_weight_ref[...] = point_weight
    point_low_ref[...] = point_weight.astype(BF16)
    grad_ref[...] = dw_ref[...]
    moment_ref[...] = MOMENTUM_DECAY * momentum_ref[...] + dw_ref[...]
    weight = master_ref[...] - SPECTRAL_RATE * turned_ref[...]
    weight_ref[...] = weight
    low_ref[...] = weight.astype(BF16)
    for copy in copies:
        copy.wait()


def per_device(
    input_field,
    cotangent,
    sample_scale,
    scale_table,
    owner_map,
    spectral_master,
    spectral_momentum,
    pointwise_master,
    pointwise_momentum,
):
    S, H, K, W = input_field.shape
    nz = lax.axis_size("row")
    nb = lax.axis_size("batch")
    slots = spectral_master.shape[0]
    channels = K // 4
    wide = 2 * K
    local_columns = COLUMN_MODES // nz
    M = ROW_MODES * local_columns
    grid = H * nz

    anywhere = pl.BlockSpec(memory_space=pltpu.HBM)
    smem = pl.BlockSpec(memory_space=pltpu.SMEM)
    vmem = pl.BlockSpec(memory_space=pltpu.VMEM)
    exchange_shape = (S, wide // 128, nb * slots, 128) if slots % 8 == 0 else (S, nb, slots, wide)
    dma = pltpu.SemaphoreType.DMA
    single = jnp.asarray(row_blocks(grid, nz))
    psi, turn, signs = (jnp.asarray(one) for one in product_signs(channels))
    column_rows = jnp.asarray(column_block(W, nz))
    unit = jnp.asarray(np.eye(256).astype(ml_dtypes.bfloat16))
    slot_shape, point_shape = spectral_master.shape, pointwise_master.shape
    kept = pl.pallas_call(
        functools.partial(layer_kernel, (nb, nz, S, H, K, W, slots, M)),
        out_shape=(
            pltpu.VMEM(input_field.shape, BF16),
            pltpu.VMEM(input_field.shape, BF16),
            pltpu.VMEM(slot_shape, F32),
            pltpu.VMEM(point_shape, F32),
            pltpu.VMEM(slot_shape, F32),
            pltpu.VMEM(point_shape, F32),
        ),
        in_specs=[anywhere, anywhere, smem, smem, smem] + [anywhere] * 4 + [vmem] * 6,
        out_specs=(vmem,) * 6,
        scratch_shapes=[
            pltpu.VMEM((2, H, K, W), BF16),
            pltpu.VMEM(single.shape[1:], BF16),
            pltpu.VMEM(psi.shape, BF16),
            pltpu.VMEM(spectral_master.shape, F32),
            pltpu.VMEM(spectral_master.shape, F32),
            pltpu.VMEM((slots, 256, 256), BF16),
            pltpu.VMEM((nz, single.shape[2], 256), BF16),
            pltpu.VMEM((H // 2, K, 128), BF16),
            pltpu.VMEM((K, 128), BF16),
            pltpu.VMEM((8, K, 128), F32),
            pltpu.VMEM((K, 128), BF16),
            pltpu.VMEM((8, K, 128), F32),
            pltpu.VMEM((M, wide), F32),
            pltpu.VMEM((K, K), F32),
            pltpu.VMEM((nb, channels, K), F32),
            pltpu.VMEM((nz, channels, K), F32),
            pltpu.VMEM((M, 2 * M), F32),
            pltpu.VMEM((M, 2 * M), F32),
            pltpu.VMEM((2, M, M), BF16),
            pltpu.VMEM((2, 2, M, 2 * M), BF16),
            pltpu.VMEM((S, nz, M, wide), BF16),
            pltpu.VMEM((S, 2, nz, M, wide), BF16),
            pltpu.VMEM((S, nz, K, 2 * M), BF16),
            pltpu.VMEM((S, nz, M, wide), BF16),
            pltpu.VMEM((S, 2, nz, M, wide), BF16),
            pltpu.VMEM((S, nz, K, 2 * M), BF16),
        ]
        + [pltpu.VMEM(exchange_shape, F32)] * 8
        + [dma((S,)), dma((S,)), dma((4,)), dma((2,))]
        + [dma((1,))] * 4
        + [dma((S, 2, nz))] * 4
        + [dma((S, 2, nz)), dma((S, nz))] * 2
        + [dma((4, S))] * 2,
        compiler_params=pltpu.CompilerParams(
            collective_id=0, has_side_effects=True, vmem_limit_bytes=37 * 1024 * 1024
        ),
    )(
        input_field, cotangent, sample_scale, scale_table, owner_map, single, psi,
        spectral_master, spectral_momentum, turn, signs, column_rows, unit, pointwise_master, pointwise_momentum,
    )

    held = [pltpu.with_memory_space_constraint(one, pltpu.VMEM) for one in kept]
    input_shape = jax.ShapeDtypeStruct(input_field.shape, BF16)
    results = pl.pallas_call(
        store_kernel,
        out_shape=(
            input_shape,
            input_shape,
            jax.ShapeDtypeStruct(slot_shape, F32),
            jax.ShapeDtypeStruct(slot_shape, F32),
            jax.ShapeDtypeStruct(slot_shape, F32),
            jax.ShapeDtypeStruct(slot_shape, BF16),
            jax.ShapeDtypeStruct(point_shape, F32),
            jax.ShapeDtypeStruct(point_shape, F32),
            jax.ShapeDtypeStruct(point_shape, F32),
            jax.ShapeDtypeStruct(point_shape, BF16),
        ),
        in_specs=[vmem] * 10,
        out_specs=(anywhere, anywhere) + (vmem,) * 8,
        scratch_shapes=[dma((2, S))],
        compiler_params=pltpu.CompilerParams(vmem_limit_bytes=6 * 1024 * 1024),
    )(*held, spectral_master, spectral_momentum, pointwise_master, pointwise_momentum)
    return tuple(results)


def solution(mesh):
    return jax.shard_map(
        per_device,
        mesh=mesh,
        in_specs=(
            P("batch", "row", None, None),
            P("batch", "row", None, None),
            P("batch"),
            P(),
            P(),
            P(("batch", "row"), None, None),
            P(("batch", "row"), None, None),
            P(),
            P(),
        ),
        out_specs=(
            P("batch", "row", None, None),
            P("batch", "row", None, None),
            P(("batch", "row"), None, None),
            P(("batch", "row"), None, None),
            P(("batch", "row"), None, None),
            P(("batch", "row"), None, None),
            P(),
            P(),
            P(),
            P(),
        ),
        check_vma=False,
    )
```

```python
import functools
import math

import jax
import jax.numpy as jnp
import ml_dtypes
import numpy as np
from jax import lax
from jax.experimental import pallas as pl
from jax.experimental.pallas import tpu as pltpu
from jax.sharding import PartitionSpec as P

ROW_MODES = 16
COLUMN_MODES = 16

BLADE_SIGNS = np.array([[1, 1, 1, 1], [1, 1, 1, 1], [1, -1, 1, -1], [1, -1, 1, -1]], np.float32)
QUINTIC_FIRST = 3.4445
QUINTIC_SECOND = -4.775
QUINTIC_THIRD = 2.0315
SPECTRAL_RATE = 4.0
POINTWISE_RATE = 0.8
MOMENTUM_DECAY = 0.5
MESH = pl.DeviceIdType.MESH
F32 = jnp.float32
BF16 = jnp.bfloat16
GELU_A = math.sqrt(2.0 / math.pi)
GELU_B = GELU_A * 0.044715


MATRIX_SIGNS = np.zeros((2, 2, 4), np.float32)
MATRIX_SIGNS[0, 0, 0] = MATRIX_SIGNS[0, 0, 1] = MATRIX_SIGNS[1, 1, 0] = 1.0
MATRIX_SIGNS[1, 1, 1] = MATRIX_SIGNS[1, 0, 3] = -1.0
MATRIX_SIGNS[0, 1, 2] = MATRIX_SIGNS[0, 1, 3] = MATRIX_SIGNS[1, 0, 2] = 1.0


def column_block(grid_size, row_count):
    angles = 2.0 * np.pi / grid_size * (np.arange(COLUMN_MODES)[:, None] * np.arange(grid_size)[None] % grid_size)
    table = np.stack([np.cos(angles), -np.sin(angles)], 0).reshape(2, row_count, -1, grid_size)
    full = np.einsum("pclw,hg->chplgw", table, np.eye(2))
    return full.reshape(4 * COLUMN_MODES, 2 * grid_size).astype(ml_dtypes.bfloat16)


def row_blocks(grid_size, row_count):
    rows = grid_size // row_count
    local = COLUMN_MODES // row_count
    r = np.arange(ROW_MODES)
    frequency = np.where(r < ROW_MODES // 2, r, grid_size - ROW_MODES + r)
    angles = 2.0 * np.pi / grid_size * (frequency[:, None] * np.arange(grid_size)[None] % grid_size)
    cosine, sine = np.cos(angles), np.sin(angles)
    table = np.stack([np.stack([cosine, sine], -1), np.stack([-sine, cosine], -1)], 0)
    table = table.reshape(2, ROW_MODES, row_count, rows, 2)
    full = np.einsum("qrzhp,cd->zqrchpd", table, np.eye(local))
    return full.reshape(row_count, 2 * ROW_MODES * local, rows * 2 * local).astype(ml_dtypes.bfloat16)


def lanes_of_columns(channels):
    half = 4 * channels
    place = np.arange(2 * half)
    cut = half // 128 * 128
    first = np.arange(half)
    second = np.where(first < cut, half + (half - cut) + first, half + first - cut)
    return place[first], place[second]


def product_signs(channels):
    unit = np.eye(channels, dtype=np.float32)
    psi = np.zeros((2, 2, 2, 4, 2, 2), np.float32)
    for q in range(2):
        for p in range(2):
            part = -1.0 if (q == 0 and p == 1) else 1.0
            for row in range(2):
                for inner in range(2):
                    psi[q, row, p ^ q, :, p, inner] = part * MATRIX_SIGNS[row, inner]
    psi = np.einsum("qrwapn,ij->qrwaipnj", psi, unit).reshape(4, 8 * channels, 4 * channels)
    psi = np.pad(psi, ((0, 0), (0, 0), (0, 256 - 4 * channels)))
    spread = np.einsum("pt,ncb,ij->pbictnj", np.eye(2), MATRIX_SIGNS, unit)
    spread = spread.reshape(8 * channels, 2, 4 * channels)
    turn = np.zeros((8 * channels, 8 * channels), np.float32)
    for col, lanes in enumerate(lanes_of_columns(channels)):
        turn[:, lanes] = spread[:, col]
    point = np.zeros((4, 4, 4), np.float32)
    for k in range(4):
        for b in range(4):
            point[k, k ^ b, b] = BLADE_SIGNS[k ^ b, b]
    point = np.einsum("kab,ij->kaibj", point, unit).reshape(4, 4 * channels, 4 * channels)
    point = np.pad(point, ((0, 0), (0, 0), (0, 256 - 4 * channels)))
    return (one.astype(ml_dtypes.bfloat16) for one in (psi, turn, point))


def dot(a, b):
    return lax.dot_general(a, b, (((1,), (0,)), ((), ())), preferred_element_type=F32)


def dot_nt(a, b):
    return lax.dot_general(a, b, (((1,), (1,)), ((), ())), preferred_element_type=F32)


def layer_kernel(
    sizes,
    x_hbm, ct_hbm, scale_ref, table_ref, owner_ref, single_hbm, psi_hbm, master_hbm, momentum_hbm,
    turn_ref, sign_ref, cblk_ref, eye_ref, point_ref, point_momentum_ref,
    ob, xb, dw_ref, pg_ref, turned_ref, point_turned_ref,
    eb, single, psi, master_ref, momentum_ref, wm, cols, l2, kt1, ktb, kk1, kkb, acc, gk_ref, pa, pz,
    lows, highs, perm_ref, back_ref,
    pb1, rb1, gb1, pb2, rb2, gb2,
    xs, xr, ps, pr, gs, gr, hs, hr,
    x_sem, ct_sem, ld_sem, ei_sem, pa_s, pa_r, pz_s, pz_r,
    rs1_s, rs1_r, rs2_s, rs2_r, ag1_s, ag1_r, ag2_s, ag2_r, a2a_s, a2a_r,
):
    nb, nz, S, H, K, W, slots, M = sizes
    wide = 2 * K
    channels = K // 4
    pairs = H // 2
    me = lax.axis_index("batch")
    z = lax.axis_index("row")
    last = nz - 1

    loads = [
        pltpu.make_async_copy(psi_hbm, psi, ld_sem.at[0]),
        pltpu.make_async_copy(single_hbm.at[z], single, ld_sem.at[1]),
        pltpu.make_async_copy(master_hbm, master_ref, ld_sem.at[2]),
        pltpu.make_async_copy(momentum_hbm, momentum_ref, ld_sem.at[3]),
    ]
    x_copy = lambda s: pltpu.make_async_copy(x_hbm.at[s], xb.at[s], x_sem.at[s])
    ct_copy = lambda s: pltpu.make_async_copy(ct_hbm.at[s], ob.at[s], ct_sem.at[s])
    ect_copy = lambda s: pltpu.make_async_copy(ct_hbm.at[s], eb.at[lax.rem(s, 2)], ei_sem.at[lax.rem(s, 2)])

    barrier = pltpu.get_barrier_semaphore()

    def greet(d, carry):
        peer = lax.rem(me + d, nb)
        pl.semaphore_signal(barrier, inc=1, device_id=(peer, z), device_id_type=MESH)
        return carry

    lax.fori_loop(1, nb, greet, 0)

    def greet_z(d, carry):
        pl.semaphore_signal(barrier, inc=1, device_id=(me, lax.rem(z + d, nz)), device_id_type=MESH)
        return carry

    lax.fori_loop(1, nz, greet_z, 0)
    x_copy(0).start()
    loads[1].start()
    x_copy(1).start()
    loads[0].start()
    loads[2].start()
    x_copy(2).start()
    loads[3].start()
    cols[...] = jnp.zeros_like(cols)
    gk_ref[...] = jnp.zeros_like(gk_ref)

    def place_modes():
        local = COLUMN_MODES // nz
        lane = lax.broadcasted_iota(jnp.int32, (1, 2 * M), 1)

        def place(d, carry):
            for i in range(slots):
                mode = owner_ref[(d * nz + z) * slots + i]
                at = lax.div(mode, COLUMN_MODES) * local + lax.rem(mode, local)
                lows[pl.ds(d * slots + i, 1), :] = jnp.where(lane == at, 1.0, 0.0)
                highs[pl.ds(d * slots + i, 1), :] = jnp.where(lane == at + M, 1.0, 0.0)
            return carry

        lax.fori_loop(0, nb, place, 0)
        inner = 1.0 / (H * nz * H * nz)
        weigh = jnp.where(z * local + lax.rem(lane, local) == 0, 0.5 * inner, inner)
        for table, pick in enumerate((lambda v: v[...], lambda v: v[...] * weigh)):
            perm_ref[table] = pick(lows)[:, 0:M].astype(BF16)
            back_ref[1 - table, 0] = pick(lows).astype(BF16)
            back_ref[1 - table, 1] = pick(highs).astype(BF16)

    def point_kernels():
        weight = point_ref[...].astype(BF16)
        kernel_t = jnp.concatenate([dot(weight, sign_ref[k]) for k in range(4)], axis=0)
        kt1[...] = kernel_t[:, 0:128].astype(BF16)
        for turn in range(8):
            ktb[turn] = pltpu.roll(kernel_t[:, 128:256], (64 + 16 * turn) % 128, 1)
        padded = jnp.concatenate([kernel_t.astype(BF16), jnp.zeros((256 - K, 256), BF16)], axis=0)
        kernel_n = dot_nt(eye_ref[0:K], padded)
        kk1[...] = kernel_n[:, 0:128].astype(BF16)
        for turn in range(8):
            kkb[turn] = pltpu.roll(kernel_n[:, 128:256], (64 + 16 * turn) % 128, 1)

    def expand_weights():
        loads[0].wait()
        loads[2].wait()
        wm[...] = jnp.zeros_like(wm)
        masters = master_ref[...].reshape(slots * channels, wide).astype(BF16)
        for part in range(4):
            block = dot(masters, psi[part]).astype(BF16)
            for i in range(slots):
                wm[i, part * channels : (part + 1) * channels, :] = block[i * channels : (i + 1) * channels]

    def rs_copy(s, up, c, pb, rb, ssem, rsem):
        way = 0 if up else 1
        return pltpu.make_async_remote_copy(
            src_ref=pb.at[s, c], dst_ref=rb.at[s, way, c],
            send_sem=ssem.at[s, way, c], recv_sem=rsem.at[s, way, c],
            device_id=(me, z + 1 if up else z - 1), device_id_type=MESH,
        )

    def rs_hop(j, s, bufs, finish=False):
        pb, rb = bufs[0], bufs[1]
        for up in (True, False):
            place = z if up else last - z
            c = (last - j + z) if up else (z - (last - j))

            @pl.when(place <= j)
            def _():
                copy = rs_copy(s, up, c, *bufs)
                if finish:
                    copy.wait_send()
                else:
                    @pl.when(place > 0)
                    def _():
                        way = 0 if up else 1
                        copy.wait_recv()
                        pb[s, c] = (pb[s, c].astype(F32) + rb[s, way, c].astype(F32)).astype(BF16)

                    copy.start()

    def rs_final(s, bufs, e):
        pb, rb = bufs[0], bufs[1]
        acc[e] = pb[s, z].astype(F32)

        @pl.when(z > 0)
        def _():
            rs_copy(s, True, z, *bufs).wait_recv()
            acc[e] += rb[s, 0, z].astype(F32)

        @pl.when(z < last)
        def _():
            rs_copy(s, False, z, *bufs).wait_recv()
            acc[e] += rb[s, 1, z].astype(F32)

    def ag_copy(s, up, c, gb, ssem, rsem):
        way = 0 if up else 1
        return pltpu.make_async_remote_copy(
            src_ref=gb.at[s, c], dst_ref=gb.at[s, c],
            send_sem=ssem.at[s, way, c], recv_sem=rsem.at[s, c],
            device_id=(me, z + 1 if up else z - 1), device_id_type=MESH,
        )

    def ag_hop(j, s, bufs, finish=False):
        for up in (True, False):
            c = z - j if up else z + j
            more = z < last if up else z > 0

            @pl.when((c >= 0) if up else (c <= last))
            def _():
                copy = ag_copy(s, up, c, *bufs)
                if j > 0 and not finish:
                    copy.wait_recv()

                if j < last:
                    @pl.when(more)
                    def _():
                        if finish:
                            copy.wait_send()
                        else:
                            copy.start()

    tiled = slots % 8 == 0

    def block_of(ref, h, d):
        if tiled:
            return ref.at[h, :, :, pl.ds(pl.multiple_of(d * slots, slots), slots)]
        return ref.at[h, :, d]

    def blocks_of(ref, h):
        if tiled:
            return ref.at[h, :, :, pl.ds(0, (nb - 1) * slots)]
        return ref.at[h, :, pl.ds(0, nb - 1)]

    def whole_of(ref, h, e):
        if tiled:
            return jnp.concatenate([ref[h, e, g] for g in range(wide // 128)], axis=1)
        return ref[h, e].reshape(nb * slots, wide)

    def put_whole(ref, h, e, value):
        if tiled:
            for g in range(wide // 128):
                ref[h, e, g] = value[:, g * 128 : (g + 1) * 128]
        else:
            ref[h, e] = value.reshape(nb, slots, wide)

    def slot_rows(ref, h, e, i):
        if tiled:
            return jnp.concatenate([ref[h, e, g, pl.ds(i, nb, stride=slots), :] for g in range(wide // 128)], axis=1)
        return ref[h, e, :, i, :]

    def put_slot_rows(ref, h, e, i, value):
        if tiled:
            for g in range(wide // 128):
                ref[h, e, g, pl.ds(i, nb, stride=slots), :] = value[:, g * 128 : (g + 1) * 128]
        else:
            ref[h, e, :, i, :] = value

    def exchange(h, src, dst, which):
        def send(d, carry):
            peer = lax.rem(me + d, nb)
            pltpu.make_async_remote_copy(
                src_ref=block_of(src, h, peer), dst_ref=block_of(dst, h, me),
                send_sem=a2a_s.at[which, h], recv_sem=a2a_r.at[which, h],
                device_id=(peer, z), device_id_type=MESH,
            ).start()
            return carry

        lax.fori_loop(1, nb, send, 0)
        block_of(dst, h, me)[...] = block_of(src, h, me)[...]

    def exchanged(h, src, dst, which):
        return pltpu.make_async_remote_copy(
            src_ref=blocks_of(src, h), dst_ref=blocks_of(dst, h),
            send_sem=a2a_s.at[which, h], recv_sem=a2a_r.at[which, h],
            device_id=(lax.rem(me + 1, nb), z), device_id_type=MESH,
        )

    def forward_rows(s, pb):
        for c in range(nz):
            part = dot(single[...], cols[c])
            first = part[0:M]
            second = pltpu.roll(part[M:], 64, 1)
            pb[s, c, :, 0:128] = first[:, 0:128].astype(BF16)
            pb[s, c, :, 128:256] = (first[:, 128:256] + second[:, 0:128]).astype(BF16)
            pb[s, c, :, 256:384] = second[:, 128:256].astype(BF16)

    def put_columns(p, value):
        step = 4 * COLUMN_MODES // nz
        for c in range(nz):
            cols[c, pl.ds(pl.multiple_of(p * step, step), step), 0:K] = value[c * step : (c + 1) * step]

    def pair_of(ref, s, p):
        return jnp.concatenate([ref[s, 2 * p], ref[s, 2 * p + 1]], axis=1)

    def stage_a(s):
        x_copy(s).wait()

        def some(blk, carry):
            for u in range(8):
                p = blk * 8 + u
                part = dot_nt(cblk_ref[...], pair_of(xb, s, p))
                put_columns(p, part.astype(BF16))
            return carry

        lax.fori_loop(0, pairs // 8, some, 0)
        forward_rows(s, pb1)
        rs_hop(0, s, rs1)

    def by_column(ref, h, i):
        first, second = [], []
        for e in range(2):
            rows = slot_rows(ref, h, e, i)
            low, mid, top = rows[:, 0:128], rows[:, 128:256], rows[:, 256:384]
            first.append(jnp.concatenate([low, mid], axis=1))
            second.append(jnp.concatenate([top, pltpu.roll(mid, 64, 1)], axis=1))
        return jnp.concatenate(first + second, axis=0).astype(BF16)

    def put_by_column(ref, h, i, value):
        for e in range(2):
            first, second = value[e * nb : (e + 1) * nb], value[(2 + e) * nb : (3 + e) * nb]
            mid = first[:, 128:256] + pltpu.roll(second[:, 128:256], 64, 1)
            put_slot_rows(ref, h, e, i, jnp.concatenate([first[:, 0:128], mid, second[:, 0:128]], axis=1))

    def stage_b(s):
        h = lax.div(s, 2)
        exchanged(h, xs, xr, 0).wait_recv()
        for i in range(slots):
            put_by_column(ps, h, i, dot_nt(by_column(xr, h, i), wm[i]))
        exchange(h, ps, pr, 1)

    def stage_d(s):
        h = lax.div(s, 2)
        exchanged(h, gs, gr, 2).wait_recv()
        for i in range(slots):
            put_by_column(hs, h, i, dot(by_column(gr, h, i), wm[i]))
        exchange(h, hs, hr, 3)

    def stage_f(s, bufs, table, src, dst, which):
        h = lax.div(s, 2)
        for e in range(2):
            rs_final(s - 1 + e, bufs, e)
        placed = [dot(perm_ref[table], acc[e].astype(BF16)).astype(BF16) for e in range(2)]
        both = dot(jnp.concatenate(placed, axis=0), turn_ref[...])
        for e in range(2):
            put_whole(src, h, e, both[e * M : (e + 1) * M])
        exchange(h, src, dst, which)

    def stage_u(s, bufs, table, src, dst, which):
        h = lax.div(s, 2)
        exchanged(h, src, dst, which).wait_recv()
        for e in range(2):
            turned = jnp.transpose(whole_of(dst, h, e))
            cut = K // 128 * 128
            first = turned[0:K]
            second = jnp.concatenate([turned[2 * K - cut :], turned[K : 2 * K - cut]], axis=0)
            parts = []
            for q in range(2):
                base = 2 * q * channels
                at = lambda col, row: col[base + row * channels : base + (row + 1) * channels]
                m00, m10, m01, m11 = at(first, 0), at(first, 1), at(second, 0), at(second, 1)
                parts.append(jnp.concatenate([m00 + m11, m00 - m11, m01 + m10, m01 - m10], axis=0).astype(BF16))
            bufs[0][s - 1 + e, z] = (dot(parts[0], back_ref[table, 0]) + dot(parts[1], back_ref[table, 1])).astype(BF16)
        gather(0, s, bufs)

    def gather(j, s, bufs):
        for e in range(2):
            ag_hop(j, s - 1 + e, bufs)

    def inverse_rows(s, gb, base):
        spread = dot(gb[s].reshape(nz * K, 2 * M), single[...])
        group = lax.broadcasted_iota(jnp.int32, (K, 128), 1) // 16
        for col in range(pairs // 8):
            cut = slice(col * 128, col * 128 + 128)
            parts = [spread[c * K : (c + 1) * K, cut] for c in range(nz)]
            parts = [parts[0]] + [pltpu.roll(parts[c], 16 * c, 1) for c in range(1, nz)]
            for first in range(4):
                which = (group + (8 - first)) % 4
                mixed = jnp.where(which == 0, parts[0], jnp.where(which == 1, parts[1], jnp.where(which == 2, parts[2], parts[3])))
                for turn in (first, first + 4):
                    inside = (group + (8 - turn)) % 8 < 4
                    l2[col * 8 + turn] = jnp.where(inside, mixed, base[turn]).astype(BF16)

    def with_columns(x2, turn):
        rows = [x2[0:128]]
        for g in range(8):
            i = (g - turn) % 8
            rows.append(cblk_ref[16 * i : 16 * i + 16, :] if i < 4 else x2[64 + 16 * i : 80 + 16 * i])
        return jnp.concatenate(rows, axis=0)

    def stage_c(s):
        ag_hop(last, s, ag1)
        inverse_rows(s, gb1, ktb)
        ct_copy(s).wait()
        f = table_ref[scale_ref[s]]

        def some(blk, carry):
            for u in range(8):
                p = blk * 8 + u
                x2 = pair_of(xb, s, p)
                both = with_columns(x2, u)
                half = (0.5 * f) * dot(jnp.concatenate([kt1[...], l2[p]], axis=1), both)
                square = half * half
                rise = 1.0 + jnp.tanh(half * (2.0 * GELU_A + 8.0 * GELU_B * square))
                y = (x2.astype(F32) + half * rise).astype(BF16)
                slope = rise + (rise * (2.0 - rise)) * (half * (2.0 * GELU_A + 24.0 * GELU_B * square))
                c2 = pair_of(ob, s, p).astype(F32)
                g2 = (((0.5 * f) * c2) * slope).astype(BF16)
                for e in range(2):
                    ob[s, 2 * p + e] = y[:, e * W : (e + 1) * W]
                    xb[s, 2 * p + e] = g2[:, e * W : (e + 1) * W]
                back = dot_nt(both, g2)
                gk_ref[0:128] += back[0:128]
                for g in range(8):
                    i = (g - u) % 8
                    piece = back[128 + 16 * g : 144 + 16 * g]
                    if i < 4:
                        cols[i, pl.ds(pl.multiple_of(p * 16, 16), 16), 0:K] = piece.astype(BF16)
                    else:
                        gk_ref[64 + 16 * i : 80 + 16 * i] += piece
            return carry

        lax.fori_loop(0, pairs // 8, some, 0)
        forward_rows(s, pb2)
        rs_hop(0, s, rs2)

    def stage_e(s):
        slot = lax.rem(s, 2)

        @pl.when(s + 1 < S)
        def _():
            ect_copy(s + 1).start()

        ag_hop(last, s, ag2)
        inverse_rows(s, gb2, kkb)
        ect_copy(s).wait()

        def some(blk, carry):
            for u in range(8):
                p = blk * 8 + u
                both = with_columns(pair_of(xb, s, p), u)
                y = dot(jnp.concatenate([kk1[...], l2[p]], axis=1), both)
                y = (y + pair_of(eb, slot, p).astype(F32)).astype(BF16)
                for e in range(2):
                    xb[s, 2 * p + e] = y[:, e * W : (e + 1) * W]
            return carry

        lax.fori_loop(0, pairs // 8, some, 0)

    def pa_copy(peer):
        return pltpu.make_async_remote_copy(
            src_ref=pa.at[me], dst_ref=pa.at[me], send_sem=pa_s.at[0], recv_sem=pa_r.at[0],
            device_id=(peer, z), device_id_type=MESH,
        )

    def pz_copy(peer):
        return pltpu.make_async_remote_copy(
            src_ref=pz.at[z], dst_ref=pz.at[z], send_sem=pz_s.at[0], recv_sem=pz_r.at[0],
            device_id=(me, peer), device_id_type=MESH,
        )

    def all_but_one(ref, count, ssem, rsem, device):
        rest = ref.at[pl.ds(0, count - 1)]
        return pltpu.make_async_remote_copy(
            src_ref=rest, dst_ref=rest, send_sem=ssem.at[0], recv_sem=rsem.at[0],
            device_id=device, device_id_type=MESH,
        )

    def point_first():
        left = gk_ref[...]
        total = jnp.zeros((channels, K), F32)
        for part in range(3):
            term = left.astype(BF16)
            left = left - term.astype(F32)
            turned = dot_nt(eye_ref[0:K, 0:K], term).astype(BF16)
            for k in range(4):
                total += dot_nt(turned[k * channels : (k + 1) * channels], sign_ref[k, :, 0:K])
        pa[me] = total

        def send(d, carry):
            pa_copy(lax.rem(me + d, nb)).start()
            return carry

        lax.fori_loop(1, nb, send, 0)

    def point_second():
        all_but_one(pa, nb, pa_s, pa_r, (lax.rem(me + 1, nb), z)).wait_recv()
        pz[z] = jnp.sum(pa[...], axis=0)

        def send(d, carry):
            pz_copy(lax.rem(z + d, nz)).start()
            return carry

        lax.fori_loop(1, nz, send, 0)

    def slot_gradients():
        loads[3].wait()
        for i in range(slots):
            g_all = jnp.concatenate([by_column(gr, h, i) for h in range(S // 2)], axis=0)
            x_all = jnp.concatenate([by_column(xr, h, i) for h in range(S // 2)], axis=0)
            g_turned = dot_nt(eye_ref[...], g_all).astype(BF16)
            wm[i] = dot(g_turned, x_all).astype(BF16)

        total = jnp.zeros((slots * channels, wide), F32)
        for part in range(4):
            rows = slice(part * channels, (part + 1) * channels)
            block = jnp.concatenate([wm[i, rows, :] for i in range(slots)], axis=0)
            total += dot_nt(block, psi[part])
        dw_ref[...] = total.reshape(slots, channels, wide)

    def orthogonal(moments):
        def split(v):
            high = v.astype(BF16)
            return high, (v - high.astype(F32)).astype(BF16)

        def product(a, b, mul):
            (ah, al), (bh, bl) = a, b
            return mul(ah, bh) + (mul(ah, bl) + mul(al, bh))

        current = [m / (jnp.sqrt(jnp.sum(m * m)) + 1e-07) for m in moments]
        for repeat in range(5):
            parts = [split(v) for v in current]
            grams = [product(v, v, dot_nt) for v in parts]
            gram_parts = [split(v) for v in grams]
            squares = [product(v, v, dot) for v in gram_parts]
            polynomials = [split(QUINTIC_SECOND * g + QUINTIC_THIRD * q) for g, q in zip(grams, squares)]
            current = [
                QUINTIC_FIRST * v + product(p, w, dot) for v, p, w in zip(current, polynomials, parts)
            ]
        return current

    def slot_updates(chosen):
        moments = [MOMENTUM_DECAY * momentum_ref[i] + dw_ref[i] for i in chosen]
        for i, value in zip(chosen, orthogonal(moments)):
            turned_ref[i] = value

    def point_update():
        all_but_one(pz, nz, pz_s, pz_r, (me, lax.rem(z + 1, nz))).wait_recv()
        total = jnp.sum(pz[...], axis=0)
        pg_ref[...] = total
        (point_turned_ref[...],) = orthogonal([MOMENTUM_DECAY * point_momentum_ref[...] + total])

    rs1 = (pb1, rb1, rs1_s, rs1_r)
    rs2 = (pb2, rb2, rs2_s, rs2_r)
    ag1 = (gb1, ag1_s, ag1_r)
    ag2 = (gb2, ag2_s, ag2_r)

    def odd(stage):
        return lambda s: pl.when(lax.rem(s, 2) == 1)(functools.partial(stage, s))

    schedule = [
        (0, stage_a),
        (3, odd(lambda s: stage_f(s, rs1, 0, xs, xr, 0))),
        (12, odd(lambda s: stage_f(s, rs2, 1, gs, gr, 2))),
        (2, lambda s: rs_hop(2, s, rs1)),
        (11, lambda s: rs_hop(2, s, rs2)),
        (1, lambda s: rs_hop(1, s, rs1)),
        (10, lambda s: rs_hop(1, s, rs2)),
        (7, odd(lambda s: gather(2, s, ag1))),
        (16, odd(lambda s: gather(2, s, ag2))),
        (6, odd(lambda s: gather(1, s, ag1))),
        (15, odd(lambda s: gather(1, s, ag2))),
        (5, odd(lambda s: stage_u(s, ag1, 0, ps, pr, 1))),
        (14, odd(lambda s: stage_u(s, ag2, 1, hs, hr, 3))),
        (4, odd(stage_b)),
        (13, odd(stage_d)),
        (9, stage_c),
        (18, stage_e),
    ]
    steps = S + max(lag for lag, _ in schedule)
    at_step = {
        0: place_modes, 1: expand_weights, 2: point_kernels, S + 9: point_first, S + 10: point_second, S + 12: point_update,
        S + 13: slot_gradients,
    }
    groups = [range(slots)[: slots // 2], range(slots)[slots // 2 :]]
    for step, group in enumerate(groups):
        if group:
            at_step[S + 14 + step] = functools.partial(slot_updates, group)

    pl.semaphore_wait(barrier, nb + nz - 2)

    loads[1].wait()

    def iteration(t, carry):
        pl.when(t + 3 < S)(lambda: x_copy(t + 3).start())
        pl.when((t >= 5) & (t < S + 5))(lambda: ct_copy(t - 5).start())
        pl.when(t == 16)(lambda: ect_copy(0).start())
        for lag, stage in schedule:
            s = t - lag
            pl.when((s >= 0) & (s < S))(functools.partial(stage, s))
        for step, work in at_step.items():
            pl.when(t == step)(work)
        return carry

    lax.fori_loop(0, steps, iteration, 0)

    def finish(s, carry):
        for j in range(last):
            rs_hop(j, s, rs1, True)
            rs_hop(j, s, rs2, True)
            ag_hop(j, s, ag1, True)
            ag_hop(j, s, ag2, True)
        return carry

    def finish_exchanges(h, carry):
        for which, (src, dst) in enumerate(((xs, xr), (ps, pr), (gs, gr), (hs, hr))):
            exchanged(h, src, dst, which).wait_send()
        return carry

    lax.fori_loop(0, S, finish, 0)
    lax.fori_loop(0, S // 2, finish_exchanges, 0)
    all_but_one(pa, nb, pa_s, pa_r, (lax.rem(me + 1, nb), z)).wait_send()
    all_but_one(pz, nz, pz_s, pz_r, (me, lax.rem(z + 1, nz))).wait_send()


def store_kernel(
    ob, xb, dw_ref, pg_ref, turned_ref, point_turned_ref, master_ref, momentum_ref, point_ref, point_momentum_ref,
    out_hbm, ig_hbm, grad_ref, moment_ref, weight_ref, low_ref,
    point_grad_ref, point_moment_ref, point_weight_ref, point_low_ref, sem,
):
    S = ob.shape[0]
    copies = []
    for s in range(S):
        copies.append(pltpu.make_async_copy(ob.at[s], out_hbm.at[s], sem.at[0, s]))
        copies.append(pltpu.make_async_copy(xb.at[s], ig_hbm.at[s], sem.at[1, s]))
    for copy in copies:
        copy.start()
    point_grad_ref[...] = pg_ref[...]
    point_moment_ref[...] = MOMENTUM_DECAY * point_momentum_ref[...] + pg_ref[...]
    point_weight = point_ref[...] - POINTWISE_RATE * point_turned_ref[...]
    point_weight_ref[...] = point_weight
    point_low_ref[...] = point_weight.astype(BF16)
    grad_ref[...] = dw_ref[...]
    moment_ref[...] = MOMENTUM_DECAY * momentum_ref[...] + dw_ref[...]
    weight = master_ref[...] - SPECTRAL_RATE * turned_ref[...]
    weight_ref[...] = weight
    low_ref[...] = weight.astype(BF16)
    for copy in copies:
        copy.wait()


def per_device(
    input_field,
    cotangent,
    sample_scale,
    scale_table,
    owner_map,
    spectral_master,
    spectral_momentum,
    pointwise_master,
    pointwise_momentum,
):
    S, H, K, W = input_field.shape
    nz = lax.axis_size("row")
    nb = lax.axis_size("batch")
    slots = spectral_master.shape[0]
    channels = K // 4
    wide = 2 * K
    local_columns = COLUMN_MODES // nz
    M = ROW_MODES * local_columns
    grid = H * nz

    anywhere = pl.BlockSpec(memory_space=pltpu.HBM)
    smem = pl.BlockSpec(memory_space=pltpu.SMEM)
    vmem = pl.BlockSpec(memory_space=pltpu.VMEM)
    exchange_shape = (S // 2, 2, wide // 128, nb * slots, 128) if slots % 8 == 0 else (S // 2, 2, nb, slots, wide)
    dma = pltpu.SemaphoreType.DMA
    single = jnp.asarray(row_blocks(grid, nz))
    psi, turn, signs = (jnp.asarray(one) for one in product_signs(channels))
    column_rows = jnp.asarray(column_block(W, nz))
    unit = jnp.asarray(np.eye(256).astype(ml_dtypes.bfloat16))
    slot_shape, point_shape = spectral_master.shape, pointwise_master.shape
    kept = pl.pallas_call(
        functools.partial(layer_kernel, (nb, nz, S, H, K, W, slots, M)),
        out_shape=(
            pltpu.VMEM(input_field.shape, BF16),
            pltpu.VMEM(input_field.shape, BF16),
            pltpu.VMEM(slot_shape, F32),
            pltpu.VMEM(point_shape, F32),
            pltpu.VMEM(slot_shape, F32),
            pltpu.VMEM(point_shape, F32),
        ),
        in_specs=[anywhere, anywhere, smem, smem, smem] + [anywhere] * 4 + [vmem] * 6,
        out_specs=(vmem,) * 6,
        scratch_shapes=[
            pltpu.VMEM((2, H, K, W), BF16),
            pltpu.VMEM(single.shape[1:], BF16),
            pltpu.VMEM(psi.shape, BF16),
            pltpu.VMEM(spectral_master.shape, F32),
            pltpu.VMEM(spectral_master.shape, F32),
            pltpu.VMEM((slots, 256, 256), BF16),
            pltpu.VMEM((nz, single.shape[2], 256), BF16),
            pltpu.VMEM((H // 2, K, 128), BF16),
            pltpu.VMEM((K, 128), BF16),
            pltpu.VMEM((8, K, 128), F32),
            pltpu.VMEM((K, 128), BF16),
            pltpu.VMEM((8, K, 128), F32),
            pltpu.VMEM((2, M, wide), F32),
            pltpu.VMEM((K, K), F32),
            pltpu.VMEM((nb, channels, K), F32),
            pltpu.VMEM((nz, channels, K), F32),
            pltpu.VMEM((M, 2 * M), F32),
            pltpu.VMEM((M, 2 * M), F32),
            pltpu.VMEM((2, M, M), BF16),
            pltpu.VMEM((2, 2, M, 2 * M), BF16),
            pltpu.VMEM((S, nz, M, wide), BF16),
            pltpu.VMEM((S, 2, nz, M, wide), BF16),
            pltpu.VMEM((S, nz, K, 2 * M), BF16),
            pltpu.VMEM((S, nz, M, wide), BF16),
            pltpu.VMEM((S, 2, nz, M, wide), BF16),
            pltpu.VMEM((S, nz, K, 2 * M), BF16),
        ]
        + [pltpu.VMEM(exchange_shape, F32)] * 8
        + [dma((S,)), dma((S,)), dma((4,)), dma((2,))]
        + [dma((1,))] * 4
        + [dma((S, 2, nz))] * 4
        + [dma((S, 2, nz)), dma((S, nz))] * 2
        + [dma((4, S // 2))] * 2,
        compiler_params=pltpu.CompilerParams(
            collective_id=0, has_side_effects=True, vmem_limit_bytes=37 * 1024 * 1024
        ),
    )(
        input_field, cotangent, sample_scale, scale_table, owner_map, single, psi,
        spectral_master, spectral_momentum, turn, signs, column_rows, unit, pointwise_master, pointwise_momentum,
    )

    held = [pltpu.with_memory_space_constraint(one, pltpu.VMEM) for one in kept]
    input_shape = jax.ShapeDtypeStruct(input_field.shape, BF16)
    results = pl.pallas_call(
        store_kernel,
        out_shape=(
            input_shape,
            input_shape,
            jax.ShapeDtypeStruct(slot_shape, F32),
            jax.ShapeDtypeStruct(slot_shape, F32),
            jax.ShapeDtypeStruct(slot_shape, F32),
            jax.ShapeDtypeStruct(slot_shape, BF16),
            jax.ShapeDtypeStruct(point_shape, F32),
            jax.ShapeDtypeStruct(point_shape, F32),
            jax.ShapeDtypeStruct(point_shape, F32),
            jax.ShapeDtypeStruct(point_shape, BF16),
        ),
        in_specs=[vmem] * 10,
        out_specs=(anywhere, anywhere) + (vmem,) * 8,
        scratch_shapes=[dma((2, S))],
        compiler_params=pltpu.CompilerParams(vmem_limit_bytes=6 * 1024 * 1024),
    )(*held, spectral_master, spectral_momentum, pointwise_master, pointwise_momentum)
    return tuple(results)


def solution(mesh):
    return jax.shard_map(
        per_device,
        mesh=mesh,
        in_specs=(
            P("batch", "row", None, None),
            P("batch", "row", None, None),
            P("batch"),
            P(),
            P(),
            P(("batch", "row"), None, None),
            P(("batch", "row"), None, None),
            P(),
            P(),
        ),
        out_specs=(
            P("batch", "row", None, None),
            P("batch", "row", None, None),
            P(("batch", "row"), None, None),
            P(("batch", "row"), None, None),
            P(("batch", "row"), None, None),
            P(("batch", "row"), None, None),
            P(),
            P(),
            P(),
            P(),
        ),
        check_vma=False,
    )
```
